128 devices in a mesh: ctx: 8 (over y_lo, z), fsdp: 16 (over x, y_hi, core).
Axes of the slice: x: 4, y: 4 (y_hi: 2, y_lo: 2; y = y_hi * 2 + y_lo), z: 4, core: 2. Of those that a mesh axis runs over, the one named last changes fastest.
Arguments:
- tokens: bfloat16 [16, 2048, 1024], P('fsdp', 'ctx'), may hold values from -6 to 6
- segment_ids: int32 [16, 2048], P('fsdp', 'ctx'), may hold values from 0 to 3, never falling along the last dimension, each value on 1 to 1920 neighbouring positions
- cotangent: bfloat16 [16, 2048, 1024], P('fsdp', 'ctx'), may hold values from -6 to 6
- ln1_gain: bfloat16 [1024], P('fsdp'), may hold values from 0.099609375 to 1.8984375
- ln1_bias: bfloat16 [1024], P('fsdp'), may hold values from -3 to 3
- qkv_weight: bfloat16 [1024, 3072], P('fsdp'), may hold values from -0.1875 to 0.1875
- qkv_bias: bfloat16 [2048], P('fsdp'), may hold values from -3 to 3
- out_weight: bfloat16 [1024, 1024], P('fsdp'), may hold values from -0.5 to 0.5
- out_bias: bfloat16 [1024], P('fsdp'), may hold values from -3 to 3
- ln2_gain: bfloat16 [1024], P('fsdp'), may hold values from 0.099609375 to 1.8984375
- ln2_bias: bfloat16 [1024], P('fsdp'), may hold values from -3 to 3
- fc1_weight: bfloat16 [1024, 4096], P('fsdp'), may hold values from -0.1875 to 0.1875
- fc1_bias: bfloat16 [4096], P('fsdp'), may hold values from -3 to 3
- fc2_weight: bfloat16 [4096, 1024], P('fsdp'), may hold values from -0.125 to 0.125
- fc2_bias: bfloat16 [1024], P('fsdp'), may hold values from -3 to 3
Outputs:
- output: bfloat16 [16, 2048, 1024], P('fsdp', 'ctx')
- input_grad: float32 [16, 2048, 1024], P('fsdp', 'ctx')
- ln1_gain_grad: float32 [1024], P('fsdp')
- ln1_bias_grad: float32 [1024], P('fsdp')
- qkv_weight_grad: float32 [1024, 3072], P('fsdp')
- qkv_bias_grad: float32 [2048], P('fsdp')
- out_weight_grad: float32 [1024, 1024], P('fsdp')
- out_bias_grad: float32 [1024], P('fsdp')
- ln2_gain_grad: float32 [1024], P('fsdp')
- ln2_bias_grad: float32 [1024], P('fsdp')
- fc1_weight_grad: float32 [1024, 4096], P('fsdp')
- fc1_bias_grad: float32 [4096], P('fsdp')
- fc2_weight_grad: float32 [4096, 1024], P('fsdp')
- fc2_bias_grad: float32 [1024], P('fsdp')
- log_sum_exp: float32 [16, 16, 2048], P('fsdp', None, 'ctx')
The draws below stay inside these ranges and needn't reach their ends.
Inputs may be any that keep to these rules, and one draw needn't show every extreme that they name: `segment_ids`: in each row the document number never falls, every document is a contiguous run of positions, and one document of each row holds exactly 1920 positions.
All inputs are finite; a program needn't handle non-finite values.
Results may differ from the reference program's by a relative error of at most 0.023.
Values may be sent and summed in bfloat16 or wider, within the bound.
A program may use at most 192 MiB of HBM per device.

```python
import math
import jax
import jax.numpy as jnp
import numpy as np
from jax import lax

D = 1024
HEADS = 16
HEAD_DIM = 64
FF = 4096
LENGTH = 2048
BLK = 256
BATCH = 16


def level_of(stream_key, extent, shards, low, largest):
    def one(position, parts):
        steps = jax.random.uniform(jax.random.fold_in(jax.random.fold_in(stream_key, 6), position), (parts,), jnp.float32, low / len(shards), largest / len(shards))
        return jnp.repeat(jnp.exp(steps), extent[position] // parts).reshape((-1,) + (1,) * (len(extent) - position - 1))

    gain = one(*shards[0])
    for cut in shards[1:]:
        gain = gain * one(*cut)
    return gain


def length_profile(amount, total, limit, slope):
    loads = [(1 << 20) // math.isqrt(grade ** slope) + 1 for grade in range(2, amount + 1)]
    surplus, counts = total - limit - (amount - 1), [1] * (amount - 1)
    while surplus > 0:
        candidates = [i for i in range(amount - 1) if counts[i] < limit]
        pool, left = sum([loads[i] for i in candidates]), surplus
        for i in candidates:
            more = min(limit - counts[i], max(1, left * loads[i] // pool), surplus)
            counts[i] = counts[i] + more
            surplus = surplus - more
    return np.array([limit] + counts)


def uneven(own_key, number_of, total, limit, skew):
    if number_of == 2:
        one = jax.random.randint(own_key, (), max(1, total - limit), min(limit, total - 1) + 1)
        return jnp.stack([one, total - one])
    tallies = jnp.asarray(length_profile(number_of, total, limit, skew), jnp.int32)
    twos = (number_of - 1) // 2
    giver, sink = tallies[1:1 + 2 * twos:2], tallies[2:2 + 2 * twos:2]
    margin = jnp.minimum(giver - 1, limit - sink)
    moved = jax.random.randint(jax.random.fold_in(own_key, 1), (twos,), 0, 1 << 20) % (margin + 1)
    tallies = tallies.at[1:1 + 2 * twos:2].set(giver - moved).at[2:2 + 2 * twos:2].set(sink + moved)
    return tallies[jax.random.permutation(jax.random.fold_in(own_key, 2), number_of)]


def gaussian(own_key, shape, deviation, bound, cuts=(), kind=jnp.bfloat16):
    loudness = level_of(own_key, shape, cuts, -0.22, 0.18) if cuts else 1.0
    drawn = jax.random.normal(own_key, shape, jnp.float32) * deviation * loudness
    return jnp.minimum(jnp.maximum(drawn, -bound), bound).astype(kind)


def setup_inputs(seed: int = 0) -> dict:
    splits = jax.random.split(jax.random.key(seed), 16)
    tokens = gaussian(splits[0], (BATCH, LENGTH, D), 1.0, 6.0, ((0, 16), (1, 8)))
    segment_ids = jax.vmap(lambda own: jnp.searchsorted(jnp.cumsum(uneven(own, 4, LENGTH, LENGTH - BLK // 2, 0)), jnp.arange(LENGTH), side="right"))(jax.random.split(splits[1], BATCH)).reshape((BATCH, LENGTH)).astype(jnp.int32)
    cotangent = gaussian(splits[2], (BATCH, LENGTH, D), 1.0, 6.0, ((0, 16), (1, 8)))
    ln1_gain = jnp.clip(1.0 + 0.18 * jax.random.normal(splits[3], (D,), jnp.float32), 0.099609375, 1.8984375).astype(jnp.bfloat16)
    ln1_bias = gaussian(splits[4], (D,), 0.3, 3.0, ((0, 16),))
    qkv_weight = gaussian(splits[5], (D, 3 * D), D ** -0.5, 0.1875, ((0, 16),))
    qkv_bias = gaussian(splits[6], (2 * D,), 0.5, 3.0, ((0, 16),))
    out_weight = gaussian(splits[7], (D, D), (D // 8) ** -0.5, 0.5, ((0, 16),))
    out_bias = gaussian(splits[8], (D,), 0.3, 3.0, ((0, 16),))
    ln2_gain = jnp.clip(1.0 + 0.18 * jax.random.normal(splits[9], (D,), jnp.float32), 0.099609375, 1.8984375).astype(jnp.bfloat16)
    ln2_bias = gaussian(splits[10], (D,), 0.3, 3.0, ((0, 16),))
    fc1_weight = gaussian(splits[11], (D, FF), D ** -0.5, 0.1875, ((0, 16),))
    fc1_bias = gaussian(splits[12], (FF,), 0.5, 3.0, ((0, 16),))
    fc2_weight = gaussian(splits[13], (FF, D), (FF // 2) ** -0.5, 0.125, ((0, 16),))
    fc2_bias = gaussian(splits[14], (D,), 0.3, 3.0, ((0, 16),))
    return dict(tokens=tokens, segment_ids=segment_ids, cotangent=cotangent, ln1_gain=ln1_gain, ln1_bias=ln1_bias, qkv_weight=qkv_weight, qkv_bias=qkv_bias, out_weight=out_weight, out_bias=out_bias, ln2_gain=ln2_gain, ln2_bias=ln2_bias, fc1_weight=fc1_weight, fc1_bias=fc1_bias, fc2_weight=fc2_weight, fc2_bias=fc2_bias)


@jax.custom_vjp
def low(v):
    return lax.optimization_barrier(v.astype(jnp.bfloat16)).astype(jnp.float32)

@jax.custom_vjp
def low_back(v):
    return v

def low_keep(v):
    return (low(v), None)

def low_pass(kept, grad):
    return (grad,)

def back_keep(v):
    return (v, None)

def back_low(kept, grad):
    return (low(grad),)
low.defvjp(low_keep, low_pass)
low_back.defvjp(back_keep, back_low)

def layer_norm(values, gain_vec, bias_vec):
    center = values - lax.optimization_barrier(jnp.mean(values, axis=-1, keepdims=True))
    spread = lax.optimization_barrier(jnp.mean(center * center, axis=-1, keepdims=True))
    return center * lax.rsqrt(spread + 1e-05) * gain_vec + bias_vec

def highest(left, right):
    return jnp.dot(left, right, precision=lax.Precision.HIGHEST, preferred_element_type=jnp.float32)

def head_slopes():
    return 2.0 ** (-8.0 * jnp.arange(1, HEADS + 1, dtype=jnp.float32) / HEADS) * (4.0 / LENGTH)

def one_row(weights, x_row, seg_row):
    gain_one, bias_one, qkv_mat, qkv_vec, out_mat, out_vec, gain_two, bias_two, up_mat, up_vec, down_mat, down_vec = weights
    normed = low(layer_norm(x_row, gain_one, bias_one))
    merged_bias = jnp.concatenate([qkv_vec[:D], jnp.zeros((D,), jnp.float32), qkv_vec[D:]])
    merged = low_back(highest(normed, qkv_mat) + merged_bias)
    query = low(merged[:, :D]).reshape(LENGTH, HEADS, HEAD_DIM)
    key_part = low(merged[:, D:2 * D]).reshape(LENGTH, HEADS, HEAD_DIM)
    value_part = low(merged[:, 2 * D:]).reshape(LENGTH, HEADS, HEAD_DIM)
    positions = jnp.arange(LENGTH, dtype=jnp.int32)
    distance = positions[:, None] - positions[None, :]
    scores = jnp.einsum('ihd,jhd->hij', query, key_part, precision=lax.Precision.HIGHEST) * HEAD_DIM ** (-0.5)
    scores = low_back(scores - head_slopes()[:, None, None] * distance.astype(jnp.float32))
    allowed = (seg_row[:, None] == seg_row[None, :]) & (distance >= 0)
    scores = jnp.where(allowed[None], scores, -1e+30)
    top_score = lax.optimization_barrier(jnp.max(scores, axis=-1, keepdims=True))
    expo = jnp.exp(scores - top_score)
    normal = lax.optimization_barrier(jnp.sum(expo, axis=-1, keepdims=True))
    probs = expo / normal
    log_sums = (top_score + jnp.log(normal))[:, :, 0]
    mixed = jnp.einsum('hij,jhd->ihd', low(probs), value_part, precision=lax.Precision.HIGHEST).reshape(LENGTH, D)
    mixed = low_back(low(mixed))
    branch = low_back(highest(mixed, out_mat) + out_vec)
    middle = x_row + branch
    normed_two = low(layer_norm(middle, gain_two, bias_two))
    hidden = low_back(highest(normed_two, up_mat) + up_vec)
    active = low(jax.nn.gelu(hidden, approximate=True))
    result = middle + low_back(highest(active, down_mat) + down_vec)
    return (result, log_sums)

def reference(tokens, segment_ids, cotangent, ln1_gain, ln1_bias, qkv_weight, qkv_bias, out_weight, out_bias, ln2_gain, ln2_bias, fc1_weight, fc1_bias, fc2_weight, fc2_bias):
    params = tuple((p_arg.astype(jnp.float32) for p_arg in (ln1_gain, ln1_bias, qkv_weight, qkv_bias, out_weight, out_bias, ln2_gain, ln2_bias, fc1_weight, fc1_bias, fc2_weight, fc2_bias)))
    inputs = tokens.astype(jnp.float32)

    def forward(weights, values):

        def scan_step(running, row_pair):
            result, log_sums = jax.checkpoint(one_row)(weights, row_pair[0], row_pair[1])
            return (running, (result, log_sums))
        _, (results, all_sums) = lax.scan(scan_step, jnp.zeros((), jnp.float32), (values, segment_ids))
        return (results, all_sums)
    results, pullback, all_sums = jax.vjp(forward, params, inputs, has_aux=True)
    grad_params, grad_inputs = pullback(cotangent.astype(jnp.float32))
    g_one, b_one, g_qkv, g_qkvb, g_out, g_outb, g_two, b_two, g_up, g_upb, g_down, g_downb = grad_params
    return (results.astype(jnp.bfloat16), grad_inputs, g_one, b_one, g_qkv, g_qkvb, g_out, g_outb, g_two, b_two, g_up, g_upb, g_down, g_downb, all_sums)
```

```python
import functools

import jax
import jax.numpy as jnp
from jax import lax
from jax.experimental import pallas as pl
from jax.experimental.pallas import tpu as pltpu
from jax.sharding import PartitionSpec as P

D = 1024
HEADS = 16
HEAD_DIM = 64
LENGTH = 2048
BLK = 256
BF = jnp.bfloat16
F32 = jnp.float32
BIG = 2.0**100
MIB = 2**20
NONE = slice(None)

QKV_SEGS = ((0, 0, 0, 1), (0, 1, 1, 1), (0, 2, 2, 1))
REST_SEGS = (
    (1, 0, 0, 1),
    (2, 0, 0, 2),
    (2, 1, 2, 1),
    (2, 2, 3, 1),
    (3, 0, 0, 1),
    (3, 1, 1, 1),
    (3, 2, 2, 2),
)


def place():
    c = lax.axis_index("ctx")
    f = lax.axis_index("fsdp")
    return f // 4, ((f // 2) % 2) * 2 + c // 4, c % 4, f % 2


def device(x, y, z, core):
    return {"ctx": (y % 2) * 4 + z, "fsdp": x * 4 + (y // 2) * 2 + core}


class Links:
    def __init__(self, send, recv):
        self.send, self.recv, self.used = send, recv, 0
        self.x, self.y, self.z, self.core = place()
        self.yh, self.yl = self.y // 2, self.y % 2
        self.me = self.yl * 4 + self.z

    def peers(self, axis):
        x, y, z, c = self.x, self.y, self.z, self.core
        if axis == "x":
            return [device((x + j) % 4, y, z, c) for j in (1, 2, 3)]
        if axis == "y":
            return [device(x, (y + j) % 4, z, c) for j in (1, 2, 3)]
        if axis == "z":
            return [device(x, y, (z + j) % 4, c) for j in (1, 2, 3)]
        return [device(x, y, z, 1 - c)]

    def rows_peers(self):
        out = []
        for j in range(1, 8):
            t = (self.me + j) % 8
            out.append((t, device(self.x, self.yh * 2 + t // 4, t % 4, self.core)))
        return out

    def barrier(self):
        everyone = self.peers("x") + self.peers("y") + self.peers("z") + self.peers("core")
        for j in (1, 2, 3):
            everyone.append(device(self.x, self.yh * 2 + 1 - self.yl, (self.z + j) % 4, self.core))
        sem = pltpu.get_barrier_semaphore()
        for who in everyone:
            pl.semaphore_signal(sem, inc=1, device_id=who)
        pl.semaphore_wait(sem, len(everyone))

    def to(self, src, dst, who):
        i = self.used
        self.used += 1
        copy = pltpu.make_async_remote_copy(
            src_ref=src,
            dst_ref=dst,
            send_sem=self.send.at[i],
            recv_sem=self.recv.at[i],
            device_id=who,
        )
        copy.start()
        return copy

    def local(self, src, dst):
        i = self.used
        self.used += 1
        copy = pltpu.make_async_copy(src, dst, self.send.at[i])
        copy.start()
        return copy


def wait_recv(copies):
    for copy in copies:
        copy.wait_recv()


def wait_send(copies):
    for copy in copies:
        copy.wait_send()


class Gather:
    def __init__(self, links, full, shard, seg):
        tensor, self.order, first, count = seg
        self.links, self.full, self.shard = links, full, shard
        self.blocked = tensor == 3
        if self.blocked:
            self.units = (pl.ds(first, count),)
            self.all_cols = pl.ds(0, D)
            width = D // 4
            self.z_cols = pl.ds(pl.multiple_of(links.z * width, width), width)
        else:
            self.units = ()
            self.all_cols = pl.ds(first * D, count * D)
            width = count * D // 4
            self.z_cols = pl.ds(pl.multiple_of(first * D + links.z * width, width), width)
        self.sent = []

    def view(self, x, yh, yl, cols):
        return self.full.at[(x, yh, self.links.core) + self.units + (yl, NONE, cols)]

    def own(self, cols):
        return self.shard.at[self.units + (self.links.yl, NONE, cols)]

    def push(self, src, dst, axis):
        now = [self.links.to(src, dst, who) for who in self.links.peers(axis)]
        self.sent += now
        return now

    def stage1(self):
        k = self.links
        cols = self.all_cols if self.order == 0 else self.z_cols
        dst = self.view(k.x, k.yh, k.yl, cols)
        self.kept = k.local(self.own(cols), dst)
        self.first = self.push(self.own(cols), dst, "x" if self.order == 1 else "y")

    def stage2(self):
        k = self.links
        self.kept.wait()
        wait_recv(self.first)
        if self.order == 0:
            part = self.view(k.x, NONE, NONE, self.all_cols)
            self.last = self.push(part, part, "x")
        elif self.order == 1:
            part = self.view(NONE, k.yh, k.yl, self.z_cols)
            self.second = self.push(part, part, "z")
        else:
            part = self.view(k.x, NONE, NONE, self.z_cols)
            self.second = self.push(part, part, "x")

    def stage3(self):
        k = self.links
        if self.order == 0:
            return
        wait_recv(self.second)
        if self.order == 1:
            part = self.view(NONE, k.yh, k.yl, self.all_cols)
            self.last = self.push(part, part, "y")
        else:
            part = self.view(NONE, NONE, NONE, self.z_cols)
            self.last = self.push(part, part, "z")

    def cross(self):
        wait_recv(self.last)
        part = self.view(NONE, NONE, NONE, self.all_cols)
        self.swapped = self.push(part, part, "core")

    def finish(self):
        wait_recv(self.swapped)

    def drain(self):
        wait_send(self.sent)


def small_row(pack, row):
    pieces = []
    for x in range(4):
        for yh in range(2):
            pieces.append(
                pack[x, yh, 0, row : row + 1, :].astype(F32)
                + pack[x, yh, 1, row : row + 1, :].astype(F32)
            )
    return jnp.concatenate(pieces, axis=1)


def dot_nt(a, b):
    return lax.dot_general(a, b, (((1,), (1,)), ((), ())), preferred_element_type=F32)


def dot_tn(a, b):
    return lax.dot_general(a, b, (((0,), (0,)), ((), ())), preferred_element_type=F32)


def dot(a, b):
    return jnp.dot(a, b, preferred_element_type=F32)


def slope_of(links, h, shape):
    power = (links.me * 2 + h + 1).astype(F32) * -0.5
    return jnp.exp2(jnp.full(shape, power, F32)) * (4.0 / LENGTH)


def extend(links, seg_ref, qkv_ref, kx_ref, qx_ref, h, t):
    rows = pl.ds(t * BLK, BLK)
    seg = jnp.broadcast_to(seg_ref[t, 0:1, :].astype(F32), (128, BLK)).T
    lane = lax.broadcasted_iota(jnp.int32, (BLK, 128), 1)
    mine = (lane // 64) == h
    e = lane - 64 * (1 - h)
    where = lax.broadcasted_iota(jnp.int32, (BLK, 128), 0) + t * BLK
    bias = slope_of(links, h, (BLK, 128)) * where.astype(F32)
    high = bias.astype(BF).astype(F32)
    mid = (bias - high).astype(BF).astype(F32)
    low = bias - high - mid
    doc = (e - 3).astype(F32)
    is_doc = (e >= 3) & (e <= 6)
    same = seg == doc
    key_extra = jnp.where(is_doc & jnp.logical_not(same), 1.0, 0.0)
    key_extra = jnp.where(e == 0, high, jnp.where(e == 1, mid, jnp.where(e == 2, low, key_extra)))
    query_extra = jnp.where(is_doc & same, -BIG, 0.0)
    query_extra = jnp.where((e >= 0) & (e <= 2), 1.0, query_extra)
    query = qkv_ref[0, rows, :].astype(F32) * 0.125
    key = qkv_ref[1, rows, :].astype(F32)
    kx_ref[h, rows, :] = jnp.where(mine, key, key_extra).astype(BF)
    qx_ref[h, rows, :] = jnp.where(mine, query, query_extra).astype(BF)


def attend(links, kx_ref, qx_ref, vt_ref, ot_ref, lse_ref, h, i):
    keys = BLK * (i + 1)
    qb = qx_ref[h, BLK * i : keys, :]
    down = lax.broadcasted_iota(jnp.int32, (BLK, BLK), 0)
    across = lax.broadcasted_iota(jnp.int32, (BLK, BLK), 1)
    edge = jnp.where(down <= across, dot_nt(kx_ref[h, BLK * i : keys, :], qb), -BIG)
    top = jnp.max(edge, axis=0, keepdims=True)
    if i:
        past = dot_nt(kx_ref[h, 0 : BLK * i, :], qb)
        top = jnp.maximum(top, jnp.max(past, axis=0, keepdims=True))
    edge = jnp.exp(edge - top)
    total = jnp.sum(edge, axis=0, keepdims=True)
    out = dot(vt_ref[h, :, BLK * i : keys], edge.astype(BF))
    if i:
        past = jnp.exp(past - top)
        total = total + jnp.sum(past, axis=0, keepdims=True)
        out = out + dot(vt_ref[h, :, 0 : BLK * i], past.astype(BF))
    ot_ref[h, :, BLK * i : keys] = out / total
    where = (lax.broadcasted_iota(jnp.int32, (1, BLK), 1) + BLK * i).astype(F32)
    lse_ref[h, :, BLK * i : keys] = jnp.broadcast_to(
        top + jnp.log(total) - slope_of(links, h, (1, BLK)) * where, (8, BLK)
    )


def forward_kernel(
    tokens,
    seg,
    small,
    wq_in,
    wo_in,
    w1_in,
    w2_in,
    wq_out,
    wo,
    w1,
    w2,
    pack_out,
    normed_out,
    qkv_out,
    ot,
    lse,
    mixed,
    lse_all,
    wq,
    pack,
    seg_all,
    row,
    merged,
    qkv,
    kx,
    qx,
    vt,
    mixed_send,
    send,
    recv,
):
    k = Links(send, recv)
    k.barrier()
    sent, kept = [], []

    kept_small = k.local(small, pack.at[k.x, k.yh, k.core])
    small_x = [k.to(small, pack.at[k.x, k.yh, k.core], who) for who in k.peers("x")]
    fulls, shards = (wq, wo, w1, w2), (wq_in, wo_in, w1_in, w2_in)
    first = [Gather(k, fulls[s[0]], shards[s[0]], s) for s in QKV_SEGS]
    rest = [Gather(k, fulls[s[0]], shards[s[0]], s) for s in REST_SEGS]
    for g in first:
        g.stage1()
    kept_seg = k.local(seg, seg_all.at[k.me])
    segs = [k.to(seg, seg_all.at[k.me], who) for _, who in k.rows_peers()]
    for g in first:
        g.stage2()
    kept_small.wait()
    wait_recv(small_x)
    part = pack.at[:, k.yh, k.core]
    small_y = [k.to(part, part, k.peers("y")[1])]
    for g in rest:
        g.stage1()
    for g in first:
        g.stage3()
    wait_recv(small_y)
    part = pack.at[:, :, k.core]
    small_c = [k.to(part, part, k.peers("core")[0])]

    values = tokens[...].astype(F32)
    center = values - jnp.mean(values, axis=1, keepdims=True)
    center = center * lax.rsqrt(jnp.mean(center * center, axis=1, keepdims=True) + 1e-05)
    wait_recv(small_c)
    normed_out[...] = (center * small_row(pack, 0) + small_row(pack, 1)).astype(BF)
    pack_out[...] = pack[...]
    pieces = []
    for f in range(16):
        pieces.append(pack[f // 4, (f // 2) % 2, f % 2, 6:7, :].astype(F32))
    row[...] = jnp.broadcast_to(
        jnp.concatenate(pieces[:8] + [jnp.zeros((1, D), F32)] + pieces[8:], axis=1), (8, 3 * D)
    )
    for g in first:
        g.cross()
    for g in rest:
        g.stage2()
    for g in first:
        g.finish()
    kept.append(k.local(wq, wq_out))

    @pl.loop(0, 12)
    def _(n):
        cols = pl.ds(pl.multiple_of(n * 256, 256), 256)
        weight = wq[:, :, :, :, :, cols].reshape(D, 256)
        block = (dot(normed_out[...], weight) + row[0:1, cols]).astype(BF)
        merged[n // 4, 2 * (n % 4)] = block[:, :128]
        merged[n // 4, 2 * (n % 4) + 1] = block[:, 128:]

    mine = pl.ds(pl.multiple_of(k.me * BLK, BLK), BLK)
    kept_qkv = k.local(merged.at[:, k.me], qkv.at[:, mine])
    moved = [k.to(merged.at[:, t], qkv.at[:, mine], who) for t, who in k.rows_peers()]
    for g in rest:
        g.stage3()
    kept_seg.wait()
    wait_recv(segs)
    kept_qkv.wait()
    wait_recv(moved)
    kept.append(k.local(qkv, qkv_out))

    @pl.loop(0, 8)
    def _(t):
        for h in range(2):
            extend(k, seg_all, qkv, kx, qx, h, t)

    for t in range(8):
        flipped = qkv[2, BLK * t : BLK * (t + 1), :].astype(F32).T.astype(BF)
        for h in range(2):
            vt[h, :, BLK * t : BLK * (t + 1)] = flipped[64 * h : 64 * (h + 1)]

    for i in range(8):

        @pl.loop(0, 2)
        def _(h):
            attend(k, kx, qx, vt, ot, lse, h, i)

        both = jnp.concatenate(
            [ot[0, :, BLK * i : BLK * (i + 1)], ot[1, :, BLK * i : BLK * (i + 1)]], axis=0
        )
        mixed_send[i] = both.T.astype(BF)

    cols = pl.ds(pl.multiple_of(k.me * 128, 128), 128)
    kept.append(k.local(mixed_send.at[k.me], mixed.at[:, cols]))
    back = [k.to(mixed_send.at[t], mixed.at[:, cols], who) for t, who in k.rows_peers()]
    part = pl.ds(pl.multiple_of(k.me * BLK, BLK), BLK)
    kept.append(k.local(lse.at[:, :, part], lse_all.at[k.me]))
    for t, who in k.rows_peers():
        part = pl.ds(pl.multiple_of(t * BLK, BLK), BLK)
        back.append(k.to(lse.at[:, :, part], lse_all.at[k.me], who))
    for g in rest:
        g.cross()
    wait_recv(back)
    for g in rest:
        g.finish()
    for copy in kept:
        copy.wait()
    for g in first + rest:
        g.drain()
    wait_send(small_x + small_y + small_c + segs + moved + back)


def full_shape(cols):
    return (4, 2, 2, 2, 32, cols)


def forward_call(tokens, seg, small, wq, wo, w1, w2):
    hbm = pl.BlockSpec(memory_space=pl.ANY)
    vmem = pl.BlockSpec(memory_space=pltpu.VMEM)
    out = jax.ShapeDtypeStruct
    return pl.pallas_call(
        forward_kernel,
        name="forward",
        out_shape=(
            out(full_shape(3 * D), BF),
            out(full_shape(D), BF),
            out(full_shape(4 * D), BF),
            out((4, 2, 2, 4, 2, 32, D), BF),
            out((4, 2, 2, 16, 128), BF),
            out((BLK, D), BF),
            out((3, LENGTH, 128), BF),
            out((2, 64, LENGTH), F32),
            out((2, 8, LENGTH), F32),
            out((BLK, D), BF),
            out((8, 2, 8, BLK), F32),
        ),
        in_specs=[vmem, vmem, vmem, hbm, hbm, hbm, hbm],
        out_specs=(hbm, hbm, hbm, hbm, vmem, vmem, hbm, vmem, vmem, hbm, hbm),
        scratch_shapes=[
            pltpu.VMEM(full_shape(3 * D), BF),
            pltpu.VMEM((4, 2, 2, 16, 128), BF),
            pltpu.VMEM((8, 8, BLK), jnp.int32),
            pltpu.VMEM((8, 3 * D), F32),
            pltpu.VMEM((3, 8, BLK, 128), BF),
            pltpu.VMEM((3, LENGTH, 128), BF),
            pltpu.VMEM((2, LENGTH, 128), BF),
            pltpu.VMEM((2, LENGTH, 128), BF),
            pltpu.VMEM((2, 64, LENGTH), BF),
            pltpu.VMEM((8, BLK, 128), BF),
            pltpu.SemaphoreType.DMA((170,)),
            pltpu.SemaphoreType.DMA((170,)),
        ],
        compiler_params=pltpu.CompilerParams(
            collective_id=0, has_side_effects=True, vmem_limit_bytes=50 * MIB
        ),
    )(
        tokens,
        seg,
        small,
        wq.reshape(2, 32, 3 * D),
        wo.reshape(2, 32, D),
        w1.reshape(2, 32, 4 * D),
        w2.reshape(4, 2, 32, D),
    )


def small_pack(ln1_gain, ln1_bias, ln2_gain, ln2_bias, out_bias, fc2_bias, qkv_bias, fc1_bias):
    core = lax.axis_index("fsdp") % 2
    six = jnp.stack([ln1_gain, ln1_bias, ln2_gain, ln2_bias, out_bias, fc2_bias])
    none = jnp.zeros_like(six)
    halves = jnp.where(
        core == 0, jnp.concatenate([six, none], 1), jnp.concatenate([none, six], 1)
    )
    return jnp.concatenate(
        [halves, qkv_bias[None], fc1_bias.reshape(2, 128), jnp.zeros((7, 128), BF)], 0
    )


def unpack_row(pack, row):
    return (pack[:, :, 0, row] + pack[:, :, 1, row]).reshape(D)


def layer_norm(values, gain_vec, bias_vec):
    center = values - jnp.mean(values, axis=-1, keepdims=True)
    spread = jnp.mean(center * center, axis=-1, keepdims=True)
    return center * lax.rsqrt(spread + 1e-05) * gain_vec + bias_vec


def gelu_tanh(values):
    return jax.nn.gelu(values, approximate=True)


def matmul_tn(left, right):
    return lax.dot_general(
        left, right, (((0,), (0,)), ((), ())), preferred_element_type=jnp.float32
    )


def matmul_nt(left, right):
    return lax.dot_general(
        left, right, (((1,), (1,)), ((), ())), preferred_element_type=jnp.float32
    )


def matmul(left, right):
    return jnp.dot(left, right, preferred_element_type=jnp.float32)


def head_slopes():
    return 2.0 ** (-8.0 * jnp.arange(1, HEADS + 1, dtype=jnp.float32) / HEADS) * (4.0 / LENGTH)


def key_spans(key_count):
    width_now = 512
    return [(offset, width_now) for offset in range(0, key_count, width_now)]


def block_scores(query, query_seg, query_pos, key_rows, key_seg, first_key):
    row_count = key_rows.shape[0]
    key_count = key_rows.shape[1]
    key_part = key_rows[:, :, :D].reshape(row_count, key_count, HEADS, HEAD_DIM)
    value_part = key_rows[:, :, D:].reshape(row_count, key_count, HEADS, HEAD_DIM)
    scores = jnp.einsum(
        "rihd,rjhd->rhij", query, key_part, preferred_element_type=jnp.float32
    ) * HEAD_DIM ** (-0.5)
    key_pos = first_key + jnp.arange(key_count, dtype=jnp.int32)
    distance = query_pos[:, None] - key_pos[None, :]
    scores = scores - head_slopes()[:, None, None] * distance.astype(jnp.float32)
    allowed = (query_seg[:, :, None] == key_seg[:, None, :]) & (distance >= 0)[None]
    return (scores, allowed[:, None], key_part, value_part)


def local(
    tokens,
    segment_ids,
    cotangent,
    ln1_gain,
    ln1_bias,
    qkv_weight,
    qkv_bias,
    out_weight,
    out_bias,
    ln2_gain,
    ln2_bias,
    fc1_weight,
    fc1_bias,
    fc2_weight,
    fc2_bias,
):
    row_count, block_len, _ = tokens.shape
    flat_rows = row_count * block_len
    full_length = block_len * lax.axis_size("ctx")
    small = small_pack(
        ln1_gain, ln1_bias, ln2_gain, ln2_bias, out_bias, fc2_bias, qkv_bias, fc1_bias
    )
    (qkv_mat, out_mat, up_mat, down_mat, pack, normed, qkv_heads, mixed_heads, lse_heads, mixed, lse_all) = forward_call(
        tokens.reshape(flat_rows, D),
        jnp.broadcast_to(segment_ids, (8, block_len)),
        small,
        qkv_weight,
        out_weight,
        fc1_weight,
        fc2_weight,
    )
    qkv_mat = qkv_mat.reshape(D, 3 * D)
    out_mat = out_mat.reshape(D, D)
    up_mat = up_mat.reshape(D, 4 * D)
    down_mat = down_mat.reshape(4 * D, D)
    gain_one_f = unpack_row(pack, 0).astype(jnp.float32)
    bias_one_f = unpack_row(pack, 1).astype(jnp.float32)
    gain_two_f = unpack_row(pack, 2).astype(jnp.float32)
    bias_two_f = unpack_row(pack, 3).astype(jnp.float32)
    out_vec = unpack_row(pack, 4)
    down_vec = unpack_row(pack, 5)
    qkv_vec = pack[:, :, :, 6].reshape(2 * D)
    up_vec = pack[:, :, :, 7:9].reshape(4 * D)
    inputs = tokens.astype(jnp.float32).reshape(flat_rows, D)
    merged_bias = jnp.concatenate([qkv_vec[:D], jnp.zeros((D,), BF), qkv_vec[D:]]).astype(jnp.float32)
    merged = (matmul(normed, qkv_mat) + merged_bias).astype(jnp.bfloat16)
    query = merged[:, :D].reshape(row_count, block_len, HEADS, HEAD_DIM)
    key_values = merged[:, D:].reshape(row_count, block_len, 2 * D)
    query_pos = lax.axis_index("ctx") * block_len + jnp.arange(block_len, dtype=jnp.int32)
    log_sums = lse_all[:, :, 0].reshape(1, HEADS, block_len)
    mixed_exact = mixed.astype(jnp.float32).reshape(row_count, block_len, HEADS, HEAD_DIM)
    middle = inputs + matmul(mixed, out_mat) + out_vec.astype(jnp.float32)
    normed_two = layer_norm(middle, gain_two_f, bias_two_f).astype(jnp.bfloat16)
    hidden = matmul(normed_two, up_mat) + up_vec.astype(jnp.float32)
    active = gelu_tanh(hidden).astype(jnp.bfloat16)
    output = middle + matmul(active, down_mat) + down_vec.astype(jnp.float32)
    qkv_back, out_back, up_back, down_back = qkv_mat, out_mat, up_mat, down_mat
    grad_down = cotangent.reshape(flat_rows, D)
    grad_output = grad_down.astype(jnp.float32)
    fc2_weight_grad = matmul_tn(active, grad_down)
    fc2_bias_grad = jnp.sum(grad_output, axis=0)
    grad_active = matmul_nt(grad_down, down_back)
    _, gelu_pull = jax.vjp(gelu_tanh, hidden)
    grad_hidden = gelu_pull(grad_active)[0].astype(jnp.bfloat16)
    fc1_weight_grad = matmul_tn(normed_two, grad_hidden)
    fc1_bias_grad = jnp.sum(grad_hidden.astype(jnp.float32), axis=0)
    grad_normed_two = matmul_nt(grad_hidden, up_back)
    _, norm_pull_two = jax.vjp(layer_norm, middle, gain_two_f, bias_two_f)
    grad_middle_part, ln2_gain_grad, ln2_bias_grad = norm_pull_two(grad_normed_two)
    grad_middle = grad_output + grad_middle_part
    grad_branch = grad_middle.astype(jnp.bfloat16)
    out_weight_grad = matmul_tn(mixed, grad_branch)
    out_bias_grad = jnp.sum(grad_branch.astype(jnp.float32), axis=0)
    grad_mixed = (
        matmul_nt(grad_branch, out_back)
        .astype(jnp.bfloat16)
        .reshape(row_count, block_len, HEADS, HEAD_DIM)
    )
    delta = jnp.swapaxes(jnp.sum(grad_mixed.astype(jnp.float32) * mixed_exact, axis=-1), 1, 2)
    first_row = jnp.int32(0)
    grad_query = jnp.zeros((row_count, block_len, HEADS, HEAD_DIM), jnp.float32)
    grad_keys = jnp.zeros((row_count, full_length, 2 * D), jnp.float32)
    key_rows = lax.all_gather(key_values, "ctx", axis=1, tiled=True)
    key_seg = lax.all_gather(segment_ids, "ctx", axis=1, tiled=True)
    for offset, width_now in key_spans(key_rows.shape[1]):
        scores, allowed, key_part, value_part = block_scores(
            query,
            segment_ids,
            query_pos,
            key_rows[:, offset : offset + width_now],
            key_seg[:, offset : offset + width_now],
            first_row + offset,
        )
        probs = jnp.where(allowed, jnp.exp(scores - log_sums[..., None]), 0.0)
        grad_probs = jnp.einsum(
            "rihd,rjhd->rhij", grad_mixed, value_part, preferred_element_type=jnp.float32
        )
        grad_scores = (probs * (grad_probs - delta[..., None])).astype(jnp.bfloat16)
        grad_query = grad_query + jnp.einsum(
            "rhij,rjhd->rihd", grad_scores, key_part, preferred_element_type=jnp.float32
        ) * HEAD_DIM ** (-0.5)
        grad_key = jnp.einsum(
            "rhij,rihd->rjhd", grad_scores, query, preferred_element_type=jnp.float32
        ) * HEAD_DIM ** (-0.5)
        grad_value = jnp.einsum(
            "rhij,rihd->rjhd",
            probs.astype(jnp.bfloat16),
            grad_mixed,
            preferred_element_type=jnp.float32,
        )
        key_term = jnp.concatenate(
            [
                grad_key.reshape(row_count, width_now, D),
                grad_value.reshape(row_count, width_now, D),
            ],
            axis=-1,
        )
        place_at = first_row + offset
        previous = lax.dynamic_slice_in_dim(grad_keys, place_at, width_now, 1)
        grad_keys = lax.dynamic_update_slice_in_dim(grad_keys, previous + key_term, place_at, 1)
    grad_query, grad_keys = (grad_query, grad_keys)
    own_key_grads = lax.psum_scatter(
        grad_keys.astype(jnp.bfloat16), "ctx", scatter_dimension=1, tiled=True
    ).astype(jnp.float32)
    grad_merged = jnp.concatenate(
        [grad_query.reshape(flat_rows, D), own_key_grads.reshape(flat_rows, 2 * D)], axis=-1
    ).astype(jnp.bfloat16)
    qkv_weight_grad = matmul_tn(normed, grad_merged)
    merged_sums = jnp.sum(grad_merged.astype(jnp.float32), axis=0)
    qkv_bias_grad = jnp.concatenate([merged_sums[:D], merged_sums[2 * D :]])
    grad_normed = matmul_nt(grad_merged, qkv_back)
    _, norm_pull_one = jax.vjp(layer_norm, inputs, gain_one_f, bias_one_f)
    grad_input_part, ln1_gain_grad, ln1_bias_grad = norm_pull_one(grad_normed)
    input_grad = (grad_middle + grad_input_part).reshape(row_count, block_len, D)
    shard_grads = (
        lax.psum_scatter(
            ln1_gain_grad.astype(jnp.bfloat16), "fsdp", scatter_dimension=0, tiled=True
        ).astype(jnp.float32),
        lax.psum_scatter(
            ln1_bias_grad.astype(jnp.bfloat16), "fsdp", scatter_dimension=0, tiled=True
        ).astype(jnp.float32),
        lax.psum_scatter(
            qkv_weight_grad.astype(jnp.bfloat16), "fsdp", scatter_dimension=0, tiled=True
        ).astype(jnp.float32),
        lax.psum_scatter(
            qkv_bias_grad.astype(jnp.bfloat16), "fsdp", scatter_dimension=0, tiled=True
        ).astype(jnp.float32),
        lax.psum_scatter(
            out_weight_grad.astype(jnp.bfloat16), "fsdp", scatter_dimension=0, tiled=True
        ).astype(jnp.float32),
        lax.psum_scatter(
            out_bias_grad.astype(jnp.bfloat16), "fsdp", scatter_dimension=0, tiled=True
        ).astype(jnp.float32),
        lax.psum_scatter(
            ln2_gain_grad.astype(jnp.bfloat16), "fsdp", scatter_dimension=0, tiled=True
        ).astype(jnp.float32),
        lax.psum_scatter(
            ln2_bias_grad.astype(jnp.bfloat16), "fsdp", scatter_dimension=0, tiled=True
        ).astype(jnp.float32),
        lax.psum_scatter(
            fc1_weight_grad.astype(jnp.bfloat16), "fsdp", scatter_dimension=0, tiled=True
        ).astype(jnp.float32),
        lax.psum_scatter(
            fc1_bias_grad.astype(jnp.bfloat16), "fsdp", scatter_dimension=0, tiled=True
        ).astype(jnp.float32),
        lax.psum_scatter(
            fc2_weight_grad.astype(jnp.bfloat16), "fsdp", scatter_dimension=0, tiled=True
        ).astype(jnp.float32),
        lax.psum_scatter(
            fc2_bias_grad.astype(jnp.bfloat16), "fsdp", scatter_dimension=0, tiled=True
        ).astype(jnp.float32),
    )
    g_one, b_one, g_qkv, g_qkvb, g_out, g_outb, g_two, b_two, g_up, g_upb, g_down, g_downb = (
        lax.psum(shard_grads[0].astype(jnp.bfloat16), "ctx").astype(jnp.float32),
        lax.psum(shard_grads[1].astype(jnp.bfloat16), "ctx").astype(jnp.float32),
        lax.psum(shard_grads[2].astype(jnp.bfloat16), "ctx").astype(jnp.float32),
        lax.psum(shard_grads[3].astype(jnp.bfloat16), "ctx").astype(jnp.float32),
        lax.psum(shard_grads[4].astype(jnp.bfloat16), "ctx").astype(jnp.float32),
        lax.psum(shard_grads[5].astype(jnp.bfloat16), "ctx").astype(jnp.float32),
        lax.psum(shard_grads[6].astype(jnp.bfloat16), "ctx").astype(jnp.float32),
        lax.psum(shard_grads[7].astype(jnp.bfloat16), "ctx").astype(jnp.float32),
        lax.psum(shard_grads[8].astype(jnp.bfloat16), "ctx").astype(jnp.float32),
        lax.psum(shard_grads[9].astype(jnp.bfloat16), "ctx").astype(jnp.float32),
        lax.psum(shard_grads[10].astype(jnp.bfloat16), "ctx").astype(jnp.float32),
        lax.psum(shard_grads[11].astype(jnp.bfloat16), "ctx").astype(jnp.float32),
    )
    return (
        output.astype(jnp.bfloat16).reshape(row_count, block_len, D),
        input_grad,
        g_one,
        b_one,
        g_qkv,
        g_qkvb,
        g_out,
        g_outb,
        g_two,
        b_two,
        g_up,
        g_upb,
        g_down,
        g_downb,
        log_sums,
    )


def solution(mesh):
    placed = (
        P("fsdp", "ctx", None),
        P("fsdp", "ctx"),
        P("fsdp", "ctx", None),
        P("fsdp"),
        P("fsdp"),
        P("fsdp", None),
        P("fsdp"),
        P("fsdp", None),
        P("fsdp"),
        P("fsdp"),
        P("fsdp"),
        P("fsdp", None),
        P("fsdp"),
        P("fsdp", None),
        P("fsdp"),
    )
    return jax.shard_map(
        local,
        mesh=mesh,
        in_specs=placed,
        out_specs=(
            P("fsdp", "ctx", None),
            P("fsdp", "ctx", None),
            P("fsdp"),
            P("fsdp"),
            P("fsdp", None),
            P("fsdp"),
            P("fsdp", None),
            P("fsdp"),
            P("fsdp"),
            P("fsdp"),
            P("fsdp", None),
            P("fsdp"),
            P("fsdp", None),
            P("fsdp"),
            P("fsdp", None, "ctx"),
        ),
        check_vma=False,
    )
```

```python
import functools

import jax
import jax.numpy as jnp
from jax import lax
from jax.experimental import pallas as pl
from jax.experimental.pallas import tpu as pltpu
from jax.sharding import PartitionSpec as P

D = 1024
HEADS = 16
HEAD_DIM = 64
LENGTH = 2048
BLK = 256
BF = jnp.bfloat16
F32 = jnp.float32
BIG = 2.0**100
MIB = 2**20
NONE = slice(None)

QKV_SEGS = ((0, 0, 0, 1), (0, 1, 1, 1), (0, 2, 2, 1))
REST_SEGS = (
    (1, 0, 0, 1),
    (2, 0, 0, 2),
    (2, 1, 2, 1),
    (2, 2, 3, 1),
    (3, 0, 0, 1),
    (3, 1, 1, 1),
    (3, 2, 2, 2),
)


def place():
    c = lax.axis_index("ctx")
    f = lax.axis_index("fsdp")
    return f // 4, ((f // 2) % 2) * 2 + c // 4, c % 4, f % 2


def device(x, y, z, core):
    return {"ctx": (y % 2) * 4 + z, "fsdp": x * 4 + (y // 2) * 2 + core}


class Links:
    def __init__(self, send, recv):
        self.send, self.recv, self.used = send, recv, 0
        self.x, self.y, self.z, self.core = place()
        self.yh, self.yl = self.y // 2, self.y % 2
        self.me = self.yl * 4 + self.z

    def peers(self, axis):
        x, y, z, c = self.x, self.y, self.z, self.core
        if axis == "x":
            return [device((x + j) % 4, y, z, c) for j in (1, 2, 3)]
        if axis == "y":
            return [device(x, (y + j) % 4, z, c) for j in (1, 2, 3)]
        if axis == "z":
            return [device(x, y, (z + j) % 4, c) for j in (1, 2, 3)]
        return [device(x, y, z, 1 - c)]

    def rows_peers(self):
        out = []
        for j in range(1, 8):
            t = (self.me + j) % 8
            out.append((t, device(self.x, self.yh * 2 + t // 4, t % 4, self.core)))
        return out

    def barrier(self):
        everyone = self.peers("x") + self.peers("y") + self.peers("z") + self.peers("core")
        for j in (1, 2, 3):
            everyone.append(device(self.x, self.yh * 2 + 1 - self.yl, (self.z + j) % 4, self.core))
        sem = pltpu.get_barrier_semaphore()
        for who in everyone:
            pl.semaphore_signal(sem, inc=1, device_id=who)
        pl.semaphore_wait(sem, len(everyone))

    def to(self, src, dst, who):
        i = self.used
        self.used += 1
        copy = pltpu.make_async_remote_copy(
            src_ref=src,
            dst_ref=dst,
            send_sem=self.send.at[i],
            recv_sem=self.recv.at[i],
            device_id=who,
        )
        copy.start()
        return copy

    def local(self, src, dst):
        i = self.used
        self.used += 1
        copy = pltpu.make_async_copy(src, dst, self.send.at[i])
        copy.start()
        return copy


def wait_recv(copies):
    for copy in copies:
        copy.wait_recv()


def wait_send(copies):
    for copy in copies:
        copy.wait_send()


class Gather:
    def __init__(self, links, full, shard, seg):
        tensor, self.order, first, count = seg
        self.links, self.full, self.shard = links, full, shard
        self.blocked = tensor == 3
        if self.blocked:
            self.units = (pl.ds(first, count),)
            self.all_cols = pl.ds(0, D)
            width = D // 4
            self.z_cols = pl.ds(pl.multiple_of(links.z * width, width), width)
        else:
            self.units = ()
            self.all_cols = pl.ds(first * D, count * D)
            width = count * D // 4
            self.z_cols = pl.ds(pl.multiple_of(first * D + links.z * width, width), width)
        self.sent = []

    def view(self, x, yh, yl, cols):
        return self.full.at[(x, yh, self.links.core) + self.units + (yl, NONE, cols)]

    def own(self, cols):
        return self.shard.at[self.units + (self.links.yl, NONE, cols)]

    def push(self, src, dst, axis):
        now = [self.links.to(src, dst, who) for who in self.links.peers(axis)]
        self.sent += now
        return now

    def stage1(self):
        k = self.links
        cols = self.all_cols if self.order == 0 else self.z_cols
        dst = self.view(k.x, k.yh, k.yl, cols)
        self.kept = k.local(self.own(cols), dst)
        self.first = self.push(self.own(cols), dst, "x" if self.order == 1 else "y")

    def stage2(self):
        k = self.links
        self.kept.wait()
        wait_recv(self.first)
        if self.order == 0:
            part = self.view(k.x, NONE, NONE, self.all_cols)
            self.last = self.push(part, part, "x")
        elif self.order == 1:
            part = self.view(NONE, k.yh, k.yl, self.z_cols)
            self.second = self.push(part, part, "z")
        else:
            part = self.view(k.x, NONE, NONE, self.z_cols)
            self.second = self.push(part, part, "x")

    def stage3(self):
        k = self.links
        if self.order == 0:
            return
        wait_recv(self.second)
        if self.order == 1:
            part = self.view(NONE, k.yh, k.yl, self.all_cols)
            self.last = self.push(part, part, "y")
        else:
            part = self.view(NONE, NONE, NONE, self.z_cols)
            self.last = self.push(part, part, "z")

    def cross(self):
        wait_recv(self.last)
        part = self.view(NONE, NONE, NONE, self.all_cols)
        self.swapped = self.push(part, part, "core")

    def finish(self):
        wait_recv(self.swapped)

    def drain(self):
        wait_send(self.sent)


def small_row(pack, row):
    pieces = []
    for x in range(4):
        for yh in range(2):
            pieces.append(
                pack[x, yh, 0, row : row + 1, :].astype(F32)
                + pack[x, yh, 1, row : row + 1, :].astype(F32)
            )
    return jnp.concatenate(pieces, axis=1)


def dot_nt(a, b):
    return lax.dot_general(a, b, (((1,), (1,)), ((), ())), preferred_element_type=F32)


def dot_tn(a, b):
    return lax.dot_general(a, b, (((0,), (0,)), ((), ())), preferred_element_type=F32)


def dot(a, b):
    return jnp.dot(a, b, preferred_element_type=F32)


def slope_of(links, h, shape):
    power = (links.me * 2 + h + 1).astype(F32) * -0.5
    return jnp.exp2(jnp.full(shape, power, F32)) * (4.0 / LENGTH)


def extend(links, seg_ref, qkv_ref, kx_ref, qx_ref, h, t):
    rows = pl.ds(t * BLK, BLK)
    seg = jnp.broadcast_to(seg_ref[t, 0:1, :].astype(F32), (128, BLK)).T
    lane = lax.broadcasted_iota(jnp.int32, (BLK, 128), 1)
    mine = (lane // 64) == h
    e = lane - 64 * (1 - h)
    where = lax.broadcasted_iota(jnp.int32, (BLK, 128), 0) + t * BLK
    bias = slope_of(links, h, (BLK, 128)) * where.astype(F32)
    high = bias.astype(BF).astype(F32)
    mid = (bias - high).astype(BF).astype(F32)
    low = bias - high - mid
    doc = (e - 3).astype(F32)
    is_doc = (e >= 3) & (e <= 6)
    same = seg == doc
    key_extra = jnp.where(is_doc & jnp.logical_not(same), 1.0, 0.0)
    key_extra = jnp.where(e == 0, high, jnp.where(e == 1, mid, jnp.where(e == 2, low, key_extra)))
    query_extra = jnp.where(is_doc & same, -BIG, 0.0)
    query_extra = jnp.where((e >= 0) & (e <= 2), 1.0, query_extra)
    query = qkv_ref[0, rows, :].astype(F32) * 0.125
    key = qkv_ref[1, rows, :].astype(F32)
    kx_ref[h, rows, :] = jnp.where(mine, key, key_extra).astype(BF)
    qx_ref[h, rows, :] = jnp.where(mine, query, query_extra).astype(BF)


def attend(links, kx_ref, qx_ref, vt_ref, ot_ref, lse_ref, h, i):
    keys = BLK * (i + 1)
    qb = qx_ref[h, BLK * i : keys, :]
    down = lax.broadcasted_iota(jnp.int32, (BLK, BLK), 0)
    across = lax.broadcasted_iota(jnp.int32, (BLK, BLK), 1)
    edge = jnp.where(down <= across, dot_nt(kx_ref[h, BLK * i : keys, :], qb), -BIG)
    top = jnp.max(edge, axis=0, keepdims=True)
    if i:
        past = dot_nt(kx_ref[h, 0 : BLK * i, :], qb)
        top = jnp.maximum(top, jnp.max(past, axis=0, keepdims=True))
    edge = jnp.exp(edge - top)
    total = jnp.sum(edge, axis=0, keepdims=True)
    out = dot(vt_ref[h, :, BLK * i : keys], edge.astype(BF))
    if i:
        past = jnp.exp(past - top)
        total = total + jnp.sum(past, axis=0, keepdims=True)
        out = out + dot(vt_ref[h, :, 0 : BLK * i], past.astype(BF))
    ot_ref[h, :, BLK * i : keys] = out / total
    where = (lax.broadcasted_iota(jnp.int32, (1, BLK), 1) + BLK * i).astype(F32)
    shifted = top + jnp.log(total)
    final = shifted - slope_of(links, h, (1, BLK)) * where
    first = lax.broadcasted_iota(jnp.int32, (8, BLK), 0) == 0
    lse_ref[h, :, BLK * i : keys] = jnp.where(first, final, shifted)


def forward_kernel(
    tokens,
    seg,
    small,
    wq_in,
    wo_in,
    w1_in,
    w2_in,
    wq_out,
    wo,
    w1,
    w2,
    pack_out,
    normed_out,
    qkv_out,
    kx,
    qx,
    ot,
    lse,
    mixed,
    lse_all,
    wq,
    pack,
    seg_all,
    row,
    merged,
    qkv,
    vt,
    mixed_send,
    send,
    recv,
):
    k = Links(send, recv)
    k.barrier()
    sent, kept = [], []

    kept_small = k.local(small, pack.at[k.x, k.yh, k.core])
    small_x = [k.to(small, pack.at[k.x, k.yh, k.core], who) for who in k.peers("x")]
    fulls, shards = (wq, wo, w1, w2), (wq_in, wo_in, w1_in, w2_in)
    first = [Gather(k, fulls[s[0]], shards[s[0]], s) for s in QKV_SEGS]
    rest = [Gather(k, fulls[s[0]], shards[s[0]], s) for s in REST_SEGS]
    for g in first:
        g.stage1()
    kept_seg = k.local(seg, seg_all.at[k.me])
    segs = [k.to(seg, seg_all.at[k.me], who) for _, who in k.rows_peers()]
    for g in first:
        g.stage2()
    kept_small.wait()
    wait_recv(small_x)
    part = pack.at[:, k.yh, k.core]
    small_y = [k.to(part, part, k.peers("y")[1])]
    for g in rest:
        g.stage1()
    for g in first:
        g.stage3()
    wait_recv(small_y)
    part = pack.at[:, :, k.core]
    small_c = [k.to(part, part, k.peers("core")[0])]

    values = tokens[...].astype(F32)
    center = values - jnp.mean(values, axis=1, keepdims=True)
    center = center * lax.rsqrt(jnp.mean(center * center, axis=1, keepdims=True) + 1e-05)
    wait_recv(small_c)
    normed_out[...] = (center * small_row(pack, 0) + small_row(pack, 1)).astype(BF)
    pack_out[...] = pack[...]
    pieces = []
    for f in range(16):
        pieces.append(pack[f // 4, (f // 2) % 2, f % 2, 6:7, :].astype(F32))
    row[...] = jnp.broadcast_to(
        jnp.concatenate(pieces[:8] + [jnp.zeros((1, D), F32)] + pieces[8:], axis=1), (8, 3 * D)
    )
    for g in first:
        g.cross()
    for g in rest:
        g.stage2()
    for g in first:
        g.finish()
    kept.append(k.local(wq, wq_out))

    @pl.loop(0, 12)
    def _(n):
        cols = pl.ds(pl.multiple_of(n * 256, 256), 256)
        weight = wq[:, :, :, :, :, cols].reshape(D, 256)
        block = (dot(normed_out[...], weight) + row[0:1, cols]).astype(BF)
        merged[n // 4, 2 * (n % 4)] = block[:, :128]
        merged[n // 4, 2 * (n % 4) + 1] = block[:, 128:]

    mine = pl.ds(pl.multiple_of(k.me * BLK, BLK), BLK)
    kept_qkv = k.local(merged.at[:, k.me], qkv.at[:, mine])
    moved = [k.to(merged.at[:, t], qkv.at[:, mine], who) for t, who in k.rows_peers()]
    for g in rest:
        g.stage3()
    kept_seg.wait()
    wait_recv(segs)
    kept_qkv.wait()
    wait_recv(moved)
    kept.append(k.local(qkv, qkv_out))

    @pl.loop(0, 8)
    def _(t):
        for h in range(2):
            extend(k, seg_all, qkv, kx, qx, h, t)

    for t in range(8):
        flipped = qkv[2, BLK * t : BLK * (t + 1), :].astype(F32).T.astype(BF)
        for h in range(2):
            vt[h, :, BLK * t : BLK * (t + 1)] = flipped[64 * h : 64 * (h + 1)]

    for i in range(8):

        @pl.loop(0, 2)
        def _(h):
            attend(k, kx, qx, vt, ot, lse, h, i)

        both = jnp.concatenate(
            [ot[0, :, BLK * i : BLK * (i + 1)], ot[1, :, BLK * i : BLK * (i + 1)]], axis=0
        )
        mixed_send[i] = both.T.astype(BF)

    cols = pl.ds(pl.multiple_of(k.me * 128, 128), 128)
    kept.append(k.local(mixed_send.at[k.me], mixed.at[:, cols]))
    back = [k.to(mixed_send.at[t], mixed.at[:, cols], who) for t, who in k.rows_peers()]
    part = pl.ds(pl.multiple_of(k.me * BLK, BLK), BLK)
    kept.append(k.local(lse.at[:, :, part], lse_all.at[k.me]))
    for t, who in k.rows_peers():
        part = pl.ds(pl.multiple_of(t * BLK, BLK), BLK)
        back.append(k.to(lse.at[:, :, part], lse_all.at[k.me], who))
    for g in rest:
        g.cross()
    wait_recv(back)
    for g in rest:
        g.finish()
    for copy in kept:
        copy.wait()
    for g in first + rest:
        g.drain()
    wait_send(small_x + small_y + small_c + segs + moved + back)


def full_shape(cols):
    return (4, 2, 2, 2, 32, cols)


def forward_call(tokens, seg, small, wq, wo, w1, w2):
    hbm = pl.BlockSpec(memory_space=pl.ANY)
    vmem = pl.BlockSpec(memory_space=pltpu.VMEM)
    out = jax.ShapeDtypeStruct
    return pl.pallas_call(
        forward_kernel,
        name="forward",
        out_shape=(
            out(full_shape(3 * D), BF),
            out(full_shape(D), BF),
            out(full_shape(4 * D), BF),
            out((4, 2, 2, 4, 2, 32, D), BF),
            out((4, 2, 2, 16, 128), BF),
            out((BLK, D), BF),
            out((3, LENGTH, 128), BF),
            out((2, LENGTH, 128), BF),
            out((2, LENGTH, 128), BF),
            out((2, 64, LENGTH), F32),
            out((2, 8, LENGTH), F32),
            out((BLK, D), BF),
            out((8, 2, 8, BLK), F32),
        ),
        in_specs=[vmem, vmem, vmem, hbm, hbm, hbm, hbm],
        out_specs=(hbm, hbm, hbm, hbm, vmem, vmem, hbm, vmem, vmem, vmem, vmem, hbm, hbm),
        scratch_shapes=[
            pltpu.VMEM(full_shape(3 * D), BF),
            pltpu.VMEM((4, 2, 2, 16, 128), BF),
            pltpu.VMEM((8, 8, BLK), jnp.int32),
            pltpu.VMEM((8, 3 * D), F32),
            pltpu.VMEM((3, 8, BLK, 128), BF),
            pltpu.VMEM((3, LENGTH, 128), BF),
            pltpu.VMEM((2, 64, LENGTH), BF),
            pltpu.VMEM((8, BLK, 128), BF),
            pltpu.SemaphoreType.DMA((170,)),
            pltpu.SemaphoreType.DMA((170,)),
        ],
        compiler_params=pltpu.CompilerParams(
            collective_id=0, has_side_effects=True, vmem_limit_bytes=50 * MIB
        ),
    )(
        tokens,
        seg,
        small,
        wq.reshape(2, 32, 3 * D),
        wo.reshape(2, 32, D),
        w1.reshape(2, 32, 4 * D),
        w2.reshape(4, 2, 32, D),
    )


def small_pack(ln1_gain, ln1_bias, ln2_gain, ln2_bias, out_bias, fc2_bias, qkv_bias, fc1_bias):
    core = lax.axis_index("fsdp") % 2
    six = jnp.stack([ln1_gain, ln1_bias, ln2_gain, ln2_bias, out_bias, fc2_bias])
    none = jnp.zeros_like(six)
    halves = jnp.where(
        core == 0, jnp.concatenate([six, none], 1), jnp.concatenate([none, six], 1)
    )
    return jnp.concatenate(
        [halves, qkv_bias[None], fc1_bias.reshape(2, 128), jnp.zeros((7, 128), BF)], 0
    )


def unpack_row(pack, row):
    return (pack[:, :, 0, row] + pack[:, :, 1, row]).reshape(D)


REST_UNITS = (
    (3, 0, 0),
    (3, 1, 1),
    (3, 2, 2),
    (3, 3, 2),
    (2, 0, 0),
    (2, 1, 0),
    (2, 2, 1),
    (2, 3, 2),
    (1, 0, 0),
)
QKV_UNITS = ((0, 0, 0), (0, 1, 1), (0, 2, 2))
UNITS = REST_UNITS + QKV_UNITS
R1 = ((3, 2, 2, 32, D), (3, 4, 32, D), (3, 4, 2, 2, 32, 256))
R2 = ((3, 32, D), (3, 4, 32, 256), (3, 2, 2, 32, 256))


def count_of(order):
    return sum(1 for unit in UNITS if unit[2] == order)


class Reduce:
    def __init__(self, links, unit, n, grads, half, slots):
        self.tensor, self.unit, self.order = unit
        self.links, self.grad = links, grads[self.tensor]
        self.half = half.at[n]
        at = sum(1 for other in UNITS[:n] if other[2] == self.order)
        self.r1 = slots[self.order].at[at]
        self.r2 = slots[3 + self.order].at[at]
        self.r3 = slots[6].at[n]
        self.z_cols = self.cols_of(links.z)
        self.sent = []

    def cols_of(self, z):
        return pl.ds(pl.multiple_of(z * 256, 256), 256)

    def of_core(self, core):
        if self.tensor == 3:
            return self.grad.at[:, :, core, self.unit]
        return self.grad.at[:, :, core, :, :, pl.ds(self.unit * D, D)]

    def stage0(self):
        k = self.links
        self.swap = k.to(self.of_core(1 - k.core), self.half, k.peers("core")[0])
        self.sent.append(self.swap)

    def push(self, axis, src_of, slot):
        k = self.links
        here = {"x": k.x, "y": k.y, "z": k.z}[axis]
        self.coming = []
        for j, who in enumerate(k.peers(axis)):
            copy = k.to(src_of((here + j + 1) % 4), slot.at[j], who)
            self.coming.append(copy)
        self.sent += self.coming

    def add0(self, own):
        self.swap.wait_recv()

        @pl.loop(0, 16)
        def _(i):
            x, yh, yl = i // 4, (i // 2) % 2, i % 2
            total = self.half[x, yh, yl].astype(F32) + own(x, yh, yl).astype(F32)
            self.half[x, yh, yl] = total.astype(BF)

    def stage1(self):
        half = self.half
        if self.order == 0:
            self.push("x", lambda x: half.at[x], self.r1)
        elif self.order == 1:
            self.push("y", lambda y: half.at[:, y // 2, y % 2], self.r1)
        else:
            self.push("z", lambda z: half.at[:, :, :, :, self.cols_of(z)], self.r1)

    def sum1(self):
        k, half, got = self.links, self.half, self.r1
        wait_recv(self.coming)

        @pl.loop(0, 16 if self.order == 2 else 4)
        def _(i):
            if self.order == 0:
                spot, index = (k.x, i // 2, i % 2), (i // 2, i % 2)
            elif self.order == 1:
                spot, index = (i, k.yh, k.yl), (i,)
            else:
                index = (i // 4, (i // 2) % 2, i % 2)
                spot = index + (NONE, self.z_cols)
            total = half[spot].astype(F32)
            for j in range(3):
                total = total + got[(j,) + index].astype(F32)
            half[spot] = total.astype(BF)

    def stage2(self):
        k, half = self.links, self.half
        if self.order == 0:
            self.push("y", lambda y: half.at[k.x, y // 2, y % 2], self.r2)
        elif self.order == 1:
            self.push("z", lambda z: half.at[:, k.yh, k.yl, :, self.cols_of(z)], self.r2)
        else:
            self.push("x", lambda x: half.at[x, :, :, :, self.z_cols], self.r2)

    def sum2(self):
        k, half, got = self.links, self.half, self.r2
        wait_recv(self.coming)
        if self.order == 0:
            spot = (k.x, k.yh, k.yl)
            total = half[spot].astype(F32)
            for j in range(3):
                total = total + got[j].astype(F32)
            half[spot] = total.astype(BF)
            return

        @pl.loop(0, 4)
        def _(i):
            if self.order == 1:
                spot, index = (i, k.yh, k.yl, NONE, self.z_cols), (i,)
            else:
                spot, index = (k.x, i // 2, i % 2, NONE, self.z_cols), (i // 2, i % 2)
            total = half[spot].astype(F32)
            for j in range(3):
                total = total + got[(j,) + index].astype(F32)
            half[spot] = total.astype(BF)

    def stage3(self):
        k, half = self.links, self.half
        if self.order == 0:
            self.push("z", lambda z: half.at[k.x, k.yh, k.yl, :, self.cols_of(z)], self.r3)
        elif self.order == 1:
            self.push("x", lambda x: half.at[x, k.yh, k.yl, :, self.z_cols], self.r3)
        else:
            self.push("y", lambda y: half.at[k.x, y // 2, y % 2, :, self.z_cols], self.r3)

    def sum3(self, out_ref, position):
        k = self.links
        wait_recv(self.coming)
        total = self.half[k.x, k.yh, k.yl, :, self.z_cols].astype(F32)
        for j in range(3):
            total = total + self.r3[j].astype(F32)
        out_ref[k.me, :, 256 * position : 256 * (position + 1)] = total.astype(BF)

    def drain(self):
        wait_send(self.sent)

    def write(self, got, position, outs):
        out = outs[self.tensor]
        for t in range(8):
            piece = got[t, :, 256 * position : 256 * (position + 1)].astype(F32)
            if self.tensor == 3:
                out[self.unit, t // 4, :, 256 * (t % 4) : 256 * (t % 4 + 1)] = piece
            else:
                first = self.unit * D + 256 * (t % 4)
                out[t // 4, :, first : first + 256] = piece


def attend_back(kx, qx, vx, kt, do, delta, lse, dqt, h, j):
    keys = slice(BLK * j, BLK * (j + 1))
    down = lax.broadcasted_iota(jnp.int32, (BLK, BLK), 0)
    across = lax.broadcasted_iota(jnp.int32, (BLK, BLK), 1)
    grad_key = grad_value = None
    cuts = [BLK * j, BLK * (j + 1)] + list(range(BLK * (j + 1) + 768, LENGTH, 768))
    if cuts[-1] < LENGTH:
        cuts.append(LENGTH)
    for n in range(len(cuts) - 1):
        rows = slice(cuts[n], cuts[n + 1])
        queries = qx[h, rows, :]
        scores = dot_nt(kx[h, keys, :], queries)
        if n == 0:
            scores = jnp.where(down <= across, scores, -BIG)
        probs = jnp.exp(scores - lse[h, 1:2, rows])
        grad_out = do[rows, :]
        grad_probs = dot_nt(vx[h, keys, :], grad_out)
        grad_scores = (probs * (grad_probs - delta[h, 0:1, rows])).astype(BF)
        value_part = dot(probs.astype(BF), grad_out)
        key_part = dot(grad_scores, queries)
        grad_value = value_part if n == 0 else grad_value + value_part
        grad_key = key_part if n == 0 else grad_key + key_part
        query_part = dot(kt[h, :, keys], grad_scores)
        if j == 0:
            dqt[h, :, rows] = query_part
        else:
            dqt[h, :, rows] += query_part
    return grad_key, grad_value


def backward_kernel(
    g_out,
    g_fc1,
    g_fc2,
    grad_mixed,
    qkv,
    kx,
    qx,
    ot,
    lse,
    normed,
    wq_in,
    pack,
    tokens,
    grad_middle,
    small_in,
    o_qkv,
    o_out,
    o_fc1,
    o_fc2,
    o_small,
    input_grad,
    half,
    r1x,
    r1y,
    r1z,
    r2x,
    r2y,
    r2z,
    r3,
    own,
    g_qkv,
    w_slot,
    vx,
    kt,
    do,
    delta,
    dqt,
    g_send,
    g_merged,
    normed_t,
    f_rest,
    f_qkv,
    small,
    small_core,
    small_x,
    small_y,
    small_z,
    gn,
    send,
    recv,
):
    k = Links(send, recv)
    k.barrier()
    grads = (g_qkv, g_out, g_fc1, g_fc2)
    slots = (r1x, r1y, r1z, r2x, r2y, r2z, r3)
    units = [Reduce(k, unit, n, grads, half, slots) for n, unit in enumerate(UNITS)]
    rest, last = units[:9], units[9:]
    for u in rest:
        u.stage0()
    mine = pl.ds(pl.multiple_of(k.me * BLK, BLK), BLK)

    def heads_of(t):
        return pl.ds(pl.multiple_of(t * 128, 128), 128)

    kept_do = k.local(grad_mixed.at[:, heads_of(k.me)], do.at[mine])
    moved = [
        k.to(grad_mixed.at[:, heads_of(t)], do.at[mine], who) for t, who in k.rows_peers()
    ]
    loads = [k.local(u.of_core(k.core), own.at[n]) for n, u in enumerate(rest[:2])]

    lane = lax.broadcasted_iota(jnp.int32, (BLK, 128), 1)
    for t in range(8):
        rows = slice(BLK * t, BLK * (t + 1))
        value = qkv[2, rows, :]
        flipped = qkv[1, rows, :].astype(F32).T.astype(BF)
        for h in range(2):
            vx[h, rows, :] = jnp.where((lane // 64) == h, value.astype(F32), 0.0).astype(BF)
            kt[h, :, rows] = flipped[64 * h : 64 * (h + 1)]
    normed_t[...] = normed[...].astype(F32).T.astype(BF)
    kept_do.wait()
    wait_recv(moved)
    for t in range(8):
        rows = slice(BLK * t, BLK * (t + 1))
        flipped = do[rows, :].astype(F32).T
        for h in range(2):
            product = flipped[64 * h : 64 * (h + 1)] * ot[h, :, rows]
            delta[h, :, rows] = jnp.broadcast_to(
                jnp.sum(product, axis=0, keepdims=True), (8, BLK)
            )
    for n, u in enumerate(rest):
        loads[n].wait()
        u.add0(lambda x, yh, yl, n=n: own[n % 2, x, yh, yl])
        u.stage1()
        if n + 2 < len(rest):
            loads.append(k.local(rest[n + 2].of_core(k.core), own.at[n % 2]))

    back = []
    for t, who in k.rows_peers():
        i = k.used
        k.used += 1
        copy = pltpu.make_async_remote_copy(
            src_ref=g_send.at[:, t],
            dst_ref=g_merged.at[:, :, heads_of(k.me)],
            send_sem=k.send.at[i],
            recv_sem=k.recv.at[i],
            device_id=who,
        )
        back.append((t, copy))
    for j in range(8):
        found = [attend_back(kx, qx, vx, kt, do, delta, lse, dqt, h, j) for h in range(2)]
        left = (lane // 64) == 0
        for s, position in ((1, 0), (2, 1)):
            both = jnp.where(left, found[0][position], found[1][position])
            g_send[s, j] = both.astype(BF)
        rows = slice(BLK * j, BLK * (j + 1))
        query = jnp.concatenate([dqt[0, :, rows], dqt[1, :, rows]], axis=0).T * 0.125
        g_send[0, j] = query.astype(BF)
        if j in (3, 7):
            for t, copy in back:
                pl.when((t // 4) == (j // 4))(copy.start)
    kept_g = k.local(g_send.at[:, k.me], g_merged.at[:, :, heads_of(k.me)])

    def w_load(s):
        cols = pl.ds(s * D, D)
        return k.local(wq_in.at[:, :, :, :, :, cols], w_slot.at[s % 2])

    w_loads = [w_load(0), w_load(1)]
    for u in rest:
        u.sum1()
        u.stage2()
    kept_g.wait()
    for _, copy in back:
        copy.wait_recv()

    for s in range(3):

        @pl.loop(0, 4)
        def _(n):
            cols = pl.ds(pl.multiple_of(n * 256, 256), 256)
            block = dot(normed_t[...], g_merged[s, :, cols]).astype(BF)
            there = pl.ds(pl.multiple_of(s * D + n * 256, 256), 256)
            g_qkv[:, :, :, :, :, there] = block.reshape(4, 2, 2, 2, 32, 256)

        last[s].stage0()
    for u in rest:
        u.sum2()
        u.stage3()

    for s in range(3):
        w_loads[s].wait()
        for n in range(4):
            weight = w_slot[s % 2, n].reshape(256, D)
            part = dot_nt(g_merged[s], weight)
            cols = slice(256 * n, 256 * (n + 1))
            if s == 0:
                gn[:, cols] = part
            else:
                gn[:, cols] += part
        if s == 0:
            w_loads.append(w_load(2))
    for s, u in enumerate(last):
        cols = pl.ds(s * D, D)
        u.add0(lambda x, yh, yl, cols=cols: g_qkv[x, yh, k.core, yl, :, cols])
        u.stage1()

    values = tokens[...].astype(F32)
    center = values - jnp.mean(values, axis=1, keepdims=True)
    scale = lax.rsqrt(jnp.mean(center * center, axis=1, keepdims=True) + 1e-05)
    center = center * scale
    grad_normed = gn[...]
    by_gain = jnp.sum(grad_normed * center, axis=0, keepdims=True)
    by_bias = jnp.sum(grad_normed, axis=0, keepdims=True)
    inner = grad_normed * small_row(pack, 0)
    part = inner - jnp.mean(inner, axis=1, keepdims=True)
    part = part - center * jnp.mean(inner * center, axis=1, keepdims=True)
    input_grad[...] = grad_middle[...] + part * scale
    by_query = jnp.sum(g_merged[0].astype(F32), axis=0, keepdims=True)
    by_value = jnp.sum(g_merged[2].astype(F32), axis=0, keepdims=True)
    small[...] = small_in[...]
    for x in range(4):
        for yh in range(2):
            n = 2 * x + yh
            cols = slice(128 * n, 128 * (n + 1))
            small[x, yh, 0:1, :] = by_gain[:, cols]
            small[x, yh, 1:2, :] = by_bias[:, cols]
            source = by_query if x < 2 else by_value
            first = 256 * (n % 4)
            small[x, yh, 6:7, :] = source[:, first : first + 128]
            small[x, yh, 7:8, :] = source[:, first + 128 : first + 256]
    small_sent = [k.to(small, small_core, k.peers("core")[0])]

    for n, u in enumerate(rest):
        u.sum3(f_rest, n)
    gathered = [k.to(f_rest.at[k.me], f_rest.at[k.me], who) for _, who in k.rows_peers()]

    small_sent[0].wait()
    small[...] = small[...] + small_core[...]
    coming = [
        k.to(small.at[(k.x + j + 1) % 4], small_x.at[j], who)
        for j, who in enumerate(k.peers("x"))
    ]
    small_sent += coming
    for u in last:
        u.sum1()
        u.stage2()
    wait_recv(coming)
    small[k.x] = small[k.x] + small_x[0] + small_x[1] + small_x[2]
    coming = [
        k.to(small.at[k.x, ((k.y + j + 1) % 4) // 2], small_y.at[j], who)
        for j, who in enumerate(k.peers("y"))
    ]
    small_sent += coming
    for u in last:
        u.sum2()
        u.stage3()
    wait_recv(coming)
    small_z[3] = small[k.x, k.yh] + small_y[0] + small_y[1] + small_y[2]
    coming = [k.to(small_z.at[3], small_z.at[j], who) for j, who in enumerate(k.peers("z"))]
    small_sent += coming
    for n, u in enumerate(last):
        u.sum3(f_qkv, n)
    gathered_qkv = [k.to(f_qkv.at[k.me], f_qkv.at[k.me], who) for _, who in k.rows_peers()]
    outs = (o_qkv, o_out, o_fc1, o_fc2)
    wait_recv(gathered)
    for n, u in enumerate(rest):
        u.write(f_rest, n, outs)
    wait_recv(coming)
    o_small[...] = small_z[0] + small_z[1] + small_z[2] + small_z[3]
    wait_recv(gathered_qkv)
    for n, u in enumerate(last):
        u.write(f_qkv, n, outs)
    for u in units:
        u.drain()
    wait_send(moved + [copy for _, copy in back] + small_sent[1:] + gathered + gathered_qkv)


def backward_call(
    g_out, g_fc1, g_fc2, grad_mixed, qkv, kx, qx, ot, lse, normed, wq, pack, tokens, grad_middle, small
):
    hbm = pl.BlockSpec(memory_space=pl.ANY)
    vmem = pl.BlockSpec(memory_space=pltpu.VMEM)
    out = jax.ShapeDtypeStruct
    mem = pltpu.VMEM
    return pl.pallas_call(
        backward_kernel,
        name="backward",
        out_shape=(
            out((2, 32, 3 * D), F32),
            out((2, 32, D), F32),
            out((2, 32, 4 * D), F32),
            out((4, 2, 32, D), F32),
            out((16, 128), F32),
            out((BLK, D), F32),
        ),
        in_specs=[hbm, hbm, hbm, hbm, vmem, vmem, vmem, vmem, vmem, vmem, hbm, vmem, vmem, vmem, vmem],
        out_specs=(vmem,) * 6,
        scratch_shapes=[
            mem((12, 4, 2, 2, 32, D), BF),
            *[mem((count_of(order),) + R1[order], BF) for order in range(3)],
            *[mem((count_of(order),) + R2[order], BF) for order in range(3)],
            mem((12, 3, 32, 256), BF),
            mem((2, 4, 2, 2, 32, D), BF),
            mem(full_shape(3 * D), BF),
            mem((2,) + full_shape(D), BF),
            mem((2, LENGTH, 128), BF),
            mem((2, 64, LENGTH), BF),
            mem((LENGTH, 128), BF),
            mem((2, 8, LENGTH), F32),
            mem((2, 64, LENGTH), F32),
            mem((3, 8, BLK, 128), BF),
            mem((3, BLK, D), BF),
            mem((D, BLK), BF),
            mem((8, 32, 9 * 256), BF),
            mem((8, 32, 3 * 256), BF),
            mem((4, 2, 16, 128), F32),
            mem((4, 2, 16, 128), F32),
            mem((3, 2, 16, 128), F32),
            mem((3, 16, 128), F32),
            mem((4, 16, 128), F32),
            mem((BLK, D), F32),
            pltpu.SemaphoreType.DMA((190,)),
            pltpu.SemaphoreType.DMA((190,)),
        ],
        compiler_params=pltpu.CompilerParams(
            collective_id=1, has_side_effects=True, vmem_limit_bytes=63 * MIB
        ),
    )(
        g_out.reshape(full_shape(D)),
        g_fc1.reshape(full_shape(4 * D)),
        g_fc2.reshape(4, 2, 2, 4, 2, 32, D),
        grad_mixed,
        qkv,
        kx,
        qx,
        ot,
        lse,
        normed,
        wq,
        pack,
        tokens,
        grad_middle,
        small,
    )


def layer_norm(values, gain_vec, bias_vec):
    center = values - jnp.mean(values, axis=-1, keepdims=True)
    spread = jnp.mean(center * center, axis=-1, keepdims=True)
    return center * lax.rsqrt(spread + 1e-05) * gain_vec + bias_vec


def gelu_tanh(values):
    return jax.nn.gelu(values, approximate=True)


def matmul_tn(left, right):
    return lax.dot_general(
        left, right, (((0,), (0,)), ((), ())), preferred_element_type=jnp.float32
    )


def matmul_nt(left, right):
    return lax.dot_general(
        left, right, (((1,), (1,)), ((), ())), preferred_element_type=jnp.float32
    )


def matmul(left, right):
    return jnp.dot(left, right, preferred_element_type=jnp.float32)


def local(
    tokens,
    segment_ids,
    cotangent,
    ln1_gain,
    ln1_bias,
    qkv_weight,
    qkv_bias,
    out_weight,
    out_bias,
    ln2_gain,
    ln2_bias,
    fc1_weight,
    fc1_bias,
    fc2_weight,
    fc2_bias,
):
    block_len = tokens.shape[1]
    small = small_pack(
        ln1_gain, ln1_bias, ln2_gain, ln2_bias, out_bias, fc2_bias, qkv_bias, fc1_bias
    )
    flat = tokens.reshape(block_len, D)
    (wq, wo, w1, w2, pack, normed, qkv, kx, qx, ot, lse, mixed, lse_all) = forward_call(
        flat,
        jnp.broadcast_to(segment_ids, (8, block_len)),
        small,
        qkv_weight,
        out_weight,
        fc1_weight,
        fc2_weight,
    )
    out_mat = wo.reshape(D, D)
    up_mat = w1.reshape(D, 4 * D)
    down_mat = w2.reshape(4 * D, D)
    gain_two = unpack_row(pack, 2).astype(jnp.float32)
    bias_two = unpack_row(pack, 3).astype(jnp.float32)
    out_vec = unpack_row(pack, 4).astype(jnp.float32)
    down_vec = unpack_row(pack, 5).astype(jnp.float32)
    up_vec = pack[:, :, :, 7:9].reshape(4 * D).astype(jnp.float32)
    log_sums = lse_all[:, :, 0].reshape(1, HEADS, block_len)

    middle = flat.astype(jnp.float32) + matmul(mixed, out_mat) + out_vec
    normed_two = layer_norm(middle, gain_two, bias_two).astype(jnp.bfloat16)
    hidden = matmul(normed_two, up_mat) + up_vec
    active = gelu_tanh(hidden).astype(jnp.bfloat16)
    output = middle + matmul(active, down_mat) + down_vec

    grad_down = cotangent.reshape(block_len, D)
    grad_output = grad_down.astype(jnp.float32)
    g_fc2 = matmul_tn(active, grad_down).astype(jnp.bfloat16)
    fc2_bias_grad = jnp.sum(grad_output, axis=0)
    grad_active = matmul_nt(grad_down, down_mat)
    _, gelu_pull = jax.vjp(gelu_tanh, hidden)
    grad_hidden = gelu_pull(grad_active)[0].astype(jnp.bfloat16)
    g_fc1 = matmul_tn(normed_two, grad_hidden).astype(jnp.bfloat16)
    fc1_bias_grad = jnp.sum(grad_hidden.astype(jnp.float32), axis=0)
    grad_normed_two = matmul_nt(grad_hidden, up_mat)
    _, norm_pull = jax.vjp(layer_norm, middle, gain_two, bias_two)
    part, ln2_gain_grad, ln2_bias_grad = norm_pull(grad_normed_two)
    grad_middle = grad_output + part
    grad_branch = grad_middle.astype(jnp.bfloat16)
    g_out = matmul_tn(mixed, grad_branch).astype(jnp.bfloat16)
    out_bias_grad = jnp.sum(grad_branch.astype(jnp.float32), axis=0)
    grad_mixed = matmul_nt(grad_branch, out_mat).astype(jnp.bfloat16)

    four = jnp.stack([ln2_gain_grad, ln2_bias_grad, out_bias_grad, fc2_bias_grad])
    four = four.reshape(4, 4, 2, 128).transpose(1, 2, 0, 3)
    none = jnp.zeros((4, 2, 2, 128), jnp.float32)
    small_grads = jnp.concatenate(
        [none, four, none, fc1_bias_grad.reshape(4, 2, 4, 128), none, none], axis=2
    )
    g_qkv, g_wo, g_up, g_down, small_sums, input_grad = backward_call(
        g_out,
        g_fc1,
        g_fc2,
        grad_mixed,
        qkv,
        kx,
        qx,
        ot,
        lse,
        normed,
        wq,
        pack,
        flat,
        grad_middle,
        small_grads,
    )
    core = lax.axis_index("fsdp") % 2
    halves = lax.dynamic_slice_in_dim(small_sums[:6], core * 64, 64, 1)
    g_qkvb = lax.dynamic_slice_in_dim(small_sums, 6 + core, 1, 0).reshape(128)
    g_upb = lax.dynamic_slice_in_dim(small_sums, 8 + 2 * core, 2, 0).reshape(256)
    return (
        output.astype(jnp.bfloat16).reshape(1, block_len, D),
        input_grad.reshape(1, block_len, D),
        halves[0],
        halves[1],
        g_qkv.reshape(64, 3 * D),
        g_qkvb,
        g_wo.reshape(64, D),
        halves[4],
        halves[2],
        halves[3],
        g_up.reshape(64, 4 * D),
        g_upb,
        g_down.reshape(256, D),
        halves[5],
        log_sums,
    )


def solution(mesh):
    placed = (
        P("fsdp", "ctx", None),
        P("fsdp", "ctx"),
        P("fsdp", "ctx", None),
        P("fsdp"),
        P("fsdp"),
        P("fsdp", None),
        P("fsdp"),
        P("fsdp", None),
        P("fsdp"),
        P("fsdp"),
        P("fsdp"),
        P("fsdp", None),
        P("fsdp"),
        P("fsdp", None),
        P("fsdp"),
    )
    return jax.shard_map(
        local,
        mesh=mesh,
        in_specs=placed,
        out_specs=(
            P("fsdp", "ctx", None),
            P("fsdp", "ctx", None),
            P("fsdp"),
            P("fsdp"),
            P("fsdp", None),
            P("fsdp"),
            P("fsdp", None),
            P("fsdp"),
            P("fsdp"),
            P("fsdp"),
            P("fsdp", None),
            P("fsdp"),
            P("fsdp", None),
            P("fsdp"),
            P("fsdp", None, "ctx"),
        ),
        check_vma=False,
    )
```

```python
import functools

import jax
import jax.numpy as jnp
from jax import lax
from jax.experimental import pallas as pl
from jax.experimental.pallas import tpu as pltpu
from jax.sharding import PartitionSpec as P

D = 1024
HEADS = 16
HEAD_DIM = 64
LENGTH = 2048
BLK = 256
BF = jnp.bfloat16
F32 = jnp.float32
BIG = 2.0**100
MIB = 2**20
NONE = slice(None)

QKV_SEGS = ((0, 0, 0, 1), (0, 1, 1, 1), (0, 2, 2, 1))
REST_SEGS = (
    (1, 0, 0, 1),
    (2, 0, 0, 2),
    (2, 1, 2, 1),
    (2, 2, 3, 1),
    (3, 0, 0, 1),
    (3, 1, 1, 1),
    (3, 2, 2, 2),
)


def place():
    c = lax.axis_index("ctx")
    f = lax.axis_index("fsdp")
    return f // 4, ((f // 2) % 2) * 2 + c // 4, c % 4, f % 2


def device(x, y, z, core):
    return {"ctx": (y % 2) * 4 + z, "fsdp": x * 4 + (y // 2) * 2 + core}


class Links:
    def __init__(self, send, recv):
        self.send, self.recv, self.used = send, recv, 0
        self.x, self.y, self.z, self.core = place()
        self.yh, self.yl = self.y // 2, self.y % 2
        self.me = self.yl * 4 + self.z

    def peers(self, axis):
        x, y, z, c = self.x, self.y, self.z, self.core
        if axis == "x":
            return [device((x + j) % 4, y, z, c) for j in (1, 2, 3)]
        if axis == "y":
            return [device(x, (y + j) % 4, z, c) for j in (1, 2, 3)]
        if axis == "z":
            return [device(x, y, (z + j) % 4, c) for j in (1, 2, 3)]
        return [device(x, y, z, 1 - c)]

    def rows_peers(self):
        out = []
        for j in range(1, 8):
            t = (self.me + j) % 8
            out.append((t, device(self.x, self.yh * 2 + t // 4, t % 4, self.core)))
        return out

    def barrier(self):
        everyone = self.peers("x") + self.peers("y") + self.peers("z") + self.peers("core")
        for j in (1, 2, 3):
            everyone.append(device(self.x, self.yh * 2 + 1 - self.yl, (self.z + j) % 4, self.core))
        sem = pltpu.get_barrier_semaphore()
        for who in everyone:
            pl.semaphore_signal(sem, inc=1, device_id=who)
        pl.semaphore_wait(sem, len(everyone))

    def to(self, src, dst, who):
        i = self.used
        self.used += 1
        copy = pltpu.make_async_remote_copy(
            src_ref=src,
            dst_ref=dst,
            send_sem=self.send.at[i],
            recv_sem=self.recv.at[i],
            device_id=who,
        )
        copy.start()
        return copy

    def local(self, src, dst):
        i = self.used
        self.used += 1
        copy = pltpu.make_async_copy(src, dst, self.send.at[i])
        copy.start()
        return copy


def wait_recv(copies):
    for copy in copies:
        copy.wait_recv()


def wait_send(copies):
    for copy in copies:
        copy.wait_send()


class Gather:
    def __init__(self, links, full, shard, seg):
        tensor, self.order, first, count = seg
        self.links, self.full, self.shard = links, full, shard
        self.blocked = tensor == 3
        if self.blocked:
            self.units = (pl.ds(first, count),)
            self.all_cols = pl.ds(0, D)
            width = D // 4
            self.z_cols = pl.ds(pl.multiple_of(links.z * width, width), width)
        else:
            self.units = ()
            self.all_cols = pl.ds(first * D, count * D)
            width = count * D // 4
            self.z_cols = pl.ds(pl.multiple_of(first * D + links.z * width, width), width)
        self.sent = []

    def view(self, x, yh, yl, cols):
        return self.full.at[(x, yh, self.links.core) + self.units + (yl, NONE, cols)]

    def own(self, cols):
        return self.shard.at[self.units + (self.links.yl, NONE, cols)]

    def push(self, src, dst, axis):
        now = [self.links.to(src, dst, who) for who in self.links.peers(axis)]
        self.sent += now
        return now

    def stage1(self):
        k = self.links
        cols = self.all_cols if self.order == 0 else self.z_cols
        dst = self.view(k.x, k.yh, k.yl, cols)
        self.kept = k.local(self.own(cols), dst)
        self.first = self.push(self.own(cols), dst, "x" if self.order == 1 else "y")

    def stage2(self):
        k = self.links
        self.kept.wait()
        wait_recv(self.first)
        if self.order == 0:
            part = self.view(k.x, NONE, NONE, self.all_cols)
            self.last = self.push(part, part, "x")
        elif self.order == 1:
            part = self.view(NONE, k.yh, k.yl, self.z_cols)
            self.second = self.push(part, part, "z")
        else:
            part = self.view(k.x, NONE, NONE, self.z_cols)
            self.second = self.push(part, part, "x")

    def stage3(self):
        k = self.links
        if self.order == 0:
            return
        wait_recv(self.second)
        if self.order == 1:
            part = self.view(NONE, k.yh, k.yl, self.all_cols)
            self.last = self.push(part, part, "y")
        else:
            part = self.view(NONE, NONE, NONE, self.z_cols)
            self.last = self.push(part, part, "z")

    def cross(self):
        wait_recv(self.last)
        part = self.view(NONE, NONE, NONE, self.all_cols)
        self.swapped = self.push(part, part, "core")

    def finish(self):
        wait_recv(self.swapped)

    def drain(self):
        wait_send(self.sent)


def small_row(pack, row):
    pieces = []
    for x in range(4):
        for yh in range(2):
            pieces.append(
                pack[x, yh, 0, row : row + 1, :].astype(F32)
                + pack[x, yh, 1, row : row + 1, :].astype(F32)
            )
    return jnp.concatenate(pieces, axis=1)


def dot_nt(a, b):
    return lax.dot_general(a, b, (((1,), (1,)), ((), ())), preferred_element_type=F32)


def dot_tn(a, b):
    return lax.dot_general(a, b, (((0,), (0,)), ((), ())), preferred_element_type=F32)


def dot(a, b):
    return jnp.dot(a, b, preferred_element_type=F32)


def slope_of(links, h, shape):
    power = (links.me * 2 + h + 1).astype(F32) * -0.5
    return jnp.exp2(jnp.full(shape, power, F32)) * (4.0 / LENGTH)


def extend(links, seg_ref, qkv_ref, kx_ref, qx_ref, h, t):
    rows = pl.ds(t * BLK, BLK)
    seg = jnp.broadcast_to(seg_ref[t, 0:1, :].astype(F32), (128, BLK)).T
    lane = lax.broadcasted_iota(jnp.int32, (BLK, 128), 1)
    mine = (lane // 64) == h
    e = lane - 64 * (1 - h)
    where = lax.broadcasted_iota(jnp.int32, (BLK, 128), 0) + t * BLK
    bias = slope_of(links, h, (BLK, 128)) * where.astype(F32)
    high = bias.astype(BF).astype(F32)
    mid = (bias - high).astype(BF).astype(F32)
    low = bias - high - mid
    doc = (e - 3).astype(F32)
    is_doc = (e >= 3) & (e <= 6)
    same = seg == doc
    key_extra = jnp.where(is_doc & jnp.logical_not(same), 1.0, 0.0)
    key_extra = jnp.where(e == 0, high, jnp.where(e == 1, mid, jnp.where(e == 2, low, key_extra)))
    query_extra = jnp.where(is_doc & same, -BIG, 0.0)
    query_extra = jnp.where((e >= 0) & (e <= 2), 1.0, query_extra)
    query = qkv_ref[0, rows, :].astype(F32) * 0.125
    key = qkv_ref[1, rows, :].astype(F32)
    kx_ref[h, rows, :] = jnp.where(mine, key, key_extra).astype(BF)
    qx_ref[h, rows, :] = jnp.where(mine, query, query_extra).astype(BF)


def attend(links, kx_ref, qx_ref, vt_ref, ot_ref, lse_ref, h, i):
    keys = BLK * (i + 1)
    qb = qx_ref[h, BLK * i : keys, :]
    down = lax.broadcasted_iota(jnp.int32, (BLK, BLK), 0)
    across = lax.broadcasted_iota(jnp.int32, (BLK, BLK), 1)
    edge = jnp.where(down <= across, dot_nt(kx_ref[h, BLK * i : keys, :], qb), -BIG)
    top = jnp.max(edge, axis=0, keepdims=True)
    if i:
        past = dot_nt(kx_ref[h, 0 : BLK * i, :], qb)
        top = jnp.maximum(top, jnp.max(past, axis=0, keepdims=True))
    edge = jnp.exp(edge - top)
    total = jnp.sum(edge, axis=0, keepdims=True)
    out = dot(vt_ref[h, :, BLK * i : keys], edge.astype(BF))
    if i:
        past = jnp.exp(past - top)
        total = total + jnp.sum(past, axis=0, keepdims=True)
        out = out + dot(vt_ref[h, :, 0 : BLK * i], past.astype(BF))
    ot_ref[h, :, BLK * i : keys] = out / total
    where = (lax.broadcasted_iota(jnp.int32, (1, BLK), 1) + BLK * i).astype(F32)
    shifted = top + jnp.log(total)
    final = shifted - slope_of(links, h, (1, BLK)) * where
    first = lax.broadcasted_iota(jnp.int32, (8, BLK), 0) == 0
    lse_ref[h, :, BLK * i : keys] = jnp.where(first, final, shifted)


def forward_kernel(
    tokens,
    seg,
    small,
    wq_in,
    wo_in,
    w1_in,
    w2_in,
    wq_out,
    wo,
    w1,
    w2,
    pack_out,
    normed_out,
    qkv_out,
    kx,
    qx,
    ot,
    lse,
    mixed,
    lse_all,
    wq,
    pack,
    seg_all,
    row,
    merged,
    qkv,
    vt,
    mixed_send,
    send,
    recv,
):
    k = Links(send, recv)
    k.barrier()
    sent, kept = [], []

    kept_small = k.local(small, pack.at[k.x, k.yh, k.core])
    small_x = [k.to(small, pack.at[k.x, k.yh, k.core], who) for who in k.peers("x")]
    fulls, shards = (wq, wo, w1, w2), (wq_in, wo_in, w1_in, w2_in)
    first = [Gather(k, fulls[s[0]], shards[s[0]], s) for s in QKV_SEGS]
    rest = [Gather(k, fulls[s[0]], shards[s[0]], s) for s in REST_SEGS]
    for g in first:
        g.stage1()
    kept_seg = k.local(seg, seg_all.at[k.me])
    segs = [k.to(seg, seg_all.at[k.me], who) for _, who in k.rows_peers()]
    for g in first:
        g.stage2()
    kept_small.wait()
    wait_recv(small_x)
    part = pack.at[:, k.yh, k.core]
    small_y = [k.to(part, part, k.peers("y")[1])]
    for g in rest:
        g.stage1()
    for g in first:
        g.stage3()
    wait_recv(small_y)
    part = pack.at[:, :, k.core]
    small_c = [k.to(part, part, k.peers("core")[0])]

    for g in rest:
        g.stage2()
    values = tokens[...].astype(F32)
    center = values - jnp.mean(values, axis=1, keepdims=True)
    center = center * lax.rsqrt(jnp.mean(center * center, axis=1, keepdims=True) + 1e-05)
    wait_recv(small_c)
    normed_out[...] = (center * small_row(pack, 0) + small_row(pack, 1)).astype(BF)
    pack_out[...] = pack[...]
    pieces = []
    for f in range(16):
        pieces.append(pack[f // 4, (f // 2) % 2, f % 2, 6:7, :].astype(F32))
    row[...] = jnp.broadcast_to(
        jnp.concatenate(pieces[:8] + [jnp.zeros((1, D), F32)] + pieces[8:], axis=1), (8, 3 * D)
    )
    for g in first:
        g.cross()
    for g in first:
        g.finish()
    kept.append(k.local(wq, wq_out))

    @pl.loop(0, 12)
    def _(n):
        cols = pl.ds(pl.multiple_of(n * 256, 256), 256)
        weight = wq[:, :, :, :, :, cols].reshape(D, 256)
        block = (dot(normed_out[...], weight) + row[0:1, cols]).astype(BF)
        merged[n // 4, 2 * (n % 4)] = block[:, :128]
        merged[n // 4, 2 * (n % 4) + 1] = block[:, 128:]

    mine = pl.ds(pl.multiple_of(k.me * BLK, BLK), BLK)
    kept_qkv = k.local(merged.at[:, k.me], qkv.at[:, mine])
    moved = [k.to(merged.at[:, t], qkv.at[:, mine], who) for t, who in k.rows_peers()]
    for g in rest:
        g.stage3()
    kept_seg.wait()
    wait_recv(segs)
    kept_qkv.wait()
    wait_recv(moved)
    kept.append(k.local(qkv, qkv_out))

    @pl.loop(0, 8)
    def _(t):
        for h in range(2):
            extend(k, seg_all, qkv, kx, qx, h, t)

    for t in range(8):
        flipped = qkv[2, BLK * t : BLK * (t + 1), :].astype(F32).T.astype(BF)
        for h in range(2):
            vt[h, :, BLK * t : BLK * (t + 1)] = flipped[64 * h : 64 * (h + 1)]

    for i in range(8):

        @pl.loop(0, 2)
        def _(h):
            attend(k, kx, qx, vt, ot, lse, h, i)
        if i == 5:
            for g in rest:
                if g.order == 0:
                    g.cross()

        both = jnp.concatenate(
            [ot[0, :, BLK * i : BLK * (i + 1)], ot[1, :, BLK * i : BLK * (i + 1)]], axis=0
        )
        mixed_send[i] = both.T.astype(BF)

    cols = pl.ds(pl.multiple_of(k.me * 128, 128), 128)
    kept.append(k.local(mixed_send.at[k.me], mixed.at[:, cols]))
    back = [k.to(mixed_send.at[t], mixed.at[:, cols], who) for t, who in k.rows_peers()]
    part = pl.ds(pl.multiple_of(k.me * BLK, BLK), BLK)
    kept.append(k.local(lse.at[:, :, part], lse_all.at[k.me]))
    for t, who in k.rows_peers():
        part = pl.ds(pl.multiple_of(t * BLK, BLK), BLK)
        back.append(k.to(lse.at[:, :, part], lse_all.at[k.me], who))
    for g in rest:
        if g.order != 0:
            g.cross()
    wait_recv(back)
    for g in rest:
        g.finish()
    for copy in kept:
        copy.wait()
    for g in first + rest:
        g.drain()
    wait_send(small_x + small_y + small_c + segs + moved + back)


def full_shape(cols):
    return (4, 2, 2, 2, 32, cols)


def forward_call(tokens, seg, small, wq, wo, w1, w2):
    hbm = pl.BlockSpec(memory_space=pl.ANY)
    vmem = pl.BlockSpec(memory_space=pltpu.VMEM)
    out = jax.ShapeDtypeStruct
    return pl.pallas_call(
        forward_kernel,
        name="forward",
        out_shape=(
            out(full_shape(3 * D), BF),
            out(full_shape(D), BF),
            out(full_shape(4 * D), BF),
            out((4, 2, 2, 4, 2, 32, D), BF),
            out((4, 2, 2, 16, 128), BF),
            out((BLK, D), BF),
            out((3, LENGTH, 128), BF),
            out((2, LENGTH, 128), BF),
            out((2, LENGTH, 128), BF),
            out((2, 64, LENGTH), F32),
            out((2, 8, LENGTH), F32),
            out((BLK, D), BF),
            out((8, 2, 8, BLK), F32),
        ),
        in_specs=[vmem, vmem, vmem, hbm, hbm, hbm, hbm],
        out_specs=(hbm, hbm, hbm, hbm, vmem, vmem, hbm, vmem, vmem, vmem, vmem, hbm, hbm),
        scratch_shapes=[
            pltpu.VMEM(full_shape(3 * D), BF),
            pltpu.VMEM((4, 2, 2, 16, 128), BF),
            pltpu.VMEM((8, 8, BLK), jnp.int32),
            pltpu.VMEM((8, 3 * D), F32),
            pltpu.VMEM((3, 8, BLK, 128), BF),
            pltpu.VMEM((3, LENGTH, 128), BF),
            pltpu.VMEM((2, 64, LENGTH), BF),
            pltpu.VMEM((8, BLK, 128), BF),
            pltpu.SemaphoreType.DMA((170,)),
            pltpu.SemaphoreType.DMA((170,)),
        ],
        compiler_params=pltpu.CompilerParams(
            collective_id=0, has_side_effects=True, vmem_limit_bytes=62 * MIB
        ),
    )(
        tokens,
        seg,
        small,
        wq.reshape(2, 32, 3 * D),
        wo.reshape(2, 32, D),
        w1.reshape(2, 32, 4 * D),
        w2.reshape(4, 2, 32, D),
    )


def small_pack(ln1_gain, ln1_bias, ln2_gain, ln2_bias, out_bias, fc2_bias, qkv_bias, fc1_bias):
    core = lax.axis_index("fsdp") % 2
    six = jnp.stack([ln1_gain, ln1_bias, ln2_gain, ln2_bias, out_bias, fc2_bias])
    none = jnp.zeros_like(six)
    halves = jnp.where(
        core == 0, jnp.concatenate([six, none], 1), jnp.concatenate([none, six], 1)
    )
    return jnp.concatenate(
        [halves, qkv_bias[None], fc1_bias.reshape(2, 128), jnp.zeros((7, 128), BF)], 0
    )


def unpack_row(pack, row):
    return (pack[:, :, 0, row] + pack[:, :, 1, row]).reshape(D)


REST_UNITS = (
    (3, 0, 0),
    (3, 1, 1),
    (3, 2, 2),
    (3, 3, 2),
    (2, 0, 0),
    (2, 1, 0),
    (2, 2, 1),
    (2, 3, 2),
    (1, 0, 0),
)
QKV_UNITS = ((0, 0, 0), (0, 1, 1), (0, 2, 2))
UNITS = REST_UNITS + QKV_UNITS
R1 = ((3, 2, 2, 32, D), (3, 4, 32, D), (3, 4, 2, 2, 32, 256))
R2 = ((3, 32, D), (3, 4, 32, 256), (3, 2, 2, 32, 256))


def count_of(order):
    return sum(1 for unit in UNITS if unit[2] == order)


class Reduce:
    def __init__(self, links, unit, n, grads, half, slots):
        self.tensor, self.unit, self.order = unit
        self.links, self.grad = links, grads[self.tensor]
        self.half = half.at[n]
        at = sum(1 for other in UNITS[:n] if other[2] == self.order)
        self.r1 = slots[self.order].at[at]
        self.r2 = slots[3 + self.order].at[at]
        self.r3 = slots[6].at[n]
        self.z_cols = self.cols_of(links.z)
        self.sent = []

    def cols_of(self, z):
        return pl.ds(pl.multiple_of(z * 256, 256), 256)

    def of_core(self, core):
        if self.tensor == 3:
            return self.grad.at[:, :, core, self.unit]
        return self.grad.at[:, :, core, :, :, pl.ds(self.unit * D, D)]

    def stage0(self):
        k = self.links
        self.swap = k.to(self.of_core(1 - k.core), self.half, k.peers("core")[0])
        self.sent.append(self.swap)

    def push(self, axis, src_of, slot):
        k = self.links
        here = {"x": k.x, "y": k.y, "z": k.z}[axis]
        self.coming = []
        for j, who in enumerate(k.peers(axis)):
            copy = k.to(src_of((here + j + 1) % 4), slot.at[j], who)
            self.coming.append(copy)
        self.sent += self.coming

    def add0(self, own):
        self.swap.wait_recv()

        @pl.loop(0, 16)
        def _(i):
            x, yh, yl = i // 4, (i // 2) % 2, i % 2
            total = self.half[x, yh, yl].astype(F32) + own(x, yh, yl).astype(F32)
            self.half[x, yh, yl] = total.astype(BF)

    def stage1(self):
        half = self.half
        if self.order == 0:
            self.push("x", lambda x: half.at[x], self.r1)
        elif self.order == 1:
            self.push("y", lambda y: half.at[:, y // 2, y % 2], self.r1)
        else:
            self.push("z", lambda z: half.at[:, :, :, :, self.cols_of(z)], self.r1)

    def sum1(self):
        k, half, got = self.links, self.half, self.r1
        wait_recv(self.coming)

        @pl.loop(0, 16 if self.order == 2 else 4)
        def _(i):
            if self.order == 0:
                spot, index = (k.x, i // 2, i % 2), (i // 2, i % 2)
            elif self.order == 1:
                spot, index = (i, k.yh, k.yl), (i,)
            else:
                index = (i // 4, (i // 2) % 2, i % 2)
                spot = index + (NONE, self.z_cols)
            total = half[spot].astype(F32)
            for j in range(3):
                total = total + got[(j,) + index].astype(F32)
            half[spot] = total.astype(BF)

    def stage2(self):
        k, half = self.links, self.half
        if self.order == 0:
            self.push("y", lambda y: half.at[k.x, y // 2, y % 2], self.r2)
        elif self.order == 1:
            self.push("z", lambda z: half.at[:, k.yh, k.yl, :, self.cols_of(z)], self.r2)
        else:
            self.push("x", lambda x: half.at[x, :, :, :, self.z_cols], self.r2)

    def sum2(self):
        k, half, got = self.links, self.half, self.r2
        wait_recv(self.coming)
        if self.order == 0:
            spot = (k.x, k.yh, k.yl)
            total = half[spot].astype(F32)
            for j in range(3):
                total = total + got[j].astype(F32)
            half[spot] = total.astype(BF)
            return

        @pl.loop(0, 4)
        def _(i):
            if self.order == 1:
                spot, index = (i, k.yh, k.yl, NONE, self.z_cols), (i,)
            else:
                spot, index = (k.x, i // 2, i % 2, NONE, self.z_cols), (i // 2, i % 2)
            total = half[spot].astype(F32)
            for j in range(3):
                total = total + got[(j,) + index].astype(F32)
            half[spot] = total.astype(BF)

    def stage3(self):
        k, half = self.links, self.half
        if self.order == 0:
            self.push("z", lambda z: half.at[k.x, k.yh, k.yl, :, self.cols_of(z)], self.r3)
        elif self.order == 1:
            self.push("x", lambda x: half.at[x, k.yh, k.yl, :, self.z_cols], self.r3)
        else:
            self.push("y", lambda y: half.at[k.x, y // 2, y % 2, :, self.z_cols], self.r3)

    def sum3(self, out_ref, position):
        k = self.links
        wait_recv(self.coming)
        total = self.half[k.x, k.yh, k.yl, :, self.z_cols].astype(F32)
        for j in range(3):
            total = total + self.r3[j].astype(F32)
        out_ref[k.me, :, 256 * position : 256 * (position + 1)] = total.astype(BF)

    def drain(self):
        wait_send(self.sent)

    def write(self, got, position, outs):
        out = outs[self.tensor]
        for t in range(8):
            piece = got[t, :, 256 * position : 256 * (position + 1)].astype(F32)
            if self.tensor == 3:
                out[self.unit, t // 4, :, 256 * (t % 4) : 256 * (t % 4 + 1)] = piece
            else:
                first = self.unit * D + 256 * (t % 4)
                out[t // 4, :, first : first + 256] = piece


def attend_back(kx, qx, vx, kt, do, delta, lse, dqt, h, j):
    keys = slice(BLK * j, BLK * (j + 1))
    down = lax.broadcasted_iota(jnp.int32, (BLK, BLK), 0)
    across = lax.broadcasted_iota(jnp.int32, (BLK, BLK), 1)
    grad_key = grad_value = None
    cuts = [BLK * j, BLK * (j + 1)] + list(range(BLK * (j + 1) + 768, LENGTH, 768))
    if cuts[-1] < LENGTH:
        cuts.append(LENGTH)
    for n in range(len(cuts) - 1):
        rows = slice(cuts[n], cuts[n + 1])
        queries = qx[h, rows, :]
        scores = dot_nt(kx[h, keys, :], queries)
        if n == 0:
            scores = jnp.where(down <= across, scores, -BIG)
        probs = jnp.exp(scores - lse[h, 1:2, rows])
        grad_out = do[rows, :]
        grad_probs = dot_nt(vx[h, keys, :], grad_out)
        grad_scores = (probs * (grad_probs - delta[h, 0:1, rows])).astype(BF)
        value_part = dot(probs.astype(BF), grad_out)
        key_part = dot(grad_scores, queries)
        grad_value = value_part if n == 0 else grad_value + value_part
        grad_key = key_part if n == 0 else grad_key + key_part
        query_part = dot(kt[h, :, keys], grad_scores)
        if j == 0:
            dqt[h, :, rows] = query_part
        else:
            dqt[h, :, rows] += query_part
    return grad_key, grad_value


def backward_kernel(
    g_out,
    g_fc1,
    g_fc2,
    grad_mixed,
    qkv,
    kx,
    qx,
    ot,
    lse,
    normed,
    wq_in,
    pack,
    tokens,
    grad_middle,
    small_in,
    o_qkv,
    o_out,
    o_fc1,
    o_fc2,
    o_small,
    input_grad,
    half,
    r1x,
    r1y,
    r1z,
    r2x,
    r2y,
    r2z,
    r3,
    own,
    g_qkv,
    w_slot,
    vx,
    kt,
    do,
    delta,
    dqt,
    g_send,
    g_merged,
    normed_t,
    f_rest,
    f_qkv,
    small,
    small_core,
    small_x,
    small_y,
    small_z,
    gn,
    send,
    recv,
):
    k = Links(send, recv)
    k.barrier()
    grads = (g_qkv, g_out, g_fc1, g_fc2)
    slots = (r1x, r1y, r1z, r2x, r2y, r2z, r3)
    units = [Reduce(k, unit, n, grads, half, slots) for n, unit in enumerate(UNITS)]
    rest, last = units[:9], units[9:]
    for u in rest:
        u.stage0()
    mine = pl.ds(pl.multiple_of(k.me * BLK, BLK), BLK)

    def heads_of(t):
        return pl.ds(pl.multiple_of(t * 128, 128), 128)

    kept_do = k.local(grad_mixed.at[:, heads_of(k.me)], do.at[mine])
    moved = [
        k.to(grad_mixed.at[:, heads_of(t)], do.at[mine], who) for t, who in k.rows_peers()
    ]
    loads = [k.local(u.of_core(k.core), own.at[n]) for n, u in enumerate(rest[:2])]

    lane = lax.broadcasted_iota(jnp.int32, (BLK, 128), 1)
    for t in range(8):
        rows = slice(BLK * t, BLK * (t + 1))
        value = qkv[2, rows, :]
        flipped = qkv[1, rows, :].astype(F32).T.astype(BF)
        for h in range(2):
            vx[h, rows, :] = jnp.where((lane // 64) == h, value.astype(F32), 0.0).astype(BF)
            kt[h, :, rows] = flipped[64 * h : 64 * (h + 1)]
    normed_t[...] = normed[...].astype(F32).T.astype(BF)
    kept_do.wait()
    wait_recv(moved)
    for t in range(8):
        rows = slice(BLK * t, BLK * (t + 1))
        flipped = do[rows, :].astype(F32).T
        for h in range(2):
            product = flipped[64 * h : 64 * (h + 1)] * ot[h, :, rows]
            delta[h, :, rows] = jnp.broadcast_to(
                jnp.sum(product, axis=0, keepdims=True), (8, BLK)
            )
    for n, u in enumerate(rest):
        loads[n].wait()
        u.add0(lambda x, yh, yl, n=n: own[n % 2, x, yh, yl])
        u.stage1()
        if n + 2 < len(rest):
            loads.append(k.local(rest[n + 2].of_core(k.core), own.at[n % 2]))

    back = []
    for t, who in k.rows_peers():
        i = k.used
        k.used += 1
        copy = pltpu.make_async_remote_copy(
            src_ref=g_send.at[:, t],
            dst_ref=g_merged.at[:, :, heads_of(k.me)],
            send_sem=k.send.at[i],
            recv_sem=k.recv.at[i],
            device_id=who,
        )
        back.append((t, copy))
    for j in range(8):
        found = [attend_back(kx, qx, vx, kt, do, delta, lse, dqt, h, j) for h in range(2)]
        left = (lane // 64) == 0
        for s, position in ((1, 0), (2, 1)):
            both = jnp.where(left, found[0][position], found[1][position])
            g_send[s, j] = both.astype(BF)
        rows = slice(BLK * j, BLK * (j + 1))
        query = jnp.concatenate([dqt[0, :, rows], dqt[1, :, rows]], axis=0).T * 0.125
        g_send[0, j] = query.astype(BF)
        if j in (3, 7):
            for t, copy in back:
                pl.when((t // 4) == (j // 4))(copy.start)
    kept_g = k.local(g_send.at[:, k.me], g_merged.at[:, :, heads_of(k.me)])

    def w_load(s):
        cols = pl.ds(s * D, D)
        return k.local(wq_in.at[:, :, :, :, :, cols], w_slot.at[s % 2])

    w_loads = [w_load(0), w_load(1)]
    for u in rest:
        u.sum1()
        u.stage2()
    kept_g.wait()
    for _, copy in back:
        copy.wait_recv()

    for s in range(3):

        @pl.loop(0, 4)
        def _(n):
            cols = pl.ds(pl.multiple_of(n * 256, 256), 256)
            block = dot(normed_t[...], g_merged[s, :, cols]).astype(BF)
            there = pl.ds(pl.multiple_of(s * D + n * 256, 256), 256)
            g_qkv[:, :, :, :, :, there] = block.reshape(4, 2, 2, 2, 32, 256)

        last[s].stage0()
    for u in rest:
        u.sum2()
        u.stage3()

    for s in range(3):
        w_loads[s].wait()
        for n in range(4):
            weight = w_slot[s % 2, n].reshape(256, D)
            part = dot_nt(g_merged[s], weight)
            cols = slice(256 * n, 256 * (n + 1))
            if s == 0:
                gn[:, cols] = part
            else:
                gn[:, cols] += part
        if s == 0:
            w_loads.append(w_load(2))
    for s, u in enumerate(last):
        cols = pl.ds(s * D, D)
        u.add0(lambda x, yh, yl, cols=cols: g_qkv[x, yh, k.core, yl, :, cols])
        u.stage1()

    values = tokens[...].astype(F32)
    center = values - jnp.mean(values, axis=1, keepdims=True)
    scale = lax.rsqrt(jnp.mean(center * center, axis=1, keepdims=True) + 1e-05)
    center = center * scale
    grad_normed = gn[...]
    by_gain = jnp.sum(grad_normed * center, axis=0, keepdims=True)
    by_bias = jnp.sum(grad_normed, axis=0, keepdims=True)
    inner = grad_normed * small_row(pack, 0)
    part = inner - jnp.mean(inner, axis=1, keepdims=True)
    part = part - center * jnp.mean(inner * center, axis=1, keepdims=True)
    input_grad[...] = grad_middle[...] + part * scale
    by_query = jnp.sum(g_merged[0].astype(F32), axis=0, keepdims=True)
    by_value = jnp.sum(g_merged[2].astype(F32), axis=0, keepdims=True)
    small[...] = small_in[...]
    for x in range(4):
        for yh in range(2):
            n = 2 * x + yh
            cols = slice(128 * n, 128 * (n + 1))
            small[x, yh, 0:1, :] = by_gain[:, cols]
            small[x, yh, 1:2, :] = by_bias[:, cols]
            source = by_query if x < 2 else by_value
            first = 256 * (n % 4)
            small[x, yh, 6:7, :] = source[:, first : first + 128]
            small[x, yh, 7:8, :] = source[:, first + 128 : first + 256]
    small_sent = [k.to(small, small_core, k.peers("core")[0])]

    for n, u in enumerate(rest):
        u.sum3(f_rest, n)
    gathered = [k.to(f_rest.at[k.me], f_rest.at[k.me], who) for _, who in k.rows_peers()]

    small_sent[0].wait()
    small[...] = small[...] + small_core[...]
    coming = [
        k.to(small.at[(k.x + j + 1) % 4], small_x.at[j], who)
        for j, who in enumerate(k.peers("x"))
    ]
    small_sent += coming
    for u in last:
        u.sum1()
        u.stage2()
    wait_recv(coming)
    small[k.x] = small[k.x] + small_x[0] + small_x[1] + small_x[2]
    coming = [
        k.to(small.at[k.x, ((k.y + j + 1) % 4) // 2], small_y.at[j], who)
        for j, who in enumerate(k.peers("y"))
    ]
    small_sent += coming
    for u in last:
        u.sum2()
        u.stage3()
    wait_recv(coming)
    small_z[3] = small[k.x, k.yh] + small_y[0] + small_y[1] + small_y[2]
    coming = [k.to(small_z.at[3], small_z.at[j], who) for j, who in enumerate(k.peers("z"))]
    small_sent += coming
    for n, u in enumerate(last):
        u.sum3(f_qkv, n)
    gathered_qkv = [k.to(f_qkv.at[k.me], f_qkv.at[k.me], who) for _, who in k.rows_peers()]
    outs = (o_qkv, o_out, o_fc1, o_fc2)
    wait_recv(gathered)
    for n, u in enumerate(rest):
        u.write(f_rest, n, outs)
    wait_recv(coming)
    o_small[...] = small_z[0] + small_z[1] + small_z[2] + small_z[3]
    wait_recv(gathered_qkv)
    for n, u in enumerate(last):
        u.write(f_qkv, n, outs)
    for u in units:
        u.drain()
    wait_send(moved + [copy for _, copy in back] + small_sent[1:] + gathered + gathered_qkv)


def backward_call(
    g_out, g_fc1, g_fc2, grad_mixed, qkv, kx, qx, ot, lse, normed, wq, pack, tokens, grad_middle, small
):
    hbm = pl.BlockSpec(memory_space=pl.ANY)
    vmem = pl.BlockSpec(memory_space=pltpu.VMEM)
    out = jax.ShapeDtypeStruct
    mem = pltpu.VMEM
    return pl.pallas_call(
        backward_kernel,
        name="backward",
        out_shape=(
            out((2, 32, 3 * D), F32),
            out((2, 32, D), F32),
            out((2, 32, 4 * D), F32),
            out((4, 2, 32, D), F32),
            out((16, 128), F32),
            out((BLK, D), F32),
        ),
        in_specs=[hbm, hbm, hbm, hbm, vmem, vmem, vmem, vmem, vmem, vmem, hbm, vmem, vmem, vmem, vmem],
        out_specs=(vmem,) * 6,
        scratch_shapes=[
            mem((12, 4, 2, 2, 32, D), BF),
            *[mem((count_of(order),) + R1[order], BF) for order in range(3)],
            *[mem((count_of(order),) + R2[order], BF) for order in range(3)],
            mem((12, 3, 32, 256), BF),
            mem((2, 4, 2, 2, 32, D), BF),
            mem(full_shape(3 * D), BF),
            mem((2,) + full_shape(D), BF),
            mem((2, LENGTH, 128), BF),
            mem((2, 64, LENGTH), BF),
            mem((LENGTH, 128), BF),
            mem((2, 8, LENGTH), F32),
            mem((2, 64, LENGTH), F32),
            mem((3, 8, BLK, 128), BF),
            mem((3, BLK, D), BF),
            mem((D, BLK), BF),
            mem((8, 32, 9 * 256), BF),
            mem((8, 32, 3 * 256), BF),
            mem((4, 2, 16, 128), F32),
            mem((4, 2, 16, 128), F32),
            mem((3, 2, 16, 128), F32),
            mem((3, 16, 128), F32),
            mem((4, 16, 128), F32),
            mem((BLK, D), F32),
            pltpu.SemaphoreType.DMA((190,)),
            pltpu.SemaphoreType.DMA((190,)),
        ],
        compiler_params=pltpu.CompilerParams(
            collective_id=1, has_side_effects=True, vmem_limit_bytes=63 * MIB
        ),
    )(
        g_out.reshape(full_shape(D)),
        g_fc1.reshape(full_shape(4 * D)),
        g_fc2.reshape(4, 2, 2, 4, 2, 32, D),
        grad_mixed,
        qkv,
        kx,
        qx,
        ot,
        lse,
        normed,
        wq,
        pack,
        tokens,
        grad_middle,
        small,
    )


def layer_norm(values, gain_vec, bias_vec):
    center = values - jnp.mean(values, axis=-1, keepdims=True)
    spread = jnp.mean(center * center, axis=-1, keepdims=True)
    return center * lax.rsqrt(spread + 1e-05) * gain_vec + bias_vec


def gelu_tanh(values):
    return jax.nn.gelu(values, approximate=True)


def matmul_tn(left, right):
    return lax.dot_general(
        left, right, (((0,), (0,)), ((), ())), preferred_element_type=jnp.float32
    )


def matmul_nt(left, right):
    return lax.dot_general(
        left, right, (((1,), (1,)), ((), ())), preferred_element_type=jnp.float32
    )


def matmul(left, right):
    return jnp.dot(left, right, preferred_element_type=jnp.float32)


def local(
    tokens,
    segment_ids,
    cotangent,
    ln1_gain,
    ln1_bias,
    qkv_weight,
    qkv_bias,
    out_weight,
    out_bias,
    ln2_gain,
    ln2_bias,
    fc1_weight,
    fc1_bias,
    fc2_weight,
    fc2_bias,
):
    block_len = tokens.shape[1]
    small = small_pack(
        ln1_gain, ln1_bias, ln2_gain, ln2_bias, out_bias, fc2_bias, qkv_bias, fc1_bias
    )
    flat = tokens.reshape(block_len, D)
    (wq, wo, w1, w2, pack, normed, qkv, kx, qx, ot, lse, mixed, lse_all) = forward_call(
        flat,
        jnp.broadcast_to(segment_ids, (8, block_len)),
        small,
        qkv_weight,
        out_weight,
        fc1_weight,
        fc2_weight,
    )
    out_mat = wo.reshape(D, D)
    up_mat = w1.reshape(D, 4 * D)
    down_mat = w2.reshape(4 * D, D)
    gain_two = unpack_row(pack, 2).astype(jnp.float32)
    bias_two = unpack_row(pack, 3).astype(jnp.float32)
    out_vec = unpack_row(pack, 4).astype(jnp.float32)
    down_vec = unpack_row(pack, 5).astype(jnp.float32)
    up_vec = pack[:, :, :, 7:9].reshape(4 * D).astype(jnp.float32)
    log_sums = lse_all[:, :, 0].reshape(1, HEADS, block_len)

    middle = flat.astype(jnp.float32) + matmul(mixed, out_mat) + out_vec
    normed_two = layer_norm(middle, gain_two, bias_two).astype(jnp.bfloat16)
    hidden = matmul(normed_two, up_mat) + up_vec
    active = gelu_tanh(hidden).astype(jnp.bfloat16)
    output = middle + matmul(active, down_mat) + down_vec

    grad_down = cotangent.reshape(block_len, D)
    grad_output = grad_down.astype(jnp.float32)
    g_fc2 = matmul_tn(active, grad_down).astype(jnp.bfloat16)
    fc2_bias_grad = jnp.sum(grad_output, axis=0)
    grad_active = matmul_nt(grad_down, down_mat)
    _, gelu_pull = jax.vjp(gelu_tanh, hidden)
    grad_hidden = gelu_pull(grad_active)[0].astype(jnp.bfloat16)
    g_fc1 = matmul_tn(normed_two, grad_hidden).astype(jnp.bfloat16)
    fc1_bias_grad = jnp.sum(grad_hidden.astype(jnp.float32), axis=0)
    grad_normed_two = matmul_nt(grad_hidden, up_mat)
    _, norm_pull = jax.vjp(layer_norm, middle, gain_two, bias_two)
    part, ln2_gain_grad, ln2_bias_grad = norm_pull(grad_normed_two)
    grad_middle = grad_output + part
    grad_branch = grad_middle.astype(jnp.bfloat16)
    g_out = matmul_tn(mixed, grad_branch).astype(jnp.bfloat16)
    out_bias_grad = jnp.sum(grad_branch.astype(jnp.float32), axis=0)
    grad_mixed = matmul_nt(grad_branch, out_mat).astype(jnp.bfloat16)

    four = jnp.stack([ln2_gain_grad, ln2_bias_grad, out_bias_grad, fc2_bias_grad])
    four = four.reshape(4, 4, 2, 128).transpose(1, 2, 0, 3)
    none = jnp.zeros((4, 2, 2, 128), jnp.float32)
    small_grads = jnp.concatenate(
        [none, four, none, fc1_bias_grad.reshape(4, 2, 4, 128), none, none], axis=2
    )
    g_qkv, g_wo, g_up, g_down, small_sums, input_grad = backward_call(
        g_out,
        g_fc1,
        g_fc2,
        grad_mixed,
        qkv,
        kx,
        qx,
        ot,
        lse,
        normed,
        wq,
        pack,
        flat,
        grad_middle,
        small_grads,
    )
    core = lax.axis_index("fsdp") % 2
    halves = lax.dynamic_slice_in_dim(small_sums[:6], core * 64, 64, 1)
    g_qkvb = lax.dynamic_slice_in_dim(small_sums, 6 + core, 1, 0).reshape(128)
    g_upb = lax.dynamic_slice_in_dim(small_sums, 8 + 2 * core, 2, 0).reshape(256)
    return (
        output.astype(jnp.bfloat16).reshape(1, block_len, D),
        input_grad.reshape(1, block_len, D),
        halves[0],
        halves[1],
        g_qkv.reshape(64, 3 * D),
        g_qkvb,
        g_wo.reshape(64, D),
        halves[4],
        halves[2],
        halves[3],
        g_up.reshape(64, 4 * D),
        g_upb,
        g_down.reshape(256, D),
        halves[5],
        log_sums,
    )


def solution(mesh):
    placed = (
        P("fsdp", "ctx", None),
        P("fsdp", "ctx"),
        P("fsdp", "ctx", None),
        P("fsdp"),
        P("fsdp"),
        P("fsdp", None),
        P("fsdp"),
        P("fsdp", None),
        P("fsdp"),
        P("fsdp"),
        P("fsdp"),
        P("fsdp", None),
        P("fsdp"),
        P("fsdp", None),
        P("fsdp"),
    )
    return jax.shard_map(
        local,
        mesh=mesh,
        in_specs=placed,
        out_specs=(
            P("fsdp", "ctx", None),
            P("fsdp", "ctx", None),
            P("fsdp"),
            P("fsdp"),
            P("fsdp", None),
            P("fsdp"),
            P("fsdp", None),
            P("fsdp"),
            P("fsdp"),
            P("fsdp"),
            P("fsdp", None),
            P("fsdp"),
            P("fsdp", None),
            P("fsdp"),
            P("fsdp", None, "ctx"),
        ),
        check_vma=False,
    )
```

```python
import functools

import jax
import jax.numpy as jnp
from jax import lax
from jax.experimental import pallas as pl
from jax.experimental.pallas import tpu as pltpu
from jax.sharding import PartitionSpec as P

D = 1024
HEADS = 16
HEAD_DIM = 64
LENGTH = 2048
BLK = 256
BF = jnp.bfloat16
F32 = jnp.float32
BIG = 2.0**100
MIB = 2**20
NONE = slice(None)

QKV_SEGS = ((0, 0, 0, 1), (0, 1, 1, 1), (0, 2, 2, 1))
REST_SEGS = (
    (1, 0, 0, 1),
    (2, 0, 0, 2),
    (2, 1, 2, 1),
    (2, 2, 3, 1),
    (3, 0, 0, 2),
    (3, 1, 2, 1),
    (3, 2, 3, 1),
)


def place():
    c = lax.axis_index("ctx")
    f = lax.axis_index("fsdp")
    return f // 4, ((f // 2) % 2) * 2 + c // 4, c % 4, f % 2


def device(x, y, z, core):
    return {"ctx": (y % 2) * 4 + z, "fsdp": x * 4 + (y // 2) * 2 + core}


class Links:
    def __init__(self, send, recv):
        self.send, self.recv, self.used = send, recv, 0
        self.x, self.y, self.z, self.core = place()
        self.yh, self.yl = self.y // 2, self.y % 2
        self.me = self.yl * 4 + self.z

    def peers(self, axis):
        x, y, z, c = self.x, self.y, self.z, self.core
        if axis == "x":
            return [device((x + j) % 4, y, z, c) for j in (1, 2, 3)]
        if axis == "y":
            return [device(x, (y + j) % 4, z, c) for j in (1, 2, 3)]
        if axis == "z":
            return [device(x, y, (z + j) % 4, c) for j in (1, 2, 3)]
        return [device(x, y, z, 1 - c)]

    def rows_peers(self):
        out = []
        for j in range(1, 8):
            t = (self.me + j) % 8
            out.append((t, device(self.x, self.yh * 2 + t // 4, t % 4, self.core)))
        return out

    def barrier(self):
        everyone = self.peers("x") + self.peers("y") + self.peers("z") + self.peers("core")
        for j in (1, 2, 3):
            everyone.append(device(self.x, self.yh * 2 + 1 - self.yl, (self.z + j) % 4, self.core))
        sem = pltpu.get_barrier_semaphore()
        for who in everyone:
            pl.semaphore_signal(sem, inc=1, device_id=who)
        pl.semaphore_wait(sem, len(everyone))

    def to(self, src, dst, who):
        i = self.used
        self.used += 1
        copy = pltpu.make_async_remote_copy(
            src_ref=src,
            dst_ref=dst,
            send_sem=self.send.at[i],
            recv_sem=self.recv.at[i],
            device_id=who,
        )
        copy.start()
        return copy

    def local(self, src, dst):
        i = self.used
        self.used += 1
        copy = pltpu.make_async_copy(src, dst, self.send.at[i])
        copy.start()
        return copy


def wait_recv(copies):
    for copy in copies:
        copy.wait_recv()


def wait_send(copies):
    for copy in copies:
        copy.wait_send()


class Gather:
    def __init__(self, links, full, shard, seg):
        tensor, self.order, first, count = seg
        self.links, self.full, self.shard = links, full, shard
        self.blocked = tensor == 3
        if self.blocked:
            self.units = (pl.ds(first, count),)
            self.all_cols = pl.ds(0, D)
            width = D // 4
            self.z_cols = pl.ds(pl.multiple_of(links.z * width, width), width)
        else:
            self.units = ()
            self.all_cols = pl.ds(first * D, count * D)
            width = count * D // 4
            self.z_cols = pl.ds(pl.multiple_of(first * D + links.z * width, width), width)
        self.sent = []

    def view(self, x, yh, yl, cols):
        return self.full.at[(x, yh, self.links.core) + self.units + (yl, NONE, cols)]

    def own(self, cols):
        return self.shard.at[self.units + (self.links.yl, NONE, cols)]

    def push(self, src, dst, axis):
        now = [self.links.to(src, dst, who) for who in self.links.peers(axis)]
        self.sent += now
        return now

    def stage1(self):
        k = self.links
        cols = self.all_cols if self.order == 0 else self.z_cols
        dst = self.view(k.x, k.yh, k.yl, cols)
        self.kept = k.local(self.own(cols), dst)
        self.first = self.push(self.own(cols), dst, "x" if self.order == 1 else "y")

    def stage2(self):
        k = self.links
        self.kept.wait()
        wait_recv(self.first)
        if self.order == 0:
            part = self.view(k.x, NONE, NONE, self.all_cols)
            self.last = self.push(part, part, "x")
        elif self.order == 1:
            part = self.view(NONE, k.yh, k.yl, self.z_cols)
            self.second = self.push(part, part, "z")
        else:
            part = self.view(k.x, NONE, NONE, self.z_cols)
            self.second = self.push(part, part, "x")

    def stage3(self):
        k = self.links
        if self.order == 0:
            return
        wait_recv(self.second)
        if self.order == 1:
            part = self.view(NONE, k.yh, k.yl, self.all_cols)
            self.last = self.push(part, part, "y")
        else:
            part = self.view(NONE, NONE, NONE, self.z_cols)
            self.last = self.push(part, part, "z")

    def cross(self):
        wait_recv(self.last)
        part = self.view(NONE, NONE, NONE, self.all_cols)
        self.swapped = self.push(part, part, "core")

    def finish(self):
        wait_recv(self.swapped)

    def drain(self):
        wait_send(self.sent)


def small_row(pack, row):
    pieces = []
    for x in range(4):
        for yh in range(2):
            pieces.append(
                pack[x, yh, 0, row : row + 1, :].astype(F32)
                + pack[x, yh, 1, row : row + 1, :].astype(F32)
            )
    return jnp.concatenate(pieces, axis=1)


def dot_nt(a, b):
    return lax.dot_general(a, b, (((1,), (1,)), ((), ())), preferred_element_type=F32)


def dot_tn(a, b):
    return lax.dot_general(a, b, (((0,), (0,)), ((), ())), preferred_element_type=F32)


def dot(a, b):
    return jnp.dot(a, b, preferred_element_type=F32)


def slope_of(links, h, shape):
    power = (links.me * 2 + h + 1).astype(F32) * -0.5
    return jnp.exp2(jnp.full(shape, power, F32)) * (4.0 / LENGTH)


def extend(links, seg_ref, qkv_ref, kx_ref, qx_ref, h, t):
    rows = pl.ds(t * BLK, BLK)
    seg = jnp.broadcast_to(seg_ref[t, 0:1, :].astype(F32), (128, BLK)).T
    lane = lax.broadcasted_iota(jnp.int32, (BLK, 128), 1)
    mine = (lane // 64) == h
    e = lane - 64 * (1 - h)
    where = lax.broadcasted_iota(jnp.int32, (BLK, 128), 0) + t * BLK
    bias = slope_of(links, h, (BLK, 128)) * where.astype(F32)
    high = bias.astype(BF).astype(F32)
    mid = (bias - high).astype(BF).astype(F32)
    low = bias - high - mid
    doc = (e - 3).astype(F32)
    is_doc = (e >= 3) & (e <= 6)
    same = seg == doc
    key_extra = jnp.where(is_doc & jnp.logical_not(same), 1.0, 0.0)
    key_extra = jnp.where(e == 0, high, jnp.where(e == 1, mid, jnp.where(e == 2, low, key_extra)))
    query_extra = jnp.where(is_doc & same, -BIG, 0.0)
    query_extra = jnp.where((e >= 0) & (e <= 2), 1.0, query_extra)
    query = qkv_ref[0, rows, :].astype(F32) * 0.125
    key = qkv_ref[1, rows, :].astype(F32)
    kx_ref[h, rows, :] = jnp.where(mine, key, key_extra).astype(BF)
    qx_ref[h, rows, :] = jnp.where(mine, query, query_extra).astype(BF)


def attend(links, kx_ref, qx_ref, vt_ref, ot_ref, lse_ref, h, i):
    keys = BLK * (i + 1)
    qb = qx_ref[h, BLK * i : keys, :]
    down = lax.broadcasted_iota(jnp.int32, (BLK, BLK), 0)
    across = lax.broadcasted_iota(jnp.int32, (BLK, BLK), 1)
    edge = jnp.where(down <= across, dot_nt(kx_ref[h, BLK * i : keys, :], qb), -BIG)
    top = jnp.max(edge, axis=0, keepdims=True)
    if i:
        past = dot_nt(kx_ref[h, 0 : BLK * i, :], qb)
        top = jnp.maximum(top, jnp.max(past, axis=0, keepdims=True))
    edge = jnp.exp(edge - top)
    total = jnp.sum(edge, axis=0, keepdims=True)
    out = dot(vt_ref[h, :, BLK * i : keys], edge.astype(BF))
    if i:
        past = jnp.exp(past - top)
        total = total + jnp.sum(past, axis=0, keepdims=True)
        out = out + dot(vt_ref[h, :, 0 : BLK * i], past.astype(BF))
    ot_ref[h, :, BLK * i : keys] = out / total
    where = (lax.broadcasted_iota(jnp.int32, (1, BLK), 1) + BLK * i).astype(F32)
    shifted = top + jnp.log(total)
    final = shifted - slope_of(links, h, (1, BLK)) * where
    first = lax.broadcasted_iota(jnp.int32, (8, BLK), 0) == 0
    lse_ref[h, :, BLK * i : keys] = jnp.where(first, final, shifted)


def forward_kernel(
    tokens,
    seg,
    small,
    wq_in,
    wo_in,
    w1_in,
    w2_in,
    wq_out,
    wo,
    w1,
    w2,
    pack_out,
    normed_out,
    qkv_out,
    kx,
    qx,
    ot,
    lse,
    mixed,
    lse_all,
    wq,
    pack,
    seg_all,
    row,
    merged,
    qkv,
    vt,
    mixed_send,
    send,
    recv,
):
    k = Links(send, recv)
    k.barrier()
    sent, kept = [], []

    kept_small = k.local(small, pack.at[k.x, k.yh, k.core])
    small_x = [k.to(small, pack.at[k.x, k.yh, k.core], who) for who in k.peers("x")]
    fulls, shards = (wq, wo, w1, w2), (wq_in, wo_in, w1_in, w2_in)
    first = [Gather(k, fulls[s[0]], shards[s[0]], s) for s in QKV_SEGS]
    rest = [Gather(k, fulls[s[0]], shards[s[0]], s) for s in REST_SEGS]
    for g in first:
        g.stage1()
    kept_seg = k.local(seg, seg_all.at[k.me])
    segs = [k.to(seg, seg_all.at[k.me], who) for _, who in k.rows_peers()]
    for g in first:
        g.stage2()
    kept_small.wait()
    wait_recv(small_x)
    part = pack.at[:, k.yh, k.core]
    small_y = [k.to(part, part, k.peers("y")[1])]
    for g in rest:
        g.stage1()
    for g in first:
        g.stage3()
    wait_recv(small_y)
    part = pack.at[:, :, k.core]
    small_c = [k.to(part, part, k.peers("core")[0])]

    for g in rest:
        g.stage2()
    values = tokens[...].astype(F32)
    center = values - jnp.mean(values, axis=1, keepdims=True)
    center = center * lax.rsqrt(jnp.mean(center * center, axis=1, keepdims=True) + 1e-05)
    wait_recv(small_c)
    normed_out[...] = (center * small_row(pack, 0) + small_row(pack, 1)).astype(BF)
    pack_out[...] = pack[...]
    pieces = []
    for f in range(16):
        pieces.append(pack[f // 4, (f // 2) % 2, f % 2, 6:7, :].astype(F32))
    row[...] = jnp.broadcast_to(
        jnp.concatenate(pieces[:8] + [jnp.zeros((1, D), F32)] + pieces[8:], axis=1), (8, 3 * D)
    )
    for g in first:
        g.cross()
    for g in first:
        g.finish()
    kept.append(k.local(wq, wq_out))

    @pl.loop(0, 12)
    def _(n):
        cols = pl.ds(pl.multiple_of(n * 256, 256), 256)
        weight = wq[:, :, :, :, :, cols].reshape(D, 256)
        block = (dot(normed_out[...], weight) + row[0:1, cols]).astype(BF)
        merged[n // 4, 2 * (n % 4)] = block[:, :128]
        merged[n // 4, 2 * (n % 4) + 1] = block[:, 128:]

    mine = pl.ds(pl.multiple_of(k.me * BLK, BLK), BLK)
    kept_qkv = k.local(merged.at[:, k.me], qkv.at[:, mine])
    moved = [k.to(merged.at[:, t], qkv.at[:, mine], who) for t, who in k.rows_peers()]
    for g in rest:
        g.stage3()
    kept_seg.wait()
    wait_recv(segs)
    kept_qkv.wait()
    wait_recv(moved)
    kept.append(k.local(qkv, qkv_out))

    @pl.loop(0, 8)
    def _(t):
        for h in range(2):
            extend(k, seg_all, qkv, kx, qx, h, t)

    for t in range(8):
        flipped = qkv[2, BLK * t : BLK * (t + 1), :].astype(F32).T.astype(BF)
        for h in range(2):
            vt[h, :, BLK * t : BLK * (t + 1)] = flipped[64 * h : 64 * (h + 1)]

    for i in range(8):

        @pl.loop(0, 2)
        def _(h):
            attend(k, kx, qx, vt, ot, lse, h, i)
        if i == 5:
            for g in rest:
                if g.order == 0:
                    g.cross()

        both = jnp.concatenate(
            [ot[0, :, BLK * i : BLK * (i + 1)], ot[1, :, BLK * i : BLK * (i + 1)]], axis=0
        )
        mixed_send[i] = both.T.astype(BF)

    cols = pl.ds(pl.multiple_of(k.me * 128, 128), 128)
    kept.append(k.local(mixed_send.at[k.me], mixed.at[:, cols]))
    back = [k.to(mixed_send.at[t], mixed.at[:, cols], who) for t, who in k.rows_peers()]
    part = pl.ds(pl.multiple_of(k.me * BLK, BLK), BLK)
    kept.append(k.local(lse.at[:, :, part], lse_all.at[k.me]))
    for t, who in k.rows_peers():
        part = pl.ds(pl.multiple_of(t * BLK, BLK), BLK)
        back.append(k.to(lse.at[:, :, part], lse_all.at[k.me], who))
    for g in rest:
        if g.order != 0:
            g.cross()
    wait_recv(back)
    for g in rest:
        g.finish()
    for copy in kept:
        copy.wait()
    for g in first + rest:
        g.drain()
    wait_send(small_x + small_y + small_c + segs + moved + back)


def full_shape(cols):
    return (4, 2, 2, 2, 32, cols)


def forward_call(tokens, seg, small, wq, wo, w1, w2):
    hbm = pl.BlockSpec(memory_space=pl.ANY)
    vmem = pl.BlockSpec(memory_space=pltpu.VMEM)
    out = jax.ShapeDtypeStruct
    return pl.pallas_call(
        forward_kernel,
        name="forward",
        out_shape=(
            out(full_shape(3 * D), BF),
            out(full_shape(D), BF),
            out(full_shape(4 * D), BF),
            out((4, 2, 2, 4, 2, 32, D), BF),
            out((4, 2, 2, 16, 128), BF),
            out((BLK, D), BF),
            out((3, LENGTH, 128), BF),
            out((2, LENGTH, 128), BF),
            out((2, LENGTH, 128), BF),
            out((2, 64, LENGTH), F32),
            out((2, 8, LENGTH), F32),
            out((BLK, D), BF),
            out((8, 2, 8, BLK), F32),
        ),
        in_specs=[vmem, vmem, vmem, hbm, hbm, hbm, hbm],
        out_specs=(hbm, hbm, hbm, hbm, vmem, vmem, hbm, vmem, vmem, vmem, vmem, hbm, hbm),
        scratch_shapes=[
            pltpu.VMEM(full_shape(3 * D), BF),
            pltpu.VMEM((4, 2, 2, 16, 128), BF),
            pltpu.VMEM((8, 8, BLK), jnp.int32),
            pltpu.VMEM((8, 3 * D), F32),
            pltpu.VMEM((3, 8, BLK, 128), BF),
            pltpu.VMEM((3, LENGTH, 128), BF),
            pltpu.VMEM((2, 64, LENGTH), BF),
            pltpu.VMEM((8, BLK, 128), BF),
            pltpu.SemaphoreType.DMA((170,)),
            pltpu.SemaphoreType.DMA((170,)),
        ],
        compiler_params=pltpu.CompilerParams(
            collective_id=0, has_side_effects=True, vmem_limit_bytes=62 * MIB
        ),
    )(
        tokens,
        seg,
        small,
        wq.reshape(2, 32, 3 * D),
        wo.reshape(2, 32, D),
        w1.reshape(2, 32, 4 * D),
        w2.reshape(4, 2, 32, D),
    )


def small_pack(ln1_gain, ln1_bias, ln2_gain, ln2_bias, out_bias, fc2_bias, qkv_bias, fc1_bias):
    core = lax.axis_index("fsdp") % 2
    six = jnp.stack([ln1_gain, ln1_bias, ln2_gain, ln2_bias, out_bias, fc2_bias])
    none = jnp.zeros_like(six)
    halves = jnp.where(
        core == 0, jnp.concatenate([six, none], 1), jnp.concatenate([none, six], 1)
    )
    return jnp.concatenate(
        [halves, qkv_bias[None], fc1_bias.reshape(2, 128), jnp.zeros((7, 128), BF)], 0
    )


def unpack_row(pack, row):
    return (pack[:, :, 0, row] + pack[:, :, 1, row]).reshape(D)


REST_UNITS = (
    (3, 0, 0),
    (3, 1, 0),
    (3, 2, 0),
    (3, 3, 2),
    (2, 0, 0),
    (2, 1, 0),
    (2, 2, 1),
    (2, 3, 2),
    (1, 0, 0),
)
QKV_UNITS = ((0, 0, 0), (0, 1, 1), (0, 2, 2))
UNITS = REST_UNITS + QKV_UNITS
R1 = ((3, 2, 2, 32, D), (3, 4, 32, D), (3, 4, 2, 2, 32, 256))
R2 = ((3, 32, D), (3, 4, 32, 256), (3, 2, 2, 32, 256))


def count_of(order):
    return sum(1 for unit in UNITS if unit[2] == order)


class Reduce:
    def __init__(self, links, unit, n, grads, half, slots):
        self.tensor, self.unit, self.order = unit
        self.links, self.grad = links, grads[self.tensor]
        self.half = half.at[n]
        at = sum(1 for other in UNITS[:n] if other[2] == self.order)
        self.r1 = slots[self.order].at[at]
        self.r2 = slots[3 + self.order].at[at]
        self.r3 = slots[6].at[n]
        self.z_cols = self.cols_of(links.z)
        self.sent = []

    def cols_of(self, z):
        return pl.ds(pl.multiple_of(z * 256, 256), 256)

    def of_core(self, core):
        if self.tensor == 3:
            return self.grad.at[:, :, core, self.unit]
        return self.grad.at[:, :, core, :, :, pl.ds(self.unit * D, D)]

    def stage0(self):
        k = self.links
        self.swap = k.to(self.of_core(1 - k.core), self.half, k.peers("core")[0])
        self.sent.append(self.swap)

    def push(self, axis, src_of, slot):
        k = self.links
        here = {"x": k.x, "y": k.y, "z": k.z}[axis]
        self.coming = []
        for j, who in enumerate(k.peers(axis)):
            copy = k.to(src_of((here + j + 1) % 4), slot.at[j], who)
            self.coming.append(copy)
        self.sent += self.coming

    def add0(self, own):
        self.swap.wait_recv()

        @pl.loop(0, 16)
        def _(i):
            x, yh, yl = i // 4, (i // 2) % 2, i % 2
            total = self.half[x, yh, yl].astype(F32) + own(x, yh, yl).astype(F32)
            self.half[x, yh, yl] = total.astype(BF)

    def stage1(self):
        half = self.half
        if self.order == 0:
            self.push("x", lambda x: half.at[x], self.r1)
        elif self.order == 1:
            self.push("y", lambda y: half.at[:, y // 2, y % 2], self.r1)
        else:
            self.push("z", lambda z: half.at[:, :, :, :, self.cols_of(z)], self.r1)

    def sum1(self):
        k, half, got = self.links, self.half, self.r1
        wait_recv(self.coming)

        @pl.loop(0, 16 if self.order == 2 else 4)
        def _(i):
            if self.order == 0:
                spot, index = (k.x, i // 2, i % 2), (i // 2, i % 2)
            elif self.order == 1:
                spot, index = (i, k.yh, k.yl), (i,)
            else:
                index = (i // 4, (i // 2) % 2, i % 2)
                spot = index + (NONE, self.z_cols)
            total = half[spot].astype(F32)
            for j in range(3):
                total = total + got[(j,) + index].astype(F32)
            half[spot] = total.astype(BF)

    def stage2(self):
        k, half = self.links, self.half
        if self.order == 0:
            self.push("y", lambda y: half.at[k.x, y // 2, y % 2], self.r2)
        elif self.order == 1:
            self.push("z", lambda z: half.at[:, k.yh, k.yl, :, self.cols_of(z)], self.r2)
        else:
            self.push("x", lambda x: half.at[x, :, :, :, self.z_cols], self.r2)

    def sum2(self):
        k, half, got = self.links, self.half, self.r2
        wait_recv(self.coming)
        if self.order == 0:
            spot = (k.x, k.yh, k.yl)
            total = half[spot].astype(F32)
            for j in range(3):
                total = total + got[j].astype(F32)
            half[spot] = total.astype(BF)
            return

        @pl.loop(0, 4)
        def _(i):
            if self.order == 1:
                spot, index = (i, k.yh, k.yl, NONE, self.z_cols), (i,)
            else:
                spot, index = (k.x, i // 2, i % 2, NONE, self.z_cols), (i // 2, i % 2)
            total = half[spot].astype(F32)
            for j in range(3):
                total = total + got[(j,) + index].astype(F32)
            half[spot] = total.astype(BF)

    def stage3(self):
        k, half = self.links, self.half
        if self.order == 0:
            self.push("z", lambda z: half.at[k.x, k.yh, k.yl, :, self.cols_of(z)], self.r3)
        elif self.order == 1:
            self.push("x", lambda x: half.at[x, k.yh, k.yl, :, self.z_cols], self.r3)
        else:
            self.push("y", lambda y: half.at[k.x, y // 2, y % 2, :, self.z_cols], self.r3)

    def sum3(self, out_ref, position):
        k = self.links
        wait_recv(self.coming)
        total = self.half[k.x, k.yh, k.yl, :, self.z_cols].astype(F32)
        for j in range(3):
            total = total + self.r3[j].astype(F32)
        out_ref[k.me, :, 256 * position : 256 * (position + 1)] = total.astype(BF)

    def drain(self):
        wait_send(self.sent)

    def write(self, got, position, outs):
        out = outs[self.tensor]
        for t in range(8):
            piece = got[t, :, 256 * position : 256 * (position + 1)].astype(F32)
            if self.tensor == 3:
                out[self.unit, t // 4, :, 256 * (t % 4) : 256 * (t % 4 + 1)] = piece
            else:
                first = self.unit * D + 256 * (t % 4)
                out[t // 4, :, first : first + 256] = piece


def attend_back(kx, qx, vx, kt, do, delta, lse, dqt, h, j):
    keys = slice(BLK * j, BLK * (j + 1))
    down = lax.broadcasted_iota(jnp.int32, (BLK, BLK), 0)
    across = lax.broadcasted_iota(jnp.int32, (BLK, BLK), 1)
    grad_key = grad_value = None
    cuts = [BLK * j, BLK * (j + 1)] + list(range(BLK * (j + 1) + 768, LENGTH, 768))
    if cuts[-1] < LENGTH:
        cuts.append(LENGTH)
    for n in range(len(cuts) - 1):
        rows = slice(cuts[n], cuts[n + 1])
        queries = qx[h, rows, :]
        scores = dot_nt(kx[h, keys, :], queries)
        if n == 0:
            scores = jnp.where(down <= across, scores, -BIG)
        probs = jnp.exp(scores - lse[h, 1:2, rows])
        grad_out = do[rows, :]
        grad_probs = dot_nt(vx[h, keys, :], grad_out)
        grad_scores = (probs * (grad_probs - delta[h, 0:1, rows])).astype(BF)
        value_part = dot(probs.astype(BF), grad_out)
        key_part = dot(grad_scores, queries)
        grad_value = value_part if n == 0 else grad_value + value_part
        grad_key = key_part if n == 0 else grad_key + key_part
        query_part = dot(kt[h, :, keys], grad_scores)
        if j == 0:
            dqt[h, :, rows] = query_part
        else:
            dqt[h, :, rows] += query_part
    return grad_key, grad_value


def backward_kernel(
    g_out,
    g_fc1,
    g_fc2,
    grad_mixed,
    qkv,
    kx,
    qx,
    ot,
    lse,
    normed,
    wq_in,
    pack,
    tokens,
    grad_middle,
    small_in,
    o_qkv,
    o_out,
    o_fc1,
    o_fc2,
    o_small,
    input_grad,
    half,
    r1x,
    r1y,
    r1z,
    r2x,
    r2y,
    r2z,
    r3,
    own,
    g_qkv,
    w_slot,
    vx,
    kt,
    do,
    delta,
    dqt,
    g_send,
    g_merged,
    normed_t,
    f_rest,
    f_qkv,
    small,
    small_core,
    small_x,
    small_y,
    small_z,
    gn,
    send,
    recv,
):
    k = Links(send, recv)
    k.barrier()
    grads = (g_qkv, g_out, g_fc1, g_fc2)
    slots = (r1x, r1y, r1z, r2x, r2y, r2z, r3)
    units = [Reduce(k, unit, n, grads, half, slots) for n, unit in enumerate(UNITS)]
    rest, last = units[:9], units[9:]
    for u in rest:
        u.stage0()
    mine = pl.ds(pl.multiple_of(k.me * BLK, BLK), BLK)

    def heads_of(t):
        return pl.ds(pl.multiple_of(t * 128, 128), 128)

    kept_do = k.local(grad_mixed.at[:, heads_of(k.me)], do.at[mine])
    moved = [
        k.to(grad_mixed.at[:, heads_of(t)], do.at[mine], who) for t, who in k.rows_peers()
    ]
    loads = [k.local(u.of_core(k.core), own.at[n]) for n, u in enumerate(rest[:2])]

    lane = lax.broadcasted_iota(jnp.int32, (BLK, 128), 1)
    for t in range(8):
        rows = slice(BLK * t, BLK * (t + 1))
        value = qkv[2, rows, :]
        flipped = qkv[1, rows, :].astype(F32).T.astype(BF)
        for h in range(2):
            vx[h, rows, :] = jnp.where((lane // 64) == h, value.astype(F32), 0.0).astype(BF)
            kt[h, :, rows] = flipped[64 * h : 64 * (h + 1)]
    normed_t[...] = normed[...].astype(F32).T.astype(BF)
    kept_do.wait()
    wait_recv(moved)
    for t in range(8):
        rows = slice(BLK * t, BLK * (t + 1))
        flipped = do[rows, :].astype(F32).T
        for h in range(2):
            product = flipped[64 * h : 64 * (h + 1)] * ot[h, :, rows]
            delta[h, :, rows] = jnp.broadcast_to(
                jnp.sum(product, axis=0, keepdims=True), (8, BLK)
            )
    for n, u in enumerate(rest):
        loads[n].wait()
        u.add0(lambda x, yh, yl, n=n: own[n % 2, x, yh, yl])
        u.stage1()
        if n + 2 < len(rest):
            loads.append(k.local(rest[n + 2].of_core(k.core), own.at[n % 2]))

    back = []
    for t, who in k.rows_peers():
        i = k.used
        k.used += 1
        copy = pltpu.make_async_remote_copy(
            src_ref=g_send.at[:, t],
            dst_ref=g_merged.at[:, :, heads_of(k.me)],
            send_sem=k.send.at[i],
            recv_sem=k.recv.at[i],
            device_id=who,
        )
        back.append((t, copy))
    for j in range(8):
        found = [attend_back(kx, qx, vx, kt, do, delta, lse, dqt, h, j) for h in range(2)]
        left = (lane // 64) == 0
        for s, position in ((1, 0), (2, 1)):
            both = jnp.where(left, found[0][position], found[1][position])
            g_send[s, j] = both.astype(BF)
        rows = slice(BLK * j, BLK * (j + 1))
        query = jnp.concatenate([dqt[0, :, rows], dqt[1, :, rows]], axis=0).T * 0.125
        g_send[0, j] = query.astype(BF)
        if j in (3, 7):
            for t, copy in back:
                pl.when((t // 4) == (j // 4))(copy.start)
    kept_g = k.local(g_send.at[:, k.me], g_merged.at[:, :, heads_of(k.me)])

    def w_load(s):
        cols = pl.ds(s * D, D)
        return k.local(wq_in.at[:, :, :, :, :, cols], w_slot.at[s % 2])

    w_loads = [w_load(0), w_load(1)]
    for u in rest:
        u.sum1()
        u.stage2()
    kept_g.wait()
    for _, copy in back:
        copy.wait_recv()

    for s in range(3):

        @pl.loop(0, 4)
        def _(n):
            cols = pl.ds(pl.multiple_of(n * 256, 256), 256)
            block = dot(normed_t[...], g_merged[s, :, cols]).astype(BF)
            there = pl.ds(pl.multiple_of(s * D + n * 256, 256), 256)
            g_qkv[:, :, :, :, :, there] = block.reshape(4, 2, 2, 2, 32, 256)

        last[s].stage0()
    for u in rest:
        u.sum2()
        u.stage3()

    for s in range(3):
        w_loads[s].wait()
        for n in range(4):
            weight = w_slot[s % 2, n].reshape(256, D)
            part = dot_nt(g_merged[s], weight)
            cols = slice(256 * n, 256 * (n + 1))
            if s == 0:
                gn[:, cols] = part
            else:
                gn[:, cols] += part
        if s == 0:
            w_loads.append(w_load(2))
    for s, u in enumerate(last):
        cols = pl.ds(s * D, D)
        u.add0(lambda x, yh, yl, cols=cols: g_qkv[x, yh, k.core, yl, :, cols])
        u.stage1()

    values = tokens[...].astype(F32)
    center = values - jnp.mean(values, axis=1, keepdims=True)
    scale = lax.rsqrt(jnp.mean(center * center, axis=1, keepdims=True) + 1e-05)
    center = center * scale
    grad_normed = gn[...]
    by_gain = jnp.sum(grad_normed * center, axis=0, keepdims=True)
    by_bias = jnp.sum(grad_normed, axis=0, keepdims=True)
    inner = grad_normed * small_row(pack, 0)
    part = inner - jnp.mean(inner, axis=1, keepdims=True)
    part = part - center * jnp.mean(inner * center, axis=1, keepdims=True)
    input_grad[...] = grad_middle[...] + part * scale
    by_query = jnp.sum(g_merged[0].astype(F32), axis=0, keepdims=True)
    by_value = jnp.sum(g_merged[2].astype(F32), axis=0, keepdims=True)
    small[...] = small_in[...]
    for x in range(4):
        for yh in range(2):
            n = 2 * x + yh
            cols = slice(128 * n, 128 * (n + 1))
            small[x, yh, 0:1, :] = by_gain[:, cols]
            small[x, yh, 1:2, :] = by_bias[:, cols]
            source = by_query if x < 2 else by_value
            first = 256 * (n % 4)
            small[x, yh, 6:7, :] = source[:, first : first + 128]
            small[x, yh, 7:8, :] = source[:, first + 128 : first + 256]
    small_sent = [k.to(small, small_core, k.peers("core")[0])]

    for n, u in enumerate(rest):
        u.sum3(f_rest, n)
    gathered = [k.to(f_rest.at[k.me], f_rest.at[k.me], who) for _, who in k.rows_peers()]

    small_sent[0].wait()
    small[...] = small[...] + small_core[...]
    coming = [
        k.to(small.at[(k.x + j + 1) % 4], small_x.at[j], who)
        for j, who in enumerate(k.peers("x"))
    ]
    small_sent += coming
    for u in last:
        u.sum1()
        u.stage2()
    wait_recv(coming)
    small[k.x] = small[k.x] + small_x[0] + small_x[1] + small_x[2]
    coming = [
        k.to(small.at[k.x, ((k.y + j + 1) % 4) // 2], small_y.at[j], who)
        for j, who in enumerate(k.peers("y"))
    ]
    small_sent += coming
    for u in last:
        u.sum2()
        u.stage3()
    wait_recv(coming)
    small_z[3] = small[k.x, k.yh] + small_y[0] + small_y[1] + small_y[2]
    coming = [k.to(small_z.at[3], small_z.at[j], who) for j, who in enumerate(k.peers("z"))]
    small_sent += coming
    for n, u in enumerate(last):
        u.sum3(f_qkv, n)
    gathered_qkv = [k.to(f_qkv.at[k.me], f_qkv.at[k.me], who) for _, who in k.rows_peers()]
    outs = (o_qkv, o_out, o_fc1, o_fc2)
    wait_recv(gathered)
    for n, u in enumerate(rest):
        u.write(f_rest, n, outs)
    wait_recv(coming)
    o_small[...] = small_z[0] + small_z[1] + small_z[2] + small_z[3]
    wait_recv(gathered_qkv)
    for n, u in enumerate(last):
        u.write(f_qkv, n, outs)
    for u in units:
        u.drain()
    wait_send(moved + [copy for _, copy in back] + small_sent[1:] + gathered + gathered_qkv)


def backward_call(
    g_out, g_fc1, g_fc2, grad_mixed, qkv, kx, qx, ot, lse, normed, wq, pack, tokens, grad_middle, small
):
    hbm = pl.BlockSpec(memory_space=pl.ANY)
    vmem = pl.BlockSpec(memory_space=pltpu.VMEM)
    out = jax.ShapeDtypeStruct
    mem = pltpu.VMEM
    return pl.pallas_call(
        backward_kernel,
        name="backward",
        out_shape=(
            out((2, 32, 3 * D), F32),
            out((2, 32, D), F32),
            out((2, 32, 4 * D), F32),
            out((4, 2, 32, D), F32),
            out((16, 128), F32),
            out((BLK, D), F32),
        ),
        in_specs=[hbm, hbm, hbm, hbm, vmem, vmem, vmem, vmem, vmem, vmem, hbm, vmem, vmem, vmem, vmem],
        out_specs=(vmem,) * 6,
        scratch_shapes=[
            mem((12, 4, 2, 2, 32, D), BF),
            *[mem((count_of(order),) + R1[order], BF) for order in range(3)],
            *[mem((count_of(order),) + R2[order], BF) for order in range(3)],
            mem((12, 3, 32, 256), BF),
            mem((2, 4, 2, 2, 32, D), BF),
            mem(full_shape(3 * D), BF),
            mem((2,) + full_shape(D), BF),
            mem((2, LENGTH, 128), BF),
            mem((2, 64, LENGTH), BF),
            mem((LENGTH, 128), BF),
            mem((2, 8, LENGTH), F32),
            mem((2, 64, LENGTH), F32),
            mem((3, 8, BLK, 128), BF),
            mem((3, BLK, D), BF),
            mem((D, BLK), BF),
            mem((8, 32, 9 * 256), BF),
            mem((8, 32, 3 * 256), BF),
            mem((4, 2, 16, 128), F32),
            mem((4, 2, 16, 128), F32),
            mem((3, 2, 16, 128), F32),
            mem((3, 16, 128), F32),
            mem((4, 16, 128), F32),
            mem((BLK, D), F32),
            pltpu.SemaphoreType.DMA((190,)),
            pltpu.SemaphoreType.DMA((190,)),
        ],
        compiler_params=pltpu.CompilerParams(
            collective_id=1, has_side_effects=True, vmem_limit_bytes=63 * MIB
        ),
    )(
        g_out.reshape(full_shape(D)),
        g_fc1.reshape(full_shape(4 * D)),
        g_fc2.reshape(4, 2, 2, 4, 2, 32, D),
        grad_mixed,
        qkv,
        kx,
        qx,
        ot,
        lse,
        normed,
        wq,
        pack,
        tokens,
        grad_middle,
        small,
    )


def norm_parts(values):
    center = values - jnp.mean(values, axis=1, keepdims=True)
    scale = lax.rsqrt(jnp.mean(center * center, axis=1, keepdims=True) + 1e-05)
    return center * scale, scale


def norm_back(grad, normal, scale, gain):
    inner = grad * gain
    part = inner - jnp.mean(inner, axis=1, keepdims=True)
    part = part - normal * jnp.mean(inner * normal, axis=1, keepdims=True)
    by_gain = jnp.sum(grad * normal, axis=0, keepdims=True)
    return part * scale, by_gain, jnp.sum(grad, axis=0, keepdims=True)


def put_small(small, row, values):
    for n in range(8):
        small[n // 2, n % 2, row : row + 1, :] = values[:, 128 * n : 128 * (n + 1)]


def dense_kernel(
    tokens, cotangent, mixed, pack, wo, w1, w2,
    g_out, g_fc1, g_fc2, grad_mixed, grad_middle, output, small,
    gp, g2, gn, middle, bias_sums, w1s, w2s, wos, out_acc, normed, normed_t, sems, out_sems,
):
    def load(u, n):
        cols = pl.ds(pl.multiple_of(u * D + n * 512, 512), 512)
        return (
            pltpu.make_async_copy(w1.at[:, :, :, :, :, cols], w1s.at[n], sems.at[n]),
            pltpu.make_async_copy(w2.at[u, n], w2s.at[n], sems.at[2 + n]),
        )

    first = pltpu.make_async_copy(wo, wos, sems.at[4])
    first.start()
    for n in range(2):
        for copy in load(0, n):
            copy.start()
    small[...] = jnp.zeros((4, 2, 16, 128), F32)
    gain, bias = small_row(pack, 2), small_row(pack, 3)
    first.wait()

    @pl.loop(0, 4)
    def _(n):
        cols = pl.ds(pl.multiple_of(n * 256, 256), 256)
        weight = wos[:, :, :, :, :, cols].reshape(D, 256)
        middle[:, cols] = dot(mixed[...], weight) + tokens[:, cols].astype(F32)

    values = middle[...] + small_row(pack, 4)
    middle[...] = values
    normal, _ = norm_parts(values)
    second = normal * gain + bias
    normed[...] = second.astype(BF)
    normed_t[...] = second.T.astype(BF)
    out_acc[...] = values + small_row(pack, 5)
    gn[...] = jnp.zeros((BLK, D), F32)

    written = []
    for u in range(4):

        @pl.loop(0, 2)
        def _(n):
            for copy in load(u, n):
                copy.wait()
            up = w1s[n].reshape(D, 512)
            pieces = [pack[u, n, i // 2, 7 + i % 2 : 8 + i % 2, :].astype(F32) for i in range(4)]
            hidden = dot(normed[...], up) + jnp.concatenate(pieces, axis=1)
            square = hidden * hidden
            bent = jnp.tanh(0.7978845608028654 * hidden * (1.0 + 0.044715 * square))
            active = (0.5 * hidden * (1.0 + bent)).astype(BF)
            bend = 0.7978845608028654 * (1.0 + 0.134145 * square)
            slope = 0.5 * (1.0 + bent) + 0.5 * hidden * (1.0 - bent * bent) * bend
            back = w2s[n].reshape(512, D)
            out_acc[...] += dot(active, back)
            grad_hidden = (dot_nt(cotangent[...], back) * slope).astype(BF)
            g2[u, n] = dot_tn(active, cotangent[...]).astype(BF).reshape(2, 4, 2, 32, D)
            cols = pl.ds(pl.multiple_of(n * 512, 512), 512)
            block = dot(normed_t[...], grad_hidden).astype(BF)
            gp[u, :, :, :, :, :, cols] = block.reshape(4, 2, 2, 2, 32, 512)
            gn[...] += dot_nt(grad_hidden, up)
            sums = jnp.sum(grad_hidden.astype(F32), axis=0, keepdims=True)
            for i in range(4):
                bias_sums[u, n, i : i + 1, :] = sums[:, 128 * i : 128 * (i + 1)]
            if u < 3:
                for copy in load(u + 1, n):
                    copy.start()

        there = g_fc1.at[:, :, :, :, :, pl.ds(u * D, D)]
        written.append(pltpu.make_async_copy(gp.at[u], there, out_sems.at[u]))
        written.append(pltpu.make_async_copy(g2.at[u], g_fc2.at[u], out_sems.at[4 + u]))
        written[-2].start()
        written[-1].start()

    output[...] = out_acc[...].astype(BF)
    values, scale = norm_parts(middle[...])
    cot = cotangent[...].astype(F32)
    part, by_gain, by_bias = norm_back(gn[...], values, scale, small_row(pack, 2))
    total = cot + part
    grad_middle[...] = total
    branch = total.astype(BF)

    @pl.loop(0, 4)
    def _(n):
        weight = wos[n].reshape(256, D)
        cols = pl.ds(pl.multiple_of(n * 256, 256), 256)
        grad_mixed[:, cols] = dot_nt(branch, weight).astype(BF)

    put_small(small, 2, by_gain)
    put_small(small, 3, by_bias)
    put_small(small, 4, jnp.sum(branch.astype(F32), axis=0, keepdims=True))
    put_small(small, 5, jnp.sum(cot, axis=0, keepdims=True))
    for x in range(4):
        for yh in range(2):
            small[x, yh, 8:12, :] = bias_sums[x, yh, 0:4, :]
    normed[...] = branch
    normed_t[...] = mixed[...].astype(F32).T.astype(BF)

    @pl.loop(0, 4)
    def _(n):
        cols = pl.ds(pl.multiple_of(n * 256, 256), 256)
        block = dot(normed_t[...], normed[:, cols]).astype(BF)
        gp[4, :, :, :, :, :, cols] = block.reshape(4, 2, 2, 2, 32, 256)

    written.append(pltpu.make_async_copy(gp.at[4], g_out, out_sems.at[8]))
    written[-1].start()
    for copy in written:
        copy.wait()


def dense_call(*args):
    hbm = pl.BlockSpec(memory_space=pl.ANY)
    vmem = pl.BlockSpec(memory_space=pltpu.VMEM)
    out = jax.ShapeDtypeStruct
    mem = pltpu.VMEM
    return pl.pallas_call(
        dense_kernel,
        name="dense",
        out_shape=(
            out(full_shape(D), BF),
            out(full_shape(4 * D), BF),
            out((4, 2, 2, 4, 2, 32, D), BF),
            out((BLK, D), BF),
            out((BLK, D), F32),
            out((BLK, D), BF),
            out((4, 2, 16, 128), F32),
        ),
        in_specs=[vmem] * 4 + [hbm] * 3,
        out_specs=(hbm, hbm, hbm, vmem, vmem, vmem, vmem),
        scratch_shapes=[
            mem((5,) + full_shape(D), BF),
            mem((4, 2, 2, 4, 2, 32, D), BF),
            mem((BLK, D), F32),
            mem((BLK, D), F32),
            mem((4, 2, 8, 128), F32),
            mem((2, 4, 2, 2, 2, 32, 512), BF),
            mem((2, 2, 4, 2, 32, D), BF),
            mem(full_shape(D), BF),
            mem((BLK, D), F32),
            mem((BLK, D), BF),
            mem((D, BLK), BF),
            pltpu.SemaphoreType.DMA((5,)),
            pltpu.SemaphoreType.DMA((9,)),
        ],
        compiler_params=pltpu.CompilerParams(vmem_limit_bytes=62 * MIB),
    )(*args)


def local(self, src, dst):
        i = self.used
        self.used += 1
        copy = pltpu.make_async_copy(src, dst, self.send.at[i])
        copy.start()
        return copy


def wait_recv(copies):
    for copy in copies:
        copy.wait_recv()


def wait_send(copies):
    for copy in copies:
        copy.wait_send()


class Gather:
    def __init__(self, links, full, shard, seg):
        tensor, self.order, first, count = seg
        self.links, self.full, self.shard = links, full, shard
        self.blocked = tensor == 3
        if self.blocked:
            self.units = (pl.ds(first, count),)
            self.all_cols = pl.ds(0, D)
            width = D // 4
            self.z_cols = pl.ds(pl.multiple_of(links.z * width, width), width)
        else:
            self.units = ()
            self.all_cols = pl.ds(first * D, count * D)
            width = count * D // 4
            self.z_cols = pl.ds(pl.multiple_of(first * D + links.z * width, width), width)
        self.sent = []

    def view(self, x, yh, yl, cols):
        return self.full.at[(x, yh, self.links.core) + self.units + (yl, NONE, cols)]

    def own(self, cols):
        return self.shard.at[self.units + (self.links.yl, NONE, cols)]

    def push(self, src, dst, axis):
        now = [self.links.to(src, dst, who) for who in self.links.peers(axis)]
        self.sent += now
        return now

    def stage1(self):
        k = self.links
        cols = self.all_cols if self.order == 0 else self.z_cols
        dst = self.view(k.x, k.yh, k.yl, cols)
        self.kept = k.local(self.own(cols), dst)
        self.first = self.push(self.own(cols), dst, "x" if self.order == 1 else "y")

    def stage2(self):
        k = self.links
        self.kept.wait()
        wait_recv(self.first)
        if self.order == 0:
            part = self.view(k.x, NONE, NONE, self.all_cols)
            self.last = self.push(part, part, "x")
        elif self.order == 1:
            part = self.view(NONE, k.yh, k.yl, self.z_cols)
            self.second = self.push(part, part, "z")
        else:
            part = self.view(k.x, NONE, NONE, self.z_cols)
            self.second = self.push(part, part, "x")

    def stage3(self):
        k = self.links
        if self.order == 0:
            return
        wait_recv(self.second)
        if self.order == 1:
            part = self.view(NONE, k.yh, k.yl, self.all_cols)
            self.last = self.push(part, part, "y")
        else:
            part = self.view(NONE, NONE, NONE, self.z_cols)
            self.last = self.push(part, part, "z")

    def cross(self):
        wait_recv(self.last)
        part = self.view(NONE, NONE, NONE, self.all_cols)
        self.swapped = self.push(part, part, "core")

    def finish(self):
        wait_recv(self.swapped)

    def drain(self):
        wait_send(self.sent)


def small_row(pack, row):
    pieces = []
    for x in range(4):
        for yh in range(2):
            pieces.append(
                pack[x, yh, 0, row : row + 1, :].astype(F32)
                + pack[x, yh, 1, row : row + 1, :].astype(F32)
            )
    return jnp.concatenate(pieces, axis=1)


def dot_nt(a, b):
    return lax.dot_general(a, b, (((1,), (1,)), ((), ())), preferred_element_type=F32)


def dot_tn(a, b):
    return lax.dot_general(a, b, (((0,), (0,)), ((), ())), preferred_element_type=F32)


def dot(a, b):
    return jnp.dot(a, b, preferred_element_type=F32)


def slope_of(links, h, shape):
    power = (links.me * 2 + h + 1).astype(F32) * -0.5
    return jnp.exp2(jnp.full(shape, power, F32)) * (4.0 / LENGTH)


def extend(links, seg_ref, qkv_ref, kx_ref, qx_ref, h, t):
    rows = pl.ds(t * BLK, BLK)
    seg = jnp.broadcast_to(seg_ref[t, 0:1, :].astype(F32), (128, BLK)).T
    lane = lax.broadcasted_iota(jnp.int32, (BLK, 128), 1)
    mine = (lane // 64) == h
    e = lane - 64 * (1 - h)
    where = lax.broadcasted_iota(jnp.int32, (BLK, 128), 0) + t * BLK
    bias = slope_of(links, h, (BLK, 128)) * where.astype(F32)
    high = bias.astype(BF).astype(F32)
    mid = (bias - high).astype(BF).astype(F32)
    low = bias - high - mid
    doc = (e - 3).astype(F32)
    is_doc = (e >= 3) & (e <= 6)
    same = seg == doc
    key_extra = jnp.where(is_doc & jnp.logical_not(same), 1.0, 0.0)
    key_extra = jnp.where(e == 0, high, jnp.where(e == 1, mid, jnp.where(e == 2, low, key_extra)))
    query_extra = jnp.where(is_doc & same, -BIG, 0.0)
    query_extra = jnp.where((e >= 0) & (e <= 2), 1.0, query_extra)
    query = qkv_ref[0, rows, :].astype(F32) * 0.125
    key = qkv_ref[1, rows, :].astype(F32)
    kx_ref[h, rows, :] = jnp.where(mine, key, key_extra).astype(BF)
    qx_ref[h, rows, :] = jnp.where(mine, query, query_extra).astype(BF)


def attend(links, kx_ref, qx_ref, vt_ref, ot_ref, lse_ref, h, i):
    keys = BLK * (i + 1)
    qb = qx_ref[h, BLK * i : keys, :]
    down = lax.broadcasted_iota(jnp.int32, (BLK, BLK), 0)
    across = lax.broadcasted_iota(jnp.int32, (BLK, BLK), 1)
    edge = jnp.where(down <= across, dot_nt(kx_ref[h, BLK * i : keys, :], qb), -BIG)
    top = jnp.max(edge, axis=0, keepdims=True)
    if i:
        past = dot_nt(kx_ref[h, 0 : BLK * i, :], qb)
        top = jnp.maximum(top, jnp.max(past, axis=0, keepdims=True))
    edge = jnp.exp(edge - top)
    total = jnp.sum(edge, axis=0, keepdims=True)
    out = dot(vt_ref[h, :, BLK * i : keys], edge.astype(BF))
    if i:
        past = jnp.exp(past - top)
        total = total + jnp.sum(past, axis=0, keepdims=True)
        out = out + dot(vt_ref[h, :, 0 : BLK * i], past.astype(BF))
    ot_ref[h, :, BLK * i : keys] = out / total
    where = (lax.broadcasted_iota(jnp.int32, (1, BLK), 1) + BLK * i).astype(F32)
    shifted = top + jnp.log(total)
    final = shifted - slope_of(links, h, (1, BLK)) * where
    first = lax.broadcasted_iota(jnp.int32, (8, BLK), 0) == 0
    lse_ref[h, :, BLK * i : keys] = jnp.where(first, final, shifted)


def forward_kernel(
    tokens,
    seg,
    small,
    wq_in,
    wo_in,
    w1_in,
    w2_in,
    wq_out,
    wo,
    w1,
    w2,
    pack_out,
    normed_out,
    qkv_out,
    kx,
    qx,
    ot,
    lse,
    mixed,
    lse_all,
    wq,
    pack,
    seg_all,
    row,
    merged,
    qkv,
    vt,
    mixed_send,
    send,
    recv,
):
    k = Links(send, recv)
    k.barrier()
    sent, kept = [], []

    kept_small = k.local(small, pack.at[k.x, k.yh, k.core])
    small_x = [k.to(small, pack.at[k.x, k.yh, k.core], who) for who in k.peers("x")]
    fulls, shards = (wq, wo, w1, w2), (wq_in, wo_in, w1_in, w2_in)
    first = [Gather(k, fulls[s[0]], shards[s[0]], s) for s in QKV_SEGS]
    rest = [Gather(k, fulls[s[0]], shards[s[0]], s) for s in REST_SEGS]
    for g in first:
        g.stage1()
    kept_seg = k.local(seg, seg_all.at[k.me])
    segs = [k.to(seg, seg_all.at[k.me], who) for _, who in k.rows_peers()]
    for g in first:
        g.stage2()
    kept_small.wait()
    wait_recv(small_x)
    part = pack.at[:, k.yh, k.core]
    small_y = [k.to(part, part, k.peers("y")[1])]
    for g in rest:
        g.stage1()
    for g in first:
        g.stage3()
    wait_recv(small_y)
    part = pack.at[:, :, k.core]
    small_c = [k.to(part, part, k.peers("core")[0])]

    for g in rest:
        g.stage2()
    values = tokens[...].astype(F32)
    center = values - jnp.mean(values, axis=1, keepdims=True)
    center = center * lax.rsqrt(jnp.mean(center * center, axis=1, keepdims=True) + 1e-05)
    wait_recv(small_c)
    normed_out[...] = (center * small_row(pack, 0) + small_row(pack, 1)).astype(BF)
    pack_out[...] = pack[...]
    pieces = []
    for f in range(16):
        pieces.append(pack[f // 4, (f // 2) % 2, f % 2, 6:7, :].astype(F32))
    row[...] = jnp.broadcast_to(
        jnp.concatenate(pieces[:8] + [jnp.zeros((1, D), F32)] + pieces[8:], axis=1), (8, 3 * D)
    )
    for g in first:
        g.cross()
    for g in first:
        g.finish()
    kept.append(k.local(wq, wq_out))

    @pl.loop(0, 12)
    def _(n):
        cols = pl.ds(pl.multiple_of(n * 256, 256), 256)
        weight = wq[:, :, :, :, :, cols].reshape(D, 256)
        block = (dot(normed_out[...], weight) + row[0:1, cols]).astype(BF)
        merged[n // 4, 2 * (n % 4)] = block[:, :128]
        merged[n // 4, 2 * (n % 4) + 1] = block[:, 128:]

    mine = pl.ds(pl.multiple_of(k.me * BLK, BLK), BLK)
    kept_qkv = k.local(merged.at[:, k.me], qkv.at[:, mine])
    moved = [k.to(merged.at[:, t], qkv.at[:, mine], who) for t, who in k.rows_peers()]
    for g in rest:
        g.stage3()
    kept_seg.wait()
    wait_recv(segs)
    kept_qkv.wait()
    wait_recv(moved)
    kept.append(k.local(qkv, qkv_out))

    @pl.loop(0, 8)
    def _(t):
        for h in range(2):
            extend(k, seg_all, qkv, kx, qx, h, t)

    for t in range(8):
        flipped = qkv[2, BLK * t : BLK * (t + 1), :].astype(F32).T.astype(BF)
        for h in range(2):
            vt[h, :, BLK * t : BLK * (t + 1)] = flipped[64 * h : 64 * (h + 1)]

    for i in range(8):

        @pl.loop(0, 2)
        def _(h):
            attend(k, kx, qx, vt, ot, lse, h, i)
        if i == 5:
            for g in rest:
                if g.order == 0:
                    g.cross()

        both = jnp.concatenate(
            [ot[0, :, BLK * i : BLK * (i + 1)], ot[1, :, BLK * i : BLK * (i + 1)]], axis=0
        )
        mixed_send[i] = both.T.astype(BF)

    cols = pl.ds(pl.multiple_of(k.me * 128, 128), 128)
    kept.append(k.local(mixed_send.at[k.me], mixed.at[:, cols]))
    back = [k.to(mixed_send.at[t], mixed.at[:, cols], who) for t, who in k.rows_peers()]
    part = pl.ds(pl.multiple_of(k.me * BLK, BLK), BLK)
    kept.append(k.local(lse.at[:, :, part], lse_all.at[k.me]))
    for t, who in k.rows_peers():
        part = pl.ds(pl.multiple_of(t * BLK, BLK), BLK)
        back.append(k.to(lse.at[:, :, part], lse_all.at[k.me], who))
    for g in rest:
        if g.order != 0:
            g.cross()
    wait_recv(back)
    for g in rest:
        g.finish()
    for copy in kept:
        copy.wait()
    for g in first + rest:
        g.drain()
    wait_send(small_x + small_y + small_c + segs + moved + back)


def full_shape(cols):
    return (4, 2, 2, 2, 32, cols)


def forward_call(tokens, seg, small, wq, wo, w1, w2):
    hbm = pl.BlockSpec(memory_space=pl.ANY)
    vmem = pl.BlockSpec(memory_space=pltpu.VMEM)
    out = jax.ShapeDtypeStruct
    return pl.pallas_call(
        forward_kernel,
        name="forward",
        out_shape=(
            out(full_shape(3 * D), BF),
            out(full_shape(D), BF),
            out(full_shape(4 * D), BF),
            out((4, 2, 2, 4, 2, 32, D), BF),
            out((4, 2, 2, 16, 128), BF),
            out((BLK, D), BF),
            out((3, LENGTH, 128), BF),
            out((2, LENGTH, 128), BF),
            out((2, LENGTH, 128), BF),
            out((2, 64, LENGTH), F32),
            out((2, 8, LENGTH), F32),
            out((BLK, D), BF),
            out((8, 2, 8, BLK), F32),
        ),
        in_specs=[vmem, vmem, vmem, hbm, hbm, hbm, hbm],
        out_specs=(hbm, hbm, hbm, hbm, vmem, vmem, hbm, vmem, vmem, vmem, vmem, hbm, hbm),
        scratch_shapes=[
            pltpu.VMEM(full_shape(3 * D), BF),
            pltpu.VMEM((4, 2, 2, 16, 128), BF),
            pltpu.VMEM((8, 8, BLK), jnp.int32),
            pltpu.VMEM((8, 3 * D), F32),
            pltpu.VMEM((3, 8, BLK, 128), BF),
            pltpu.VMEM((3, LENGTH, 128), BF),
            pltpu.VMEM((2, 64, LENGTH), BF),
            pltpu.VMEM((8, BLK, 128), BF),
            pltpu.SemaphoreType.DMA((170,)),
            pltpu.SemaphoreType.DMA((170,)),
        ],
        compiler_params=pltpu.CompilerParams(
            collective_id=0, has_side_effects=True, vmem_limit_bytes=62 * MIB
        ),
    )(
        tokens,
        seg,
        small,
        wq.reshape(2, 32, 3 * D),
        wo.reshape(2, 32, D),
        w1.reshape(2, 32, 4 * D),
        w2.reshape(4, 2, 32, D),
    )


def small_pack(ln1_gain, ln1_bias, ln2_gain, ln2_bias, out_bias, fc2_bias, qkv_bias, fc1_bias):
    core = lax.axis_index("fsdp") % 2
    six = jnp.stack([ln1_gain, ln1_bias, ln2_gain, ln2_bias, out_bias, fc2_bias])
    none = jnp.zeros_like(six)
    halves = jnp.where(
        core == 0, jnp.concatenate([six, none], 1), jnp.concatenate([none, six], 1)
    )
    return jnp.concatenate(
        [halves, qkv_bias[None], fc1_bias.reshape(2, 128), jnp.zeros((7, 128), BF)], 0
    )


def unpack_row(pack, row):
    return (pack[:, :, 0, row] + pack[:, :, 1, row]).reshape(D)


REST_UNITS = (
    (3, 0, 0),
    (3, 1, 1),
    (3, 2, 2),
    (3, 3, 2),
    (2, 0, 0),
    (2, 1, 0),
    (2, 2, 1),
    (2, 3, 2),
    (1, 0, 0),
)
QKV_UNITS = ((0, 0, 0), (0, 1, 1), (0, 2, 2))
UNITS = REST_UNITS + QKV_UNITS
R1 = ((3, 2, 2, 32, D), (3, 4, 32, D), (3, 4, 2, 2, 32, 256))
R2 = ((3, 32, D), (3, 4, 32, 256), (3, 2, 2, 32, 256))


def count_of(order):
    return sum(1 for unit in UNITS if unit[2] == order)


class Reduce:
    def __init__(self, links, unit, n, grads, half, slots):
        self.tensor, self.unit, self.order = unit
        self.links, self.grad = links, grads[self.tensor]
        self.half = half.at[n]
        at = sum(1 for other in UNITS[:n] if other[2] == self.order)
        self.r1 = slots[self.order].at[at]
        self.r2 = slots[3 + self.order].at[at]
        self.r3 = slots[6].at[n]
        self.z_cols = self.cols_of(links.z)
        self.sent = []

    def cols_of(self, z):
        return pl.ds(pl.multiple_of(z * 256, 256), 256)

    def of_core(self, core):
        if self.tensor == 3:
            return self.grad.at[:, :, core, self.unit]
        return self.grad.at[:, :, core, :, :, pl.ds(self.unit * D, D)]

    def stage0(self):
        k = self.links
        self.swap = k.to(self.of_core(1 - k.core), self.half, k.peers("core")[0])
        self.sent.append(self.swap)

    def push(self, axis, src_of, slot):
        k = self.links
        here = {"x": k.x, "y": k.y, "z": k.z}[axis]
        self.coming = []
        for j, who in enumerate(k.peers(axis)):
            copy = k.to(src_of((here + j + 1) % 4), slot.at[j], who)
            self.coming.append(copy)
        self.sent += self.coming

    def add0(self, own):
        self.swap.wait_recv()

        @pl.loop(0, 16)
        def _(i):
            x, yh, yl = i // 4, (i // 2) % 2, i % 2
            total = self.half[x, yh, yl].astype(F32) + own(x, yh, yl).astype(F32)
            self.half[x, yh, yl] = total.astype(BF)

    def stage1(self):
        half = self.half
        if self.order == 0:
            self.push("x", lambda x: half.at[x], self.r1)
        elif self.order == 1:
            self.push("y", lambda y: half.at[:, y // 2, y % 2], self.r1)
        else:
            self.push("z", lambda z: half.at[:, :, :, :, self.cols_of(z)], self.r1)

    def sum1(self):
        k, half, got = self.links, self.half, self.r1
        wait_recv(self.coming)

        @pl.loop(0, 16 if self.order == 2 else 4)
        def _(i):
            if self.order == 0:
                spot, index = (k.x, i // 2, i % 2), (i // 2, i % 2)
            elif self.order == 1:
                spot, index = (i, k.yh, k.yl), (i,)
            else:
                index = (i // 4, (i // 2) % 2, i % 2)
                spot = index + (NONE, self.z_cols)
            total = half[spot].astype(F32)
            for j in range(3):
                total = total + got[(j,) + index].astype(F32)
            half[spot] = total.astype(BF)

    def stage2(self):
        k, half = self.links, self.half
        if self.order == 0:
            self.push("y", lambda y: half.at[k.x, y // 2, y % 2], self.r2)
        elif self.order == 1:
            self.push("z", lambda z: half.at[:, k.yh, k.yl, :, self.cols_of(z)], self.r2)
        else:
            self.push("x", lambda x: half.at[x, :, :, :, self.z_cols], self.r2)

    def sum2(self):
        k, half, got = self.links, self.half, self.r2
        wait_recv(self.coming)
        if self.order == 0:
            spot = (k.x, k.yh, k.yl)
            total = half[spot].astype(F32)
            for j in range(3):
                total = total + got[j].astype(F32)
            half[spot] = total.astype(BF)
            return

        @pl.loop(0, 4)
        def _(i):
            if self.order == 1:
                spot, index = (i, k.yh, k.yl, NONE, self.z_cols), (i,)
            else:
                spot, index = (k.x, i // 2, i % 2, NONE, self.z_cols), (i // 2, i % 2)
            total = half[spot].astype(F32)
            for j in range(3):
                total = total + got[(j,) + index].astype(F32)
            half[spot] = total.astype(BF)

    def stage3(self):
        k, half = self.links, self.half
        if self.order == 0:
            self.push("z", lambda z: half.at[k.x, k.yh, k.yl, :, self.cols_of(z)], self.r3)
        elif self.order == 1:
            self.push("x", lambda x: half.at[x, k.yh, k.yl, :, self.z_cols], self.r3)
        else:
            self.push("y", lambda y: half.at[k.x, y // 2, y % 2, :, self.z_cols], self.r3)

    def sum3(self, out_ref, position):
        k = self.links
        wait_recv(self.coming)
        total = self.half[k.x, k.yh, k.yl, :, self.z_cols].astype(F32)
        for j in range(3):
            total = total + self.r3[j].astype(F32)
        out_ref[k.me, :, 256 * position : 256 * (position + 1)] = total.astype(BF)

    def drain(self):
        wait_send(self.sent)

    def write(self, got, position, outs):
        out = outs[self.tensor]
        for t in range(8):
            piece = got[t, :, 256 * position : 256 * (position + 1)].astype(F32)
            if self.tensor == 3:
                out[self.unit, t // 4, :, 256 * (t % 4) : 256 * (t % 4 + 1)] = piece
            else:
                first = self.unit * D + 256 * (t % 4)
                out[t // 4, :, first : first + 256] = piece


def attend_back(kx, qx, vx, kt, do, delta, lse, dqt, h, j):
    keys = slice(BLK * j, BLK * (j + 1))
    down = lax.broadcasted_iota(jnp.int32, (BLK, BLK), 0)
    across = lax.broadcasted_iota(jnp.int32, (BLK, BLK), 1)
    grad_key = grad_value = None
    cuts = [BLK * j, BLK * (j + 1)] + list(range(BLK * (j + 1) + 768, LENGTH, 768))
    if cuts[-1] < LENGTH:
        cuts.append(LENGTH)
    for n in range(len(cuts) - 1):
        rows = slice(cuts[n], cuts[n + 1])
        queries = qx[h, rows, :]
        scores = dot_nt(kx[h, keys, :], queries)
        if n == 0:
            scores = jnp.where(down <= across, scores, -BIG)
        probs = jnp.exp(scores - lse[h, 1:2, rows])
        grad_out = do[rows, :]
        grad_probs = dot_nt(vx[h, keys, :], grad_out)
        grad_scores = (probs * (grad_probs - delta[h, 0:1, rows])).astype(BF)
        value_part = dot(probs.astype(BF), grad_out)
        key_part = dot(grad_scores, queries)
        grad_value = value_part if n == 0 else grad_value + value_part
        grad_key = key_part if n == 0 else grad_key + key_part
        query_part = dot(kt[h, :, keys], grad_scores)
        if j == 0:
            dqt[h, :, rows] = query_part
        else:
            dqt[h, :, rows] += query_part
    return grad_key, grad_value


def backward_kernel(
    g_out,
    g_fc1,
    g_fc2,
    grad_mixed,
    qkv,
    kx,
    qx,
    ot,
    lse,
    normed,
    wq_in,
    pack,
    tokens,
    grad_middle,
    small_in,
    o_qkv,
    o_out,
    o_fc1,
    o_fc2,
    o_small,
    input_grad,
    half,
    r1x,
    r1y,
    r1z,
    r2x,
    r2y,
    r2z,
    r3,
    own,
    g_qkv,
    w_slot,
    vx,
    kt,
    do,
    delta,
    dqt,
    g_send,
    g_merged,
    normed_t,
    f_rest,
    f_qkv,
    small,
    small_core,
    small_x,
    small_y,
    small_z,
    gn,
    send,
    recv,
):
    k = Links(send, recv)
    k.barrier()
    grads = (g_qkv, g_out, g_fc1, g_fc2)
    slots = (r1x, r1y, r1z, r2x, r2y, r2z, r3)
    units = [Reduce(k, unit, n, grads, half, slots) for n, unit in enumerate(UNITS)]
    rest, last = units[:9], units[9:]
    for u in rest:
        u.stage0()
    mine = pl.ds(pl.multiple_of(k.me * BLK, BLK), BLK)

    def heads_of(t):
        return pl.ds(pl.multiple_of(t * 128, 128), 128)

    kept_do = k.local(grad_mixed.at[:, heads_of(k.me)], do.at[mine])
    moved = [
        k.to(grad_mixed.at[:, heads_of(t)], do.at[mine], who) for t, who in k.rows_peers()
    ]
    loads = [k.local(u.of_core(k.core), own.at[n]) for n, u in enumerate(rest[:2])]

    lane = lax.broadcasted_iota(jnp.int32, (BLK, 128), 1)
    for t in range(8):
        rows = slice(BLK * t, BLK * (t + 1))
        value = qkv[2, rows, :]
        flipped = qkv[1, rows, :].astype(F32).T.astype(BF)
        for h in range(2):
            vx[h, rows, :] = jnp.where((lane // 64) == h, value.astype(F32), 0.0).astype(BF)
            kt[h, :, rows] = flipped[64 * h : 64 * (h + 1)]
    normed_t[...] = normed[...].astype(F32).T.astype(BF)
    kept_do.wait()
    wait_recv(moved)
    for t in range(8):
        rows = slice(BLK * t, BLK * (t + 1))
        flipped = do[rows, :].astype(F32).T
        for h in range(2):
            product = flipped[64 * h : 64 * (h + 1)] * ot[h, :, rows]
            delta[h, :, rows] = jnp.broadcast_to(
                jnp.sum(product, axis=0, keepdims=True), (8, BLK)
            )
    for n, u in enumerate(rest):
        loads[n].wait()
        u.add0(lambda x, yh, yl, n=n: own[n % 2, x, yh, yl])
        u.stage1()
        if n + 2 < len(rest):
            loads.append(k.local(rest[n + 2].of_core(k.core), own.at[n % 2]))

    back = []
    for t, who in k.rows_peers():
        i = k.used
        k.used += 1
        copy = pltpu.make_async_remote_copy(
            src_ref=g_send.at[:, t],
            dst_ref=g_merged.at[:, :, heads_of(k.me)],
            send_sem=k.send.at[i],
            recv_sem=k.recv.at[i],
            device_id=who,
        )
        back.append((t, copy))
    for j in range(8):
        found = [attend_back(kx, qx, vx, kt, do, delta, lse, dqt, h, j) for h in range(2)]
        left = (lane // 64) == 0
        for s, position in ((1, 0), (2, 1)):
            both = jnp.where(left, found[0][position], found[1][position])
            g_send[s, j] = both.astype(BF)
        rows = slice(BLK * j, BLK * (j + 1))
        query = jnp.concatenate([dqt[0, :, rows], dqt[1, :, rows]], axis=0).T * 0.125
        g_send[0, j] = query.astype(BF)
        if j in (3, 7):
            for t, copy in back:
                pl.when((t // 4) == (j // 4))(copy.start)
    kept_g = k.local(g_send.at[:, k.me], g_merged.at[:, :, heads_of(k.me)])

    def w_load(s):
        cols = pl.ds(s * D, D)
        return k.local(wq_in.at[:, :, :, :, :, cols], w_slot.at[s % 2])

    w_loads = [w_load(0), w_load(1)]
    for u in rest:
        u.sum1()
        u.stage2()
    kept_g.wait()
    for _, copy in back:
        copy.wait_recv()

    for s in range(3):

        @pl.loop(0, 4)
        def _(n):
            cols = pl.ds(pl.multiple_of(n * 256, 256), 256)
            block = dot(normed_t[...], g_merged[s, :, cols]).astype(BF)
            there = pl.ds(pl.multiple_of(s * D + n * 256, 256), 256)
            g_qkv[:, :, :, :, :, there] = block.reshape(4, 2, 2, 2, 32, 256)

        last[s].stage0()
    for u in rest:
        u.sum2()
        u.stage3()

    for s in range(3):
        w_loads[s].wait()
        for n in range(4):
            weight = w_slot[s % 2, n].reshape(256, D)
            part = dot_nt(g_merged[s], weight)
            cols = slice(256 * n, 256 * (n + 1))
            if s == 0:
                gn[:, cols] = part
            else:
                gn[:, cols] += part
        if s == 0:
            w_loads.append(w_load(2))
    for s, u in enumerate(last):
        cols = pl.ds(s * D, D)
        u.add0(lambda x, yh, yl, cols=cols: g_qkv[x, yh, k.core, yl, :, cols])
        u.stage1()

    values = tokens[...].astype(F32)
    center = values - jnp.mean(values, axis=1, keepdims=True)
    scale = lax.rsqrt(jnp.mean(center * center, axis=1, keepdims=True) + 1e-05)
    center = center * scale
    grad_normed = gn[...]
    by_gain = jnp.sum(grad_normed * center, axis=0, keepdims=True)
    by_bias = jnp.sum(grad_normed, axis=0, keepdims=True)
    inner = grad_normed * small_row(pack, 0)
    part = inner - jnp.mean(inner, axis=1, keepdims=True)
    part = part - center * jnp.mean(inner * center, axis=1, keepdims=True)
    input_grad[...] = grad_middle[...] + part * scale
    by_query = jnp.sum(g_merged[0].astype(F32), axis=0, keepdims=True)
    by_value = jnp.sum(g_merged[2].astype(F32), axis=0, keepdims=True)
    small[...] = small_in[...]
    for x in range(4):
        for yh in range(2):
            n = 2 * x + yh
            cols = slice(128 * n, 128 * (n + 1))
            small[x, yh, 0:1, :] = by_gain[:, cols]
            small[x, yh, 1:2, :] = by_bias[:, cols]
            source = by_query if x < 2 else by_value
            first = 256 * (n % 4)
            small[x, yh, 6:7, :] = source[:, first : first + 128]
            small[x, yh, 7:8, :] = source[:, first + 128 : first + 256]
    small_sent = [k.to(small, small_core, k.peers("core")[0])]

    for n, u in enumerate(rest):
        u.sum3(f_rest, n)
    gathered = [k.to(f_rest.at[k.me], f_rest.at[k.me], who) for _, who in k.rows_peers()]

    small_sent[0].wait()
    small[...] = small[...] + small_core[...]
    coming = [
        k.to(small.at[(k.x + j + 1) % 4], small_x.at[j], who)
        for j, who in enumerate(k.peers("x"))
    ]
    small_sent += coming
    for u in last:
        u.sum1()
        u.stage2()
    wait_recv(coming)
    small[k.x] = small[k.x] + small_x[0] + small_x[1] + small_x[2]
    coming = [
        k.to(small.at[k.x, ((k.y + j + 1) % 4) // 2], small_y.at[j], who)
        for j, who in enumerate(k.peers("y"))
    ]
    small_sent += coming
    for u in last:
        u.sum2()
        u.stage3()
    wait_recv(coming)
    small_z[3] = small[k.x, k.yh] + small_y[0] + small_y[1] + small_y[2]
    coming = [k.to(small_z.at[3], small_z.at[j], who) for j, who in enumerate(k.peers("z"))]
    small_sent += coming
    for n, u in enumerate(last):
        u.sum3(f_qkv, n)
    gathered_qkv = [k.to(f_qkv.at[k.me], f_qkv.at[k.me], who) for _, who in k.rows_peers()]
    outs = (o_qkv, o_out, o_fc1, o_fc2)
    wait_recv(gathered)
    for n, u in enumerate(rest):
        u.write(f_rest, n, outs)
    wait_recv(coming)
    o_small[...] = small_z[0] + small_z[1] + small_z[2] + small_z[3]
    wait_recv(gathered_qkv)
    for n, u in enumerate(last):
        u.write(f_qkv, n, outs)
    for u in units:
        u.drain()
    wait_send(moved + [copy for _, copy in back] + small_sent[1:] + gathered + gathered_qkv)


def backward_call(
    g_out, g_fc1, g_fc2, grad_mixed, qkv, kx, qx, ot, lse, normed, wq, pack, tokens, grad_middle, small
):
    hbm = pl.BlockSpec(memory_space=pl.ANY)
    vmem = pl.BlockSpec(memory_space=pltpu.VMEM)
    out = jax.ShapeDtypeStruct
    mem = pltpu.VMEM
    return pl.pallas_call(
        backward_kernel,
        name="backward",
        out_shape=(
            out((2, 32, 3 * D), F32),
            out((2, 32, D), F32),
            out((2, 32, 4 * D), F32),
            out((4, 2, 32, D), F32),
            out((16, 128), F32),
            out((BLK, D), F32),
        ),
        in_specs=[hbm, hbm, hbm, hbm, vmem, vmem, vmem, vmem, vmem, vmem, hbm, vmem, vmem, vmem, vmem],
        out_specs=(vmem,) * 6,
        scratch_shapes=[
            mem((12, 4, 2, 2, 32, D), BF),
            *[mem((count_of(order),) + R1[order], BF) for order in range(3)],
            *[mem((count_of(order),) + R2[order], BF) for order in range(3)],
            mem((12, 3, 32, 256), BF),
            mem((2, 4, 2, 2, 32, D), BF),
            mem(full_shape(3 * D), BF),
            mem((2,) + full_shape(D), BF),
            mem((2, LENGTH, 128), BF),
            mem((2, 64, LENGTH), BF),
            mem((LENGTH, 128), BF),
            mem((2, 8, LENGTH), F32),
            mem((2, 64, LENGTH), F32),
            mem((3, 8, BLK, 128), BF),
            mem((3, BLK, D), BF),
            mem((D, BLK), BF),
            mem((8, 32, 9 * 256), BF),
            mem((8, 32, 3 * 256), BF),
            mem((4, 2, 16, 128), F32),
            mem((4, 2, 16, 128), F32),
            mem((3, 2, 16, 128), F32),
            mem((3, 16, 128), F32),
            mem((4, 16, 128), F32),
            mem((BLK, D), F32),
            pltpu.SemaphoreType.DMA((190,)),
            pltpu.SemaphoreType.DMA((190,)),
        ],
        compiler_params=pltpu.CompilerParams(
            collective_id=1, has_side_effects=True, vmem_limit_bytes=63 * MIB
        ),
    )(
        g_out.reshape(full_shape(D)),
        g_fc1.reshape(full_shape(4 * D)),
        g_fc2.reshape(4, 2, 2, 4, 2, 32, D),
        grad_mixed,
        qkv,
        kx,
        qx,
        ot,
        lse,
        normed,
        wq,
        pack,
        tokens,
        grad_middle,
        small,
    )


def layer_norm(values, gain_vec, bias_vec):
    center = values - jnp.mean(values, axis=-1, keepdims=True)
    spread = jnp.mean(center * center, axis=-1, keepdims=True)
    return center * lax.rsqrt(spread + 1e-05) * gain_vec + bias_vec


def gelu_tanh(values):
    return jax.nn.gelu(values, approximate=True)


def matmul_tn(left, right):
    return lax.dot_general(
        left, right, (((0,), (0,)), ((), ())), preferred_element_type=jnp.float32
    )


def matmul_nt(left, right):
    return lax.dot_general(
        left, right, (((1,), (1,)), ((), ())), preferred_element_type=jnp.float32
    )


def matmul(left, right):
    return jnp.dot(left, right, preferred_element_type=jnp.float32)


def local(
    tokens,
    segment_ids,
    cotangent,
    ln1_gain,
    ln1_bias,
    qkv_weight,
    qkv_bias,
    out_weight,
    out_bias,
    ln2_gain,
    ln2_bias,
    fc1_weight,
    fc1_bias,
    fc2_weight,
    fc2_bias,
):
    block_len = tokens.shape[1]
    small = small_pack(
        ln1_gain, ln1_bias, ln2_gain, ln2_bias, out_bias, fc2_bias, qkv_bias, fc1_bias
    )
    flat = tokens.reshape(block_len, D)
    (wq, wo, w1, w2, pack, normed, qkv, kx, qx, ot, lse, mixed, lse_all) = forward_call(
        flat,
        jnp.broadcast_to(segment_ids, (8, block_len)),
        small,
        qkv_weight,
        out_weight,
        fc1_weight,
        fc2_weight,
    )
    log_sums = lse_all[:, :, 0].reshape(1, HEADS, block_len)

    g_out, g_fc1, g_fc2, grad_mixed, grad_middle, output, small_grads = dense_call(
        flat, cotangent.reshape(block_len, D), mixed, pack, wo, w1, w2
    )
    g_qkv, g_wo, g_up, g_down, small_sums, input_grad = backward_call(
        g_out,
        g_fc1,
        g_fc2,
        grad_mixed,
        qkv,
        kx,
        qx,
        ot,
        lse,
        normed,
        wq,
        pack,
        flat,
        grad_middle,
        small_grads,
    )
    core = lax.axis_index("fsdp") % 2
    halves = lax.dynamic_slice_in_dim(small_sums[:6], core * 64, 64, 1)
    g_qkvb = lax.dynamic_slice_in_dim(small_sums, 6 + core, 1, 0).reshape(128)
    g_upb = lax.dynamic_slice_in_dim(small_sums, 8 + 2 * core, 2, 0).reshape(256)
    return (
        output.reshape(1, block_len, D),
        input_grad.reshape(1, block_len, D),
        halves[0],
        halves[1],
        g_qkv.reshape(64, 3 * D),
        g_qkvb,
        g_wo.reshape(64, D),
        halves[4],
        halves[2],
        halves[3],
        g_up.reshape(64, 4 * D),
        g_upb,
        g_down.reshape(256, D),
        halves[5],
        log_sums,
    )


def solution(mesh):
    placed = (
        P("fsdp", "ctx", None),
        P("fsdp", "ctx"),
        P("fsdp", "ctx", None),
        P("fsdp"),
        P("fsdp"),
        P("fsdp", None),
        P("fsdp"),
        P("fsdp", None),
        P("fsdp"),
        P("fsdp"),
        P("fsdp"),
        P("fsdp", None),
        P("fsdp"),
        P("fsdp", None),
        P("fsdp"),
    )
    return jax.shard_map(
        local,
        mesh=mesh,
        in_specs=placed,
        out_specs=(
            P("fsdp", "ctx", None),
            P("fsdp", "ctx", None),
            P("fsdp"),
            P("fsdp"),
            P("fsdp", None),
            P("fsdp"),
            P("fsdp", None),
            P("fsdp"),
            P("fsdp"),
            P("fsdp"),
            P("fsdp", None),
            P("fsdp"),
            P("fsdp", None),
            P("fsdp"),
            P("fsdp", None, "ctx"),
        ),
        check_vma=False,
    )
```

```python
import functools

import jax
import jax.numpy as jnp
from jax import lax
from jax.experimental import pallas as pl
from jax.experimental.pallas import tpu as pltpu
from jax.sharding import PartitionSpec as P

D = 1024
HEADS = 16
HEAD_DIM = 64
LENGTH = 2048
BLK = 256
BF = jnp.bfloat16
F32 = jnp.float32
BIG = 2.0**100
MIB = 2**20
NONE = slice(None)

QKV_SEGS = ((0, 0, 0, 1), (0, 1, 1, 1), (0, 2, 2, 1))
REST_SEGS = (
    (1, 0, 0, 1),
    (2, 0, 0, 2),
    (2, 1, 2, 1),
    (2, 2, 3, 1),
    (3, 0, 0, 2),
    (3, 1, 2, 1),
    (3, 2, 3, 1),
)


def place():
    c = lax.axis_index("ctx")
    f = lax.axis_index("fsdp")
    return f // 4, ((f // 2) % 2) * 2 + c // 4, c % 4, f % 2


def device(x, y, z, core):
    return {"ctx": (y % 2) * 4 + z, "fsdp": x * 4 + (y // 2) * 2 + core}


class Links:
    def __init__(self, send, recv):
        self.send, self.recv, self.used = send, recv, 0
        self.x, self.y, self.z, self.core = place()
        self.yh, self.yl = self.y // 2, self.y % 2
        self.me = self.yl * 4 + self.z

    def peers(self, axis):
        x, y, z, c = self.x, self.y, self.z, self.core
        if axis == "x":
            return [device((x + j) % 4, y, z, c) for j in (1, 2, 3)]
        if axis == "y":
            return [device(x, (y + j) % 4, z, c) for j in (1, 2, 3)]
        if axis == "z":
            return [device(x, y, (z + j) % 4, c) for j in (1, 2, 3)]
        return [device(x, y, z, 1 - c)]

    def rows_peers(self):
        out = []
        for j in range(1, 8):
            t = (self.me + j) % 8
            out.append((t, device(self.x, self.yh * 2 + t // 4, t % 4, self.core)))
        return out

    def barrier(self):
        everyone = self.peers("x") + self.peers("y") + self.peers("z") + self.peers("core")
        for j in (1, 2, 3):
            everyone.append(device(self.x, self.yh * 2 + 1 - self.yl, (self.z + j) % 4, self.core))
        sem = pltpu.get_barrier_semaphore()
        for who in everyone:
            pl.semaphore_signal(sem, inc=1, device_id=who)
        pl.semaphore_wait(sem, len(everyone))

    def to(self, src, dst, who):
        i = self.used
        self.used += 1
        copy = pltpu.make_async_remote_copy(
            src_ref=src,
            dst_ref=dst,
            send_sem=self.send.at[i],
            recv_sem=self.recv.at[i],
            device_id=who,
        )
        copy.start()
        return copy

    def local(self, src, dst):
        i = self.used
        self.used += 1
        copy = pltpu.make_async_copy(src, dst, self.send.at[i])
        copy.start()
        return copy


def wait_recv(copies):
    for copy in copies:
        copy.wait_recv()


def wait_send(copies):
    for copy in copies:
        copy.wait_send()


class Gather:
    def __init__(self, links, full, shard, seg):
        tensor, self.order, first, count = seg
        self.links, self.full, self.shard = links, full, shard
        self.blocked = tensor == 3
        if self.blocked:
            self.units = (pl.ds(first, count),)
            self.all_cols = pl.ds(0, D)
            width = D // 4
            self.z_cols = pl.ds(pl.multiple_of(links.z * width, width), width)
        else:
            self.units = ()
            self.all_cols = pl.ds(first * D, count * D)
            width = count * D // 4
            self.z_cols = pl.ds(pl.multiple_of(first * D + links.z * width, width), width)
        self.sent = []

    def view(self, x, yh, yl, cols):
        return self.full.at[(x, yh, self.links.core) + self.units + (yl, NONE, cols)]

    def own(self, cols):
        return self.shard.at[self.units + (self.links.yl, NONE, cols)]

    def push(self, src, dst, axis):
        now = [self.links.to(src, dst, who) for who in self.links.peers(axis)]
        self.sent += now
        return now

    def stage1(self):
        k = self.links
        cols = self.all_cols if self.order == 0 else self.z_cols
        dst = self.view(k.x, k.yh, k.yl, cols)
        self.kept = k.local(self.own(cols), dst)
        self.first = self.push(self.own(cols), dst, "x" if self.order == 1 else "y")

    def stage2(self):
        k = self.links
        self.kept.wait()
        wait_recv(self.first)
        if self.order == 0:
            part = self.view(k.x, NONE, NONE, self.all_cols)
            self.last = self.push(part, part, "x")
        elif self.order == 1:
            part = self.view(NONE, k.yh, k.yl, self.z_cols)
            self.second = self.push(part, part, "z")
        else:
            part = self.view(k.x, NONE, NONE, self.z_cols)
            self.second = self.push(part, part, "x")

    def stage3(self):
        k = self.links
        if self.order == 0:
            return
        wait_recv(self.second)
        if self.order == 1:
            part = self.view(NONE, k.yh, k.yl, self.all_cols)
            self.last = self.push(part, part, "y")
        else:
            part = self.view(NONE, NONE, NONE, self.z_cols)
            self.last = self.push(part, part, "z")

    def cross(self):
        wait_recv(self.last)
        part = self.view(NONE, NONE, NONE, self.all_cols)
        self.swapped = self.push(part, part, "core")

    def finish(self):
        wait_recv(self.swapped)

    def drain(self):
        wait_send(self.sent)


def small_row(pack, row):
    pieces = []
    for x in range(4):
        for yh in range(2):
            pieces.append(
                pack[x, yh, 0, row : row + 1, :].astype(F32)
                + pack[x, yh, 1, row : row + 1, :].astype(F32)
            )
    return jnp.concatenate(pieces, axis=1)


def dot_nt(a, b):
    return lax.dot_general(a, b, (((1,), (1,)), ((), ())), preferred_element_type=F32)


def dot_tn(a, b):
    return lax.dot_general(a, b, (((0,), (0,)), ((), ())), preferred_element_type=F32)


def dot(a, b):
    return jnp.dot(a, b, preferred_element_type=F32)


def slope_of(links, h, shape):
    power = (links.me * 2 + h + 1).astype(F32) * -0.5
    return jnp.exp2(jnp.full(shape, power, F32)) * (4.0 / LENGTH)


def extend(links, seg_ref, qkv_ref, kx_ref, qx_ref, h, t):
    rows = pl.ds(t * BLK, BLK)
    seg = jnp.broadcast_to(seg_ref[t, 0:1, :].astype(F32), (128, BLK)).T
    lane = lax.broadcasted_iota(jnp.int32, (BLK, 128), 1)
    mine = (lane // 64) == h
    e = lane - 64 * (1 - h)
    where = lax.broadcasted_iota(jnp.int32, (BLK, 128), 0) + t * BLK
    bias = slope_of(links, h, (BLK, 128)) * where.astype(F32)
    high = bias.astype(BF).astype(F32)
    mid = (bias - high).astype(BF).astype(F32)
    low = bias - high - mid
    doc = (e - 3).astype(F32)
    is_doc = (e >= 3) & (e <= 6)
    same = seg == doc
    key_extra = jnp.where(is_doc & jnp.logical_not(same), 1.0, 0.0)
    key_extra = jnp.where(e == 0, high, jnp.where(e == 1, mid, jnp.where(e == 2, low, key_extra)))
    query_extra = jnp.where(is_doc & same, -BIG, 0.0)
    query_extra = jnp.where((e >= 0) & (e <= 2), 1.0, query_extra)
    query = qkv_ref[0, rows, :].astype(F32) * 0.125
    key = qkv_ref[1, rows, :].astype(F32)
    kx_ref[h, rows, :] = jnp.where(mine, key, key_extra).astype(BF)
    qx_ref[h, rows, :] = jnp.where(mine, query, query_extra).astype(BF)


def attend(links, kx_ref, qx_ref, vt_ref, ot_ref, lse_ref, h, i):
    keys = BLK * (i + 1)
    qb = qx_ref[h, BLK * i : keys, :]
    down = lax.broadcasted_iota(jnp.int32, (BLK, BLK), 0)
    across = lax.broadcasted_iota(jnp.int32, (BLK, BLK), 1)
    edge = jnp.where(down <= across, dot_nt(kx_ref[h, BLK * i : keys, :], qb), -BIG)
    top = jnp.max(edge, axis=0, keepdims=True)
    if i:
        past = dot_nt(kx_ref[h, 0 : BLK * i, :], qb)
        top = jnp.maximum(top, jnp.max(past, axis=0, keepdims=True))
    edge = jnp.exp(edge - top)
    total = jnp.sum(edge, axis=0, keepdims=True)
    out = dot(vt_ref[h, :, BLK * i : keys], edge.astype(BF))
    if i:
        past = jnp.exp(past - top)
        total = total + jnp.sum(past, axis=0, keepdims=True)
        out = out + dot(vt_ref[h, :, 0 : BLK * i], past.astype(BF))
    ot_ref[h, :, BLK * i : keys] = out / total
    where = (lax.broadcasted_iota(jnp.int32, (1, BLK), 1) + BLK * i).astype(F32)
    shifted = top + jnp.log(total)
    final = shifted - slope_of(links, h, (1, BLK)) * where
    first = lax.broadcasted_iota(jnp.int32, (8, BLK), 0) == 0
    lse_ref[h, :, BLK * i : keys] = jnp.where(first, final, shifted)


def forward_kernel(
    tokens,
    seg,
    small,
    wq_in,
    wo_in,
    w1_in,
    w2_in,
    wq_out,
    wo,
    w1,
    w2,
    pack_out,
    normed_out,
    qkv_out,
    kx,
    qx,
    ot,
    lse,
    mixed,
    lse_all,
    wq,
    pack,
    seg_all,
    row,
    merged,
    qkv,
    vt,
    mixed_send,
    send,
    recv,
):
    k = Links(send, recv)
    k.barrier()
    sent, kept = [], []

    kept_small = k.local(small, pack.at[k.x, k.yh, k.core])
    small_x = [k.to(small, pack.at[k.x, k.yh, k.core], who) for who in k.peers("x")]
    fulls, shards = (wq, wo, w1, w2), (wq_in, wo_in, w1_in, w2_in)
    first = [Gather(k, fulls[s[0]], shards[s[0]], s) for s in QKV_SEGS]
    rest = [Gather(k, fulls[s[0]], shards[s[0]], s) for s in REST_SEGS]
    for g in first:
        g.stage1()
    kept_seg = k.local(seg, seg_all.at[k.me])
    segs = [k.to(seg, seg_all.at[k.me], who) for _, who in k.rows_peers()]
    for g in first:
        g.stage2()
    kept_small.wait()
    wait_recv(small_x)
    part = pack.at[:, k.yh, k.core]
    small_y = [k.to(part, part, k.peers("y")[1])]
    for g in rest:
        g.stage1()
    for g in first:
        g.stage3()
    wait_recv(small_y)
    part = pack.at[:, :, k.core]
    small_c = [k.to(part, part, k.peers("core")[0])]

    for g in rest:
        g.stage2()
    values = tokens[...].astype(F32)
    center = values - jnp.mean(values, axis=1, keepdims=True)
    center = center * lax.rsqrt(jnp.mean(center * center, axis=1, keepdims=True) + 1e-05)
    wait_recv(small_c)
    normed_out[...] = (center * small_row(pack, 0) + small_row(pack, 1)).astype(BF)
    pack_out[...] = pack[...]
    pieces = []
    for f in range(16):
        pieces.append(pack[f // 4, (f // 2) % 2, f % 2, 6:7, :].astype(F32))
    row[...] = jnp.broadcast_to(
        jnp.concatenate(pieces[:8] + [jnp.zeros((1, D), F32)] + pieces[8:], axis=1), (8, 3 * D)
    )
    for g in first:
        g.cross()
    for g in first:
        g.finish()
    kept.append(k.local(wq, wq_out))

    @pl.loop(0, 12)
    def _(n):
        cols = pl.ds(pl.multiple_of(n * 256, 256), 256)
        weight = wq[:, :, :, :, :, cols].reshape(D, 256)
        block = (dot(normed_out[...], weight) + row[0:1, cols]).astype(BF)
        merged[n // 4, 2 * (n % 4)] = block[:, :128]
        merged[n // 4, 2 * (n % 4) + 1] = block[:, 128:]

    mine = pl.ds(pl.multiple_of(k.me * BLK, BLK), BLK)
    kept_qkv = k.local(merged.at[:, k.me], qkv.at[:, mine])
    moved = [k.to(merged.at[:, t], qkv.at[:, mine], who) for t, who in k.rows_peers()]
    for g in rest:
        g.stage3()
    kept_seg.wait()
    wait_recv(segs)
    kept_qkv.wait()
    wait_recv(moved)
    kept.append(k.local(qkv, qkv_out))

    @pl.loop(0, 8)
    def _(t):
        for h in range(2):
            extend(k, seg_all, qkv, kx, qx, h, t)

    for t in range(8):
        flipped = qkv[2, BLK * t : BLK * (t + 1), :].astype(F32).T.astype(BF)
        for h in range(2):
            vt[h, :, BLK * t : BLK * (t + 1)] = flipped[64 * h : 64 * (h + 1)]

    for i in range(8):

        @pl.loop(0, 2)
        def _(h):
            attend(k, kx, qx, vt, ot, lse, h, i)
        if i == 5:
            for g in rest:
                if g.order == 0:
                    g.cross()

        both = jnp.concatenate(
            [ot[0, :, BLK * i : BLK * (i + 1)], ot[1, :, BLK * i : BLK * (i + 1)]], axis=0
        )
        mixed_send[i] = both.T.astype(BF)

    cols = pl.ds(pl.multiple_of(k.me * 128, 128), 128)
    kept.append(k.local(mixed_send.at[k.me], mixed.at[:, cols]))
    back = [k.to(mixed_send.at[t], mixed.at[:, cols], who) for t, who in k.rows_peers()]
    part = pl.ds(pl.multiple_of(k.me * BLK, BLK), BLK)
    kept.append(k.local(lse.at[:, :, part], lse_all.at[k.me]))
    for t, who in k.rows_peers():
        part = pl.ds(pl.multiple_of(t * BLK, BLK), BLK)
        back.append(k.to(lse.at[:, :, part], lse_all.at[k.me], who))
    for g in rest:
        if g.order != 0:
            g.cross()
    wait_recv(back)
    for g in rest:
        g.finish()
    for copy in kept:
        copy.wait()
    for g in first + rest:
        g.drain()
    wait_send(small_x + small_y + small_c + segs + moved + back)


def full_shape(cols):
    return (4, 2, 2, 2, 32, cols)


def forward_call(tokens, seg, small, wq, wo, w1, w2):
    hbm = pl.BlockSpec(memory_space=pl.ANY)
    vmem = pl.BlockSpec(memory_space=pltpu.VMEM)
    out = jax.ShapeDtypeStruct
    return pl.pallas_call(
        forward_kernel,
        name="forward",
        out_shape=(
            out(full_shape(3 * D), BF),
            out(full_shape(D), BF),
            out(full_shape(4 * D), BF),
            out((4, 2, 2, 4, 2, 32, D), BF),
            out((4, 2, 2, 16, 128), BF),
            out((BLK, D), BF),
            out((3, LENGTH, 128), BF),
            out((2, LENGTH, 128), BF),
            out((2, LENGTH, 128), BF),
            out((2, 64, LENGTH), F32),
            out((2, 8, LENGTH), F32),
            out((BLK, D), BF),
            out((8, 2, 8, BLK), F32),
        ),
        in_specs=[vmem, vmem, vmem, hbm, hbm, hbm, hbm],
        out_specs=(hbm, hbm, hbm, hbm, vmem, vmem, hbm, vmem, vmem, vmem, vmem, hbm, hbm),
        scratch_shapes=[
            pltpu.VMEM(full_shape(3 * D), BF),
            pltpu.VMEM((4, 2, 2, 16, 128), BF),
            pltpu.VMEM((8, 8, BLK), jnp.int32),
            pltpu.VMEM((8, 3 * D), F32),
            pltpu.VMEM((3, 8, BLK, 128), BF),
            pltpu.VMEM((3, LENGTH, 128), BF),
            pltpu.VMEM((2, 64, LENGTH), BF),
            pltpu.VMEM((8, BLK, 128), BF),
            pltpu.SemaphoreType.DMA((170,)),
            pltpu.SemaphoreType.DMA((170,)),
        ],
        compiler_params=pltpu.CompilerParams(
            collective_id=0, has_side_effects=True, vmem_limit_bytes=62 * MIB
        ),
    )(
        tokens,
        seg,
        small,
        wq.reshape(2, 32, 3 * D),
        wo.reshape(2, 32, D),
        w1.reshape(2, 32, 4 * D),
        w2.reshape(4, 2, 32, D),
    )


def small_pack(ln1_gain, ln1_bias, ln2_gain, ln2_bias, out_bias, fc2_bias, qkv_bias, fc1_bias):
    core = lax.axis_index("fsdp") % 2
    six = jnp.stack([ln1_gain, ln1_bias, ln2_gain, ln2_bias, out_bias, fc2_bias])
    none = jnp.zeros_like(six)
    halves = jnp.where(
        core == 0, jnp.concatenate([six, none], 1), jnp.concatenate([none, six], 1)
    )
    return jnp.concatenate(
        [halves, qkv_bias[None], fc1_bias.reshape(2, 128), jnp.zeros((7, 128), BF)], 0
    )


def unpack_row(pack, row):
    return (pack[:, :, 0, row] + pack[:, :, 1, row]).reshape(D)


REST_UNITS = (
    (3, 0, 0),
    (3, 1, 1),
    (3, 2, 2),
    (3, 3, 2),
    (2, 0, 0),
    (2, 1, 0),
    (2, 2, 1),
    (2, 3, 2),
    (1, 0, 0),
)
QKV_UNITS = ((0, 0, 0), (0, 1, 1), (0, 2, 2))
UNITS = REST_UNITS + QKV_UNITS
R1 = ((3, 2, 2, 32, D), (3, 4, 32, D), (3, 4, 2, 2, 32, 256))
R2 = ((3, 32, D), (3, 4, 32, 256), (3, 2, 2, 32, 256))


def count_of(order):
    return sum(1 for unit in UNITS if unit[2] == order)


class Reduce:
    def __init__(self, links, unit, n, grads, half, slots):
        self.tensor, self.unit, self.order = unit
        self.links, self.grad = links, grads[self.tensor]
        self.half = half.at[n]
        at = sum(1 for other in UNITS[:n] if other[2] == self.order)
        self.r1 = slots[self.order].at[at]
        self.r2 = slots[3 + self.order].at[at]
        self.r3 = slots[6].at[n]
        self.z_cols = self.cols_of(links.z)
        self.sent = []

    def cols_of(self, z):
        return pl.ds(pl.multiple_of(z * 256, 256), 256)

    def of_core(self, core):
        if self.tensor == 3:
            return self.grad.at[:, :, core, self.unit]
        return self.grad.at[:, :, core, :, :, pl.ds(self.unit * D, D)]

    def stage0(self):
        k = self.links
        self.swap = k.to(self.of_core(1 - k.core), self.half, k.peers("core")[0])
        self.sent.append(self.swap)

    def push(self, axis, src_of, slot):
        k = self.links
        here = {"x": k.x, "y": k.y, "z": k.z}[axis]
        self.coming = []
        for j, who in enumerate(k.peers(axis)):
            copy = k.to(src_of((here + j + 1) % 4), slot.at[j], who)
            self.coming.append(copy)
        self.sent += self.coming

    def add0(self, own):
        self.swap.wait_recv()

        @pl.loop(0, 16)
        def _(i):
            x, yh, yl = i // 4, (i // 2) % 2, i % 2
            total = self.half[x, yh, yl].astype(F32) + own(x, yh, yl).astype(F32)
            self.half[x, yh, yl] = total.astype(BF)

    def stage1(self):
        half = self.half
        if self.order == 0:
            self.push("x", lambda x: half.at[x], self.r1)
        elif self.order == 1:
            self.push("y", lambda y: half.at[:, y // 2, y % 2], self.r1)
        else:
            self.push("z", lambda z: half.at[:, :, :, :, self.cols_of(z)], self.r1)

    def sum1(self):
        k, half, got = self.links, self.half, self.r1
        wait_recv(self.coming)

        @pl.loop(0, 16 if self.order == 2 else 4)
        def _(i):
            if self.order == 0:
                spot, index = (k.x, i // 2, i % 2), (i // 2, i % 2)
            elif self.order == 1:
                spot, index = (i, k.yh, k.yl), (i,)
            else:
                index = (i // 4, (i // 2) % 2, i % 2)
                spot = index + (NONE, self.z_cols)
            total = half[spot].astype(F32)
            for j in range(3):
                total = total + got[(j,) + index].astype(F32)
            half[spot] = total.astype(BF)

    def stage2(self):
        k, half = self.links, self.half
        if self.order == 0:
            self.push("y", lambda y: half.at[k.x, y // 2, y % 2], self.r2)
        elif self.order == 1:
            self.push("z", lambda z: half.at[:, k.yh, k.yl, :, self.cols_of(z)], self.r2)
        else:
            self.push("x", lambda x: half.at[x, :, :, :, self.z_cols], self.r2)

    def sum2(self):
        k, half, got = self.links, self.half, self.r2
        wait_recv(self.coming)
        if self.order == 0:
            spot = (k.x, k.yh, k.yl)
            total = half[spot].astype(F32)
            for j in range(3):
                total = total + got[j].astype(F32)
            half[spot] = total.astype(BF)
            return

        @pl.loop(0, 4)
        def _(i):
            if self.order == 1:
                spot, index = (i, k.yh, k.yl, NONE, self.z_cols), (i,)
            else:
                spot, index = (k.x, i // 2, i % 2, NONE, self.z_cols), (i // 2, i % 2)
            total = half[spot].astype(F32)
            for j in range(3):
                total = total + got[(j,) + index].astype(F32)
            half[spot] = total.astype(BF)

    def stage3(self):
        k, half = self.links, self.half
        if self.order == 0:
            self.push("z", lambda z: half.at[k.x, k.yh, k.yl, :, self.cols_of(z)], self.r3)
        elif self.order == 1:
            self.push("x", lambda x: half.at[x, k.yh, k.yl, :, self.z_cols], self.r3)
        else:
            self.push("y", lambda y: half.at[k.x, y // 2, y % 2, :, self.z_cols], self.r3)

    def sum3(self, out_ref, position):
        k = self.links
        wait_recv(self.coming)
        total = self.half[k.x, k.yh, k.yl, :, self.z_cols].astype(F32)
        for j in range(3):
            total = total + self.r3[j].astype(F32)
        out_ref[k.me, :, 256 * position : 256 * (position + 1)] = total.astype(BF)

    def drain(self):
        wait_send(self.sent)

    def write(self, got, position, outs):
        out = outs[self.tensor]
        for t in range(8):
            piece = got[t, :, 256 * position : 256 * (position + 1)]
            if self.tensor == 3:
                out[self.unit, t // 4, :, 256 * (t % 4) : 256 * (t % 4 + 1)] = piece
            else:
                first = self.unit * D + 256 * (t % 4)
                out[t // 4, :, first : first + 256] = piece


def attend_back(kx, qx, vx, kt, do, delta, lse, dqt, h, j):
    keys = slice(BLK * j, BLK * (j + 1))
    down = lax.broadcasted_iota(jnp.int32, (BLK, BLK), 0)
    across = lax.broadcasted_iota(jnp.int32, (BLK, BLK), 1)
    grad_key = grad_value = None
    cuts = [BLK * j, BLK * (j + 1)] + list(range(BLK * (j + 1) + 768, LENGTH, 768))
    if cuts[-1] < LENGTH:
        cuts.append(LENGTH)
    for n in range(len(cuts) - 1):
        rows = slice(cuts[n], cuts[n + 1])
        queries = qx[h, rows, :]
        scores = dot_nt(kx[h, keys, :], queries)
        if n == 0:
            scores = jnp.where(down <= across, scores, -BIG)
        probs = jnp.exp(scores - lse[h, 1:2, rows])
        grad_out = do[rows, :]
        grad_probs = dot_nt(vx[h, keys, :], grad_out)
        grad_scores = (probs * (grad_probs - delta[h, 0:1, rows])).astype(BF)
        value_part = dot(probs.astype(BF), grad_out)
        key_part = dot(grad_scores, queries)
        grad_value = value_part if n == 0 else grad_value + value_part
        grad_key = key_part if n == 0 else grad_key + key_part
        query_part = dot(kt[h, :, keys], grad_scores)
        if j == 0:
            dqt[h, :, rows] = query_part
        else:
            dqt[h, :, rows] += query_part
    return grad_key, grad_value


def backward_kernel(
    g_out,
    g_fc1,
    g_fc2,
    grad_mixed,
    qkv,
    kx,
    qx,
    ot,
    lse,
    normed,
    wq_in,
    pack,
    tokens,
    small_in,
    o_qkv,
    o_out,
    o_fc1,
    o_fc2,
    o_small,
    input_grad,
    half,
    r1x,
    r1y,
    r1z,
    r2x,
    r2y,
    r2z,
    r3,
    own,
    g_qkv,
    w_slot,
    vx,
    kt,
    do,
    delta,
    dqt,
    g_send,
    g_merged,
    normed_t,
    f_rest,
    f_qkv,
    small,
    small_core,
    small_x,
    small_y,
    small_z,
    gn,
    send,
    recv,
):
    k = Links(send, recv)
    k.barrier()
    grads = (g_qkv, g_out, g_fc1, g_fc2)
    slots = (r1x, r1y, r1z, r2x, r2y, r2z, r3)
    units = [Reduce(k, unit, n, grads, half, slots) for n, unit in enumerate(UNITS)]
    rest, last = units[:9], units[9:]
    for u in rest:
        u.stage0()
    mine = pl.ds(pl.multiple_of(k.me * BLK, BLK), BLK)

    def heads_of(t):
        return pl.ds(pl.multiple_of(t * 128, 128), 128)

    kept_do = k.local(grad_mixed.at[:, heads_of(k.me)], do.at[mine])
    moved = [
        k.to(grad_mixed.at[:, heads_of(t)], do.at[mine], who) for t, who in k.rows_peers()
    ]
    loads = [k.local(u.of_core(k.core), own.at[n]) for n, u in enumerate(rest[:2])]

    lane = lax.broadcasted_iota(jnp.int32, (BLK, 128), 1)
    for t in range(8):
        rows = slice(BLK * t, BLK * (t + 1))
        value = qkv[2, rows, :]
        flipped = qkv[1, rows, :].astype(F32).T.astype(BF)
        for h in range(2):
            vx[h, rows, :] = jnp.where((lane // 64) == h, value.astype(F32), 0.0).astype(BF)
            kt[h, :, rows] = flipped[64 * h : 64 * (h + 1)]
    normed_t[...] = normed[...].astype(F32).T.astype(BF)
    kept_do.wait()
    wait_recv(moved)
    for t in range(8):
        rows = slice(BLK * t, BLK * (t + 1))
        flipped = do[rows, :].astype(F32).T
        for h in range(2):
            product = flipped[64 * h : 64 * (h + 1)] * ot[h, :, rows]
            delta[h, :, rows] = jnp.broadcast_to(
                jnp.sum(product, axis=0, keepdims=True), (8, BLK)
            )
    for n, u in enumerate(rest):
        loads[n].wait()
        u.add0(lambda x, yh, yl, n=n: own[n % 2, x, yh, yl])
        u.stage1()
        if n + 2 < len(rest):
            loads.append(k.local(rest[n + 2].of_core(k.core), own.at[n % 2]))

    back = []
    for t, who in k.rows_peers():
        i = k.used
        k.used += 1
        copy = pltpu.make_async_remote_copy(
            src_ref=g_send.at[:, t],
            dst_ref=g_merged.at[:, :, heads_of(k.me)],
            send_sem=k.send.at[i],
            recv_sem=k.recv.at[i],
            device_id=who,
        )
        back.append((t, copy))
    for j in range(8):
        found = [attend_back(kx, qx, vx, kt, do, delta, lse, dqt, h, j) for h in range(2)]
        left = (lane // 64) == 0
        for s, position in ((1, 0), (2, 1)):
            both = jnp.where(left, found[0][position], found[1][position])
            g_send[s, j] = both.astype(BF)
        rows = slice(BLK * j, BLK * (j + 1))
        query = jnp.concatenate([dqt[0, :, rows], dqt[1, :, rows]], axis=0).T * 0.125
        g_send[0, j] = query.astype(BF)
        if j in (3, 7):
            for t, copy in back:
                pl.when((t // 4) == (j // 4))(copy.start)
    kept_g = k.local(g_send.at[:, k.me], g_merged.at[:, :, heads_of(k.me)])

    def w_load(s):
        cols = pl.ds(s * D, D)
        return k.local(wq_in.at[:, :, :, :, :, cols], w_slot.at[s % 2])

    w_loads = [w_load(0), w_load(1)]
    for u in rest:
        u.sum1()
        u.stage2()
    kept_g.wait()
    for _, copy in back:
        copy.wait_recv()

    for s in range(3):

        @pl.loop(0, 4)
        def _(n):
            cols = pl.ds(pl.multiple_of(n * 256, 256), 256)
            block = dot(normed_t[...], g_merged[s, :, cols]).astype(BF)
            there = pl.ds(pl.multiple_of(s * D + n * 256, 256), 256)
            g_qkv[:, :, :, :, :, there] = block.reshape(4, 2, 2, 2, 32, 256)

        last[s].stage0()
    for u in rest:
        u.sum2()
        u.stage3()

    for s in range(3):
        w_loads[s].wait()
        for n in range(4):
            weight = w_slot[s % 2, n].reshape(256, D)
            part = dot_nt(g_merged[s], weight)
            cols = slice(256 * n, 256 * (n + 1))
            if s == 0:
                gn[:, cols] = part
            else:
                gn[:, cols] += part
        if s == 0:
            w_loads.append(w_load(2))
    for s, u in enumerate(last):
        cols = pl.ds(s * D, D)
        u.add0(lambda x, yh, yl, cols=cols: g_qkv[x, yh, k.core, yl, :, cols])
        u.stage1()

    values = tokens[...].astype(F32)
    center = values - jnp.mean(values, axis=1, keepdims=True)
    scale = lax.rsqrt(jnp.mean(center * center, axis=1, keepdims=True) + 1e-05)
    center = center * scale
    grad_normed = gn[...]
    by_gain = jnp.sum(grad_normed * center, axis=0, keepdims=True)
    by_bias = jnp.sum(grad_normed, axis=0, keepdims=True)
    inner = grad_normed * small_row(pack, 0)
    part = inner - jnp.mean(inner, axis=1, keepdims=True)
    part = part - center * jnp.mean(inner * center, axis=1, keepdims=True)
    input_grad[...] = part * scale
    by_query = jnp.sum(g_merged[0].astype(F32), axis=0, keepdims=True)
    by_value = jnp.sum(g_merged[2].astype(F32), axis=0, keepdims=True)
    small[...] = small_in[...]
    for x in range(4):
        for yh in range(2):
            n = 2 * x + yh
            cols = slice(128 * n, 128 * (n + 1))
            small[x, yh, 0:1, :] = by_gain[:, cols]
            small[x, yh, 1:2, :] = by_bias[:, cols]
            source = by_query if x < 2 else by_value
            first = 256 * (n % 4)
            small[x, yh, 6:7, :] = source[:, first : first + 128]
            small[x, yh, 7:8, :] = source[:, first + 128 : first + 256]
    small_sent = [k.to(small, small_core, k.peers("core")[0])]

    for n, u in enumerate(rest):
        u.sum3(f_rest, n)
    gathered = [k.to(f_rest.at[k.me], f_rest.at[k.me], who) for _, who in k.rows_peers()]

    small_sent[0].wait()
    small[...] = small[...] + small_core[...]
    coming = [
        k.to(small.at[(k.x + j + 1) % 4], small_x.at[j], who)
        for j, who in enumerate(k.peers("x"))
    ]
    small_sent += coming
    for u in last:
        u.sum1()
        u.stage2()
    wait_recv(coming)
    small[k.x] = small[k.x] + small_x[0] + small_x[1] + small_x[2]
    coming = [
        k.to(small.at[k.x, ((k.y + j + 1) % 4) // 2], small_y.at[j], who)
        for j, who in enumerate(k.peers("y"))
    ]
    small_sent += coming
    for u in last:
        u.sum2()
        u.stage3()
    wait_recv(coming)
    small_z[3] = small[k.x, k.yh] + small_y[0] + small_y[1] + small_y[2]
    coming = [k.to(small_z.at[3], small_z.at[j], who) for j, who in enumerate(k.peers("z"))]
    small_sent += coming
    for n, u in enumerate(last):
        u.sum3(f_qkv, n)
    gathered_qkv = [k.to(f_qkv.at[k.me], f_qkv.at[k.me], who) for _, who in k.rows_peers()]
    outs = (o_qkv, o_out, o_fc1, o_fc2)
    wait_recv(gathered)
    for n, u in enumerate(rest):
        u.write(f_rest, n, outs)
    wait_recv(coming)
    o_small[...] = small_z[0] + small_z[1] + small_z[2] + small_z[3]
    wait_recv(gathered_qkv)
    for n, u in enumerate(last):
        u.write(f_qkv, n, outs)
    for u in units:
        u.drain()
    wait_send(moved + [copy for _, copy in back] + small_sent[1:] + gathered + gathered_qkv)


def backward_call(
    g_out, g_fc1, g_fc2, grad_mixed, qkv, kx, qx, ot, lse, normed, wq, pack, tokens, small
):
    hbm = pl.BlockSpec(memory_space=pl.ANY)
    vmem = pl.BlockSpec(memory_space=pltpu.VMEM)
    out = jax.ShapeDtypeStruct
    mem = pltpu.VMEM
    return pl.pallas_call(
        backward_kernel,
        name="backward",
        out_shape=(
            out((2, 32, 3 * D), BF),
            out((2, 32, D), BF),
            out((2, 32, 4 * D), BF),
            out((4, 2, 32, D), BF),
            out((16, 128), F32),
            out((BLK, D), F32),
        ),
        in_specs=[hbm, hbm, hbm, hbm, vmem, vmem, vmem, vmem, vmem, vmem, hbm, vmem, vmem, vmem],
        out_specs=(vmem,) * 6,
        scratch_shapes=[
            mem((12, 4, 2, 2, 32, D), BF),
            *[mem((count_of(order),) + R1[order], BF) for order in range(3)],
            *[mem((count_of(order),) + R2[order], BF) for order in range(3)],
            mem((12, 3, 32, 256), BF),
            mem((2, 4, 2, 2, 32, D), BF),
            mem(full_shape(3 * D), BF),
            mem((2,) + full_shape(D), BF),
            mem((2, LENGTH, 128), BF),
            mem((2, 64, LENGTH), BF),
            mem((LENGTH, 128), BF),
            mem((2, 8, LENGTH), F32),
            mem((2, 64, LENGTH), F32),
            mem((3, 8, BLK, 128), BF),
            mem((3, BLK, D), BF),
            mem((D, BLK), BF),
            mem((8, 32, 9 * 256), BF),
            mem((8, 32, 3 * 256), BF),
            mem((4, 2, 16, 128), F32),
            mem((4, 2, 16, 128), F32),
            mem((3, 2, 16, 128), F32),
            mem((3, 16, 128), F32),
            mem((4, 16, 128), F32),
            mem((BLK, D), F32),
            pltpu.SemaphoreType.DMA((190,)),
            pltpu.SemaphoreType.DMA((190,)),
        ],
        compiler_params=pltpu.CompilerParams(
            collective_id=1, has_side_effects=True, vmem_limit_bytes=63 * MIB
        ),
    )(
        g_out.reshape(full_shape(D)),
        g_fc1.reshape(full_shape(4 * D)),
        g_fc2.reshape(4, 2, 2, 4, 2, 32, D),
        grad_mixed,
        qkv,
        kx,
        qx,
        ot,
        lse,
        normed,
        wq,
        pack,
        tokens,
        small,
    )


def norm_parts(values):
    center = values - jnp.mean(values, axis=1, keepdims=True)
    scale = lax.rsqrt(jnp.mean(center * center, axis=1, keepdims=True) + 1e-05)
    return center * scale, scale


def norm_back(grad, normal, scale, gain):
    inner = grad * gain
    part = inner - jnp.mean(inner, axis=1, keepdims=True)
    part = part - normal * jnp.mean(inner * normal, axis=1, keepdims=True)
    by_gain = jnp.sum(grad * normal, axis=0, keepdims=True)
    return part * scale, by_gain, jnp.sum(grad, axis=0, keepdims=True)


def put_small(small, row, values):
    for n in range(8):
        small[n // 2, n % 2, row : row + 1, :] = values[:, 128 * n : 128 * (n + 1)]


def dense_kernel(
    tokens, cotangent, mixed, pack, wo, w1, w2,
    g_out, g_fc1, g_fc2, grad_mixed, grad_middle, output, small,
    gp, g2, gn, middle, bias_sums, w1s, w2s, wos, out_acc, normed, normed_t, sems, out_sems,
):
    def load(u, n):
        cols = pl.ds(pl.multiple_of(u * D + n * 512, 512), 512)
        return (
            pltpu.make_async_copy(w1.at[:, :, :, :, :, cols], w1s.at[n], sems.at[n]),
            pltpu.make_async_copy(w2.at[u, n], w2s.at[n], sems.at[2 + n]),
        )

    first = pltpu.make_async_copy(wo, wos, sems.at[4])
    first.start()
    for n in range(2):
        for copy in load(0, n):
            copy.start()
    small[...] = jnp.zeros((4, 2, 16, 128), F32)
    gain, bias = small_row(pack, 2), small_row(pack, 3)
    first.wait()

    @pl.loop(0, 4)
    def _(n):
        cols = pl.ds(pl.multiple_of(n * 256, 256), 256)
        weight = wos[:, :, :, :, :, cols].reshape(D, 256)
        middle[:, cols] = dot(mixed[...], weight) + tokens[:, cols].astype(F32)

    values = middle[...] + small_row(pack, 4)
    middle[...] = values
    normal, _ = norm_parts(values)
    second = normal * gain + bias
    normed[...] = second.astype(BF)
    normed_t[...] = second.T.astype(BF)
    out_acc[...] = values + small_row(pack, 5)
    gn[...] = jnp.zeros((BLK, D), F32)

    written = []
    for u in range(4):

        @pl.loop(0, 2)
        def _(n):
            for copy in load(u, n):
                copy.wait()
            up = w1s[n].reshape(D, 512)
            pieces = [pack[u, n, i // 2, 7 + i % 2 : 8 + i % 2, :].astype(F32) for i in range(4)]
            hidden = dot(normed[...], up) + jnp.concatenate(pieces, axis=1)
            square = hidden * hidden
            bent = jnp.tanh(0.7978845608028654 * hidden * (1.0 + 0.044715 * square))
            active = (0.5 * hidden * (1.0 + bent)).astype(BF)
            bend = 0.7978845608028654 * (1.0 + 0.134145 * square)
            slope = 0.5 * (1.0 + bent) + 0.5 * hidden * (1.0 - bent * bent) * bend
            back = w2s[n].reshape(512, D)
            out_acc[...] += dot(active, back)
            grad_hidden = (dot_nt(cotangent[...], back) * slope).astype(BF)
            g2[u, n] = dot_tn(active, cotangent[...]).astype(BF).reshape(2, 4, 2, 32, D)
            cols = pl.ds(pl.multiple_of(n * 512, 512), 512)
            block = dot(normed_t[...], grad_hidden).astype(BF)
            gp[u, :, :, :, :, :, cols] = block.reshape(4, 2, 2, 2, 32, 512)
            gn[...] += dot_nt(grad_hidden, up)
            sums = jnp.sum(grad_hidden.astype(F32), axis=0, keepdims=True)
            for i in range(4):
                bias_sums[u, n, i : i + 1, :] = sums[:, 128 * i : 128 * (i + 1)]
            if u < 3:
                for copy in load(u + 1, n):
                    copy.start()

        there = g_fc1.at[:, :, :, :, :, pl.ds(u * D, D)]
        written.append(pltpu.make_async_copy(gp.at[u], there, out_sems.at[u]))
        written.append(pltpu.make_async_copy(g2.at[u], g_fc2.at[u], out_sems.at[4 + u]))
        written[-2].start()
        written[-1].start()

    output[...] = out_acc[...].astype(BF)
    values, scale = norm_parts(middle[...])
    cot = cotangent[...].astype(F32)
    part, by_gain, by_bias = norm_back(gn[...], values, scale, small_row(pack, 2))
    total = cot + part
    grad_middle[...] = total
    branch = total.astype(BF)

    @pl.loop(0, 4)
    def _(n):
        weight = wos[n].reshape(256, D)
        cols = pl.ds(pl.multiple_of(n * 256, 256), 256)
        grad_mixed[:, cols] = dot_nt(branch, weight).astype(BF)

    put_small(small, 2, by_gain)
    put_small(small, 3, by_bias)
    put_small(small, 4, jnp.sum(branch.astype(F32), axis=0, keepdims=True))
    put_small(small, 5, jnp.sum(cot, axis=0, keepdims=True))
    for x in range(4):
        for yh in range(2):
            small[x, yh, 8:12, :] = bias_sums[x, yh, 0:4, :]
    normed[...] = branch
    normed_t[...] = mixed[...].astype(F32).T.astype(BF)

    @pl.loop(0, 4)
    def _(n):
        cols = pl.ds(pl.multiple_of(n * 256, 256), 256)
        block = dot(normed_t[...], normed[:, cols]).astype(BF)
        gp[4, :, :, :, :, :, cols] = block.reshape(4, 2, 2, 2, 32, 256)

    written.append(pltpu.make_async_copy(gp.at[4], g_out, out_sems.at[8]))
    written[-1].start()
    for copy in written:
        copy.wait()


def dense_call(*args):
    hbm = pl.BlockSpec(memory_space=pl.ANY)
    vmem = pl.BlockSpec(memory_space=pltpu.VMEM)
    out = jax.ShapeDtypeStruct
    mem = pltpu.VMEM
    return pl.pallas_call(
        dense_kernel,
        name="dense",
        out_shape=(
            out(full_shape(D), BF),
            out(full_shape(4 * D), BF),
            out((4, 2, 2, 4, 2, 32, D), BF),
            out((BLK, D), BF),
            out((BLK, D), F32),
            out((BLK, D), BF),
            out((4, 2, 16, 128), F32),
        ),
        in_specs=[vmem] * 4 + [hbm] * 3,
        out_specs=(hbm, hbm, hbm, vmem, vmem, vmem, vmem),
        scratch_shapes=[
            mem((5,) + full_shape(D), BF),
            mem((4, 2, 2, 4, 2, 32, D), BF),
            mem((BLK, D), F32),
            mem((BLK, D), F32),
            mem((4, 2, 8, 128), F32),
            mem((2, 4, 2, 2, 2, 32, 512), BF),
            mem((2, 2, 4, 2, 32, D), BF),
            mem(full_shape(D), BF),
            mem((BLK, D), F32),
            mem((BLK, D), BF),
            mem((D, BLK), BF),
            pltpu.SemaphoreType.DMA((5,)),
            pltpu.SemaphoreType.DMA((9,)),
        ],
        compiler_params=pltpu.CompilerParams(vmem_limit_bytes=62 * MIB),
    )(*args)


def local(
    tokens,
    segment_ids,
    cotangent,
    ln1_gain,
    ln1_bias,
    qkv_weight,
    qkv_bias,
    out_weight,
    out_bias,
    ln2_gain,
    ln2_bias,
    fc1_weight,
    fc1_bias,
    fc2_weight,
    fc2_bias,
):
    block_len = tokens.shape[1]
    small = small_pack(
        ln1_gain, ln1_bias, ln2_gain, ln2_bias, out_bias, fc2_bias, qkv_bias, fc1_bias
    )
    flat = tokens.reshape(block_len, D)
    (wq, wo, w1, w2, pack, normed, qkv, kx, qx, ot, lse, mixed, lse_all) = forward_call(
        flat,
        jnp.broadcast_to(segment_ids, (8, block_len)),
        small,
        qkv_weight,
        out_weight,
        fc1_weight,
        fc2_weight,
    )
    log_sums = lse_all[:, :, 0].reshape(1, HEADS, block_len)

    g_out, g_fc1, g_fc2, grad_mixed, grad_middle, output, small_grads = dense_call(
        flat, cotangent.reshape(block_len, D), mixed, pack, wo, w1, w2
    )
    g_qkv, g_wo, g_up, g_down, small_sums, input_grad = backward_call(
        g_out,
        g_fc1,
        g_fc2,
        grad_mixed,
        qkv,
        kx,
        qx,
        ot,
        lse,
        normed,
        wq,
        pack,
        flat,
        small_grads,
    )
    core = lax.axis_index("fsdp") % 2
    halves = lax.dynamic_slice_in_dim(small_sums[:6], core * 64, 64, 1)
    g_qkvb = lax.dynamic_slice_in_dim(small_sums, 6 + core, 1, 0).reshape(128)
    g_upb = lax.dynamic_slice_in_dim(small_sums, 8 + 2 * core, 2, 0).reshape(256)
    return (
        output.reshape(1, block_len, D),
        (grad_middle + input_grad).reshape(1, block_len, D),
        halves[0],
        halves[1],
        g_qkv.reshape(64, 3 * D).astype(jnp.float32),
        g_qkvb,
        g_wo.reshape(64, D).astype(jnp.float32),
        halves[4],
        halves[2],
        halves[3],
        g_up.reshape(64, 4 * D).astype(jnp.float32),
        g_upb,
        g_down.reshape(256, D).astype(jnp.float32),
        halves[5],
        log_sums,
    )


def solution(mesh):
    placed = (
        P("fsdp", "ctx", None),
        P("fsdp", "ctx"),
        P("fsdp", "ctx", None),
        P("fsdp"),
        P("fsdp"),
        P("fsdp", None),
        P("fsdp"),
        P("fsdp", None),
        P("fsdp"),
        P("fsdp"),
        P("fsdp"),
        P("fsdp", None),
        P("fsdp"),
        P("fsdp", None),
        P("fsdp"),
    )
    return jax.shard_map(
        local,
        mesh=mesh,
        in_specs=placed,
        out_specs=(
            P("fsdp", "ctx", None),
            P("fsdp", "ctx", None),
            P("fsdp"),
            P("fsdp"),
            P("fsdp", None),
            P("fsdp"),
            P("fsdp", None),
            P("fsdp"),
            P("fsdp"),
            P("fsdp"),
            P("fsdp", None),
            P("fsdp"),
            P("fsdp", None),
            P("fsdp"),
            P("fsdp", None, "ctx"),
        ),
        check_vma=False,
    )
```
